512 devices in a mesh: dp: 128 (over y, z, core), replica: 4 (over x).
Axes of the slice: x: 4, y: 4, z: 16, core: 2. Of those that a mesh axis runs over, the one named last changes fastest.
Arguments:
- grad_local: float32 [4, 128, 4096, 128], P('replica', 'dp'), may hold values from -384 to 384
- first_moment: float32 [4, 4096, 128], P('replica', 'dp'), as said below
- second_moment: float32 [4, 4096, 128], P('replica', 'dp'), as said below
- master_weight: float32 [4, 4096, 128], P('replica', 'dp'), as said below
- lost_rows: int32 [4, 128], replicated, may hold values from 0 to 1, as said below
- source: int32 [4096], replicated, may hold values from 0 to 3, as said below
- new_owner: int32 [4096], replicated, may hold values from 0 to 127, as said below
- new_slot: int32 [4096], replicated, may hold values from 0 to 31
Outputs:
- fresh_first_moment: float32 [4096, 128], P('dp')
- new_second_moment: float32 [4096, 128], P('dp')
- new_weight: float32 [4096, 128], P('dp')
The draws below stay inside these ranges and needn't reach their ends.
Inputs may be any that keep to these rules, and one draw needn't show every extreme that they name: `lost_rows`: every dp index survives in at least one replica group. source[b] names a replica group whose rank at dp index b // 32 is not lost; copies held by lost ranks are unrelated values. `new_owner`: together with new_slot a bijection onto owner and slot pairs: every dp index receives 32 blocks at distinct slots. Every old owner keeps 4 of its own blocks and hands at most 1 block to any one other dp index; that bound is reached in every draw. `first_moment`: equal on all replica groups except at lost ranks. `second_moment`: equal on all replica groups except at lost ranks; positive where not lost. `master_weight`: equal on all replica groups except at lost ranks.
All inputs are finite; a program needn't handle non-finite values.
Results may differ from the reference program's by a relative error of at most 0.000071.
Values sent between devices are 32-bit elements; how exact they have to be, the bound alone decides.
A program may use at most 64 MiB of HBM per device.

```python
import math
import jax
import jax.numpy as jnp
from jax import lax

BLK_DEV = 32
BLOCK = 128
NBLK = 4096
STAY = 4
N_DP = 128
N_REPLICA = 4


def lost_table(key):
    inner = jax.random.fold_in(key, 11)
    keeper_key, toss_key = jax.random.split(inner)
    keeper = jax.random.randint(keeper_key, (N_DP,), 0, N_REPLICA)
    tosses = jax.random.randint(toss_key, (N_REPLICA, N_DP), 0, 4)
    replica_ids = jnp.arange(N_REPLICA, dtype=jnp.int32)[:, None]
    return jnp.where((tosses == 0) & (replica_ids != keeper[None, :]), 1, 0).astype(jnp.int32)


def layout_pair(key):
    inner = jax.random.fold_in(key, 21)
    shuffle_key, local_key, place_key = jax.random.split(inner, 3)
    shuffle_order = jax.random.permutation(shuffle_key, N_DP).astype(jnp.int32)
    shuffle_back = jnp.zeros((N_DP,), jnp.int32).at[shuffle_order].set(jnp.arange(N_DP, dtype=jnp.int32))
    local_perm = jax.vmap(lambda subkey: jax.random.permutation(subkey, BLK_DEV))(jax.random.split(local_key, N_DP)).astype(jnp.int32)
    place_perm = jax.vmap(lambda subkey: jax.random.permutation(subkey, BLK_DEV))(jax.random.split(place_key, N_DP)).astype(jnp.int32)
    index_list = jnp.arange(BLK_DEV, dtype=jnp.int32)
    shifts = jnp.where(index_list < STAY, 0, 1 + (index_list - STAY) % (N_DP - 1)).astype(jnp.int32)
    shift_of = shifts[local_perm]
    owners = jnp.arange(N_DP, dtype=jnp.int32)[:, None]
    target = shuffle_back[(shuffle_order[owners] + shift_of) % N_DP]
    new_place = place_perm[target, local_perm]
    return (target.reshape(-1).astype(jnp.int32), new_place.reshape(-1).astype(jnp.int32))


def spread_lost(key, good_copy, wild_copy):
    lost_here = lost_table(key)
    owners = jnp.arange(NBLK, dtype=jnp.int32) // BLK_DEV
    flags = lost_here[:, owners]
    return jnp.where(flags[:, :, None] == 1, wild_copy, good_copy[None, :, :]).astype(jnp.float32)


def draw_lost_rows(key, part):
    return lost_table(key)


def draw_source(key, part):
    lost_here = lost_table(key)
    inner = jax.random.fold_in(key, 2)
    first_key, second_key = jax.random.split(inner)
    owners = jnp.arange(NBLK, dtype=jnp.int32) // BLK_DEV
    tosses = jax.random.randint(first_key, (NBLK,), 0, 4)
    begin_at = jnp.where(tosses < 3, 0, jax.random.randint(second_key, (NBLK,), 0, N_REPLICA)).astype(jnp.int32)
    chosen = jnp.full((NBLK,), -1, jnp.int32)
    for offset in range(N_REPLICA):
        candidate = (begin_at + offset) % N_REPLICA
        is_lost = lost_here[candidate, owners]
        chosen = jnp.where((chosen < 0) & (is_lost == 0), candidate, chosen)
    return chosen.astype(jnp.int32)


def draw_new_owner(key, part):
    return layout_pair(key)[0]


def draw_new_slot(key, part):
    return layout_pair(key)[1]


def draw_first_moment(key, part):
    inner = jax.random.fold_in(key, 31)
    good_key, wild_key = jax.random.split(inner)
    good_copy = 0.5 * jax.random.normal(good_key, (NBLK, BLOCK), jnp.float32)
    wild_copy = 40.0 * jax.random.normal(wild_key, (N_REPLICA, NBLK, BLOCK), jnp.float32)
    return spread_lost(key, good_copy, wild_copy)


def draw_second_moment(key, part):
    inner = jax.random.fold_in(key, 41)
    good_key, wild_key = jax.random.split(inner)
    good_copy = jnp.exp(jax.random.uniform(good_key, (NBLK, BLOCK), jnp.float32, math.log(0.05), math.log(2.0)))
    wild_copy = 40.0 * jax.random.normal(wild_key, (N_REPLICA, NBLK, BLOCK), jnp.float32)
    return spread_lost(key, good_copy, wild_copy)


def draw_master_weight(key, part):
    inner = jax.random.fold_in(key, 51)
    good_key, wild_key = jax.random.split(inner)
    good_copy = jax.random.normal(good_key, (NBLK, BLOCK), jnp.float32)
    wild_copy = 40.0 * jax.random.normal(wild_key, (N_REPLICA, NBLK, BLOCK), jnp.float32)
    return spread_lost(key, good_copy, wild_copy)


def with_spikes(values, key, source, target, shards_of, factor):
    def block_of(position):
        return (jnp.arange(values.shape[position]) // (values.shape[position] // shards_of)).reshape((-1,) + (1,) * (values.ndim - 1 - position))

    one_side = jax.random.permutation(key, shards_of)[block_of(target)]
    far = (block_of(target) + shards_of // 2) % shards_of
    return jnp.where((block_of(source) == one_side) | (block_of(source) == far), factor * values, values)


def block_scale(key, dims, cuts, least, high):
    level, own = 1.0, jax.random.fold_in(key, 6)
    for position, parts in cuts:
        draws = jnp.exp(jax.random.uniform(jax.random.fold_in(own, position), (parts,), jnp.float32, least / len(cuts), high / len(cuts)))
        level = level * jnp.repeat(draws, dims[position] // parts).reshape([-1 if axis == position else 1 for axis in range(len(dims))])
    return level


def gaussian_with(stream_key, dims, spread, limit, shards, heavy, kind=jnp.bfloat16):
    result = spread * jax.random.normal(stream_key, dims, jnp.float32)
    if shards:
        result = result * block_scale(stream_key, dims, shards, -0.22, 0.18)
    return jnp.clip(with_spikes(result, jax.random.fold_in(stream_key, 3), *heavy), -limit, limit).astype(kind)


def setup_inputs(seed: int = 0) -> dict:
    arg_keys = jax.random.split(jax.random.key(seed), 9)
    grad_local = gaussian_with(arg_keys[0], (N_REPLICA, N_DP, NBLK, BLOCK), 16.0, 384.0, ((0, 4), (1, 128)), (1, 2, 128, 5.5), jnp.float32)
    first_moment = draw_first_moment(jax.random.fold_in(arg_keys[8], 71), 0)
    second_moment = draw_second_moment(jax.random.fold_in(arg_keys[8], 71), 0)
    master_weight = draw_master_weight(jax.random.fold_in(arg_keys[8], 71), 0)
    lost_rows = draw_lost_rows(jax.random.fold_in(arg_keys[8], 71), 0)
    source = draw_source(jax.random.fold_in(arg_keys[8], 71), 0)
    new_owner = draw_new_owner(jax.random.fold_in(arg_keys[8], 71), 0)
    new_slot = draw_new_slot(jax.random.fold_in(arg_keys[8], 71), 0)
    return dict(grad_local=grad_local, first_moment=first_moment, second_moment=second_moment, master_weight=master_weight, lost_rows=lost_rows, source=source, new_owner=new_owner, new_slot=new_slot)


BETA_ONE = 0.9
BETA_TWO = 0.95
BIAS_FIRST = 1.0 - 0.9 ** 10
BIAS_SECOND = 1.0 - 0.95 ** 10
EPSILON = 1e-08
LEARN_RATE = 0.1
DECAY_RATE = 0.1

def adamw_update(moment_one, moment_two, weight, gradient_rows):
    first = BETA_ONE * moment_one + (1.0 - BETA_ONE) * gradient_rows
    second = BETA_TWO * moment_two + (1.0 - BETA_TWO) * gradient_rows * gradient_rows
    update = first / BIAS_FIRST / (jnp.sqrt(second / BIAS_SECOND) + EPSILON)
    return (first, second, weight - LEARN_RATE * (update + DECAY_RATE * weight))

def reference(grad_local, first_moment, second_moment, master_weight, lost_rows, source, new_owner, new_slot):
    living_flags = (1 - lost_rows).astype(jnp.float32)
    summed = jnp.tensordot(living_flags, grad_local, axes=([0, 1], [0, 1]), precision=lax.Precision.HIGHEST)
    gradient_rows = summed / jnp.sum(living_flags)
    all_blocks = new_owner.shape[0]
    columns = jnp.arange(all_blocks, dtype=jnp.int32)
    good_first = first_moment[source, columns]
    good_second = second_moment[source, columns]
    good_weight = master_weight[source, columns]
    placed = (new_owner * BLK_DEV + new_slot).astype(jnp.int32)
    fresh_ordering = jnp.zeros((all_blocks,), jnp.int32).at[placed].set(columns)
    return adamw_update(good_first[fresh_ordering], good_second[fresh_ordering], good_weight[fresh_ordering], gradient_rows[fresh_ordering])
```

```python
import functools
import math

import jax
import jax.numpy as jnp
from jax import lax
from jax.experimental import pallas as pl
from jax.experimental.pallas import tpu as pltpu
from jax.sharding import PartitionSpec as P

BETA_ONE = 0.9
BETA_TWO = 0.95
BIAS_FIRST = 1.0 - 0.9**10
BIAS_SECOND = 1.0 - 0.95**10
EPSILON = 1e-08
LEARN_RATE = 0.1
DECAY_RATE = 0.1

NX = 4
NY = 4
NZ = 16
JR = 8
LANES = 128
UNROLL = 32

MESH = pl.DeviceIdType.MESH
F32 = jnp.float32
BF16 = jnp.bfloat16
I32 = jnp.int32


def log2(n):
    return int(math.log2(n))


def iota(shape, dim):
    return lax.broadcasted_iota(I32, shape, dim)


def three_parts(value):
    one = value.astype(BF16)
    rest = value - one.astype(F32)
    two = rest.astype(BF16)
    three = (rest - two.astype(F32)).astype(BF16)
    return one, two, three


def pick(onehot, parts):
    total = jnp.dot(onehot, parts[2], preferred_element_type=F32)
    total = total + jnp.dot(onehot, parts[1], preferred_element_type=F32)
    return total + jnp.dot(onehot, parts[0], preferred_element_type=F32)


def prepare(owner_ref, slot_ref, source_ref, m_ref, v_ref, w_ref, lost_ref,
            order_ref, out_ref, wsel_ref, stay_ref, aux_ref, held):
    blk = NX * JR
    segs = LANES // blk
    rows = owner_ref.shape[0]
    zh = NZ // 2
    x = lax.axis_index("replica")
    dp = lax.axis_index("dp")
    y = dp // (2 * NZ)
    c = dp % 2
    partner = dp + 1 - 2 * c

    living = (1 - lost_ref[...]).astype(F32)
    at_row = iota(living.shape, 0)
    at_col = iota(living.shape, 1)
    mine = jnp.sum(jnp.where((at_row == x) & (at_col == dp), living, 0.0))
    other = jnp.sum(jnp.where((at_row == x) & (at_col == partner), living, 0.0))
    aux_ref[0:8, :] = jnp.full((8, LANES), mine, F32)
    aux_ref[8:16, :] = jnp.full((8, LANES), other, F32)
    aux_ref[16:24, :] = jnp.full((8, LANES), jnp.sum(living), F32)

    owner = owner_ref[...]
    slot = slot_ref[...]
    oy = owner >> log2(2 * NZ)
    oz = (owner >> 1) & (NZ - 1)
    oc = owner & 1
    ox = slot >> log2(JR)
    oj = slot & (JR - 1)
    half = oz >> log2(zh)
    zl = oz & (zh - 1)
    first = jnp.where(half == 0, ox, oy)
    second = jnp.where(half == 0, oy, ox)
    pos = ((((oc * 2 + half) * NX + first) * NY + second) * zh + zl) * JR + oj
    pos_row = pos >> 7
    pos_col = pos & 127
    row_pad = max(rows, 8)
    sub_row = iota((row_pad, LANES), 0)
    sub_col = iota((LANES, LANES), 0)
    lane = iota((1, LANES), 1)
    left, right = [], []
    for r in range(rows):
        hit = sub_row == pos_row[r:r + 1, :]
        high = (2 * r + (lane >> 6)).astype(F32)
        low = (lane & 63).astype(F32)
        left.append(jnp.concatenate(
            [jnp.where(hit, high, 0.0), jnp.where(hit, low, 0.0)], axis=0).astype(BF16))
        right.append(jnp.where(sub_col == pos_col[r:r + 1, :], 1.0, 0.0).astype(BF16))
    both = lax.dot_general(
        jnp.concatenate(left, axis=1), jnp.concatenate(right, axis=1),
        (((1,), (1,)), ((), ())), preferred_element_type=F32)
    order = both[:row_pad] * 64.0 + both[row_pad:]
    order_ref[...] = order[:rows].astype(I32)

    seg = dp % segs
    held[...] = jnp.zeros_like(held)
    at = pl.ds(pl.multiple_of(seg * blk, 8), blk)
    keep = jnp.full((blk, LANES), mine, F32) > 0.5
    held[at, 0:128] = jnp.where(keep, m_ref[...], 0.0)
    held[at, 128:256] = jnp.where(keep, v_ref[...], 0.0)
    held[at, 256:384] = jnp.where(keep, w_ref[...], 0.0)
    parts = three_parts(held[...])
    own_row = dp // segs
    owner_row = owner_ref[pl.ds(own_row, 1), :]
    slot_row = slot_ref[pl.ds(own_row, 1), :]
    source_row = source_ref[pl.ds(own_row, 1), :]
    here = ((lane >> log2(blk)) == seg) & (source_row == x)

    leaving = jnp.where(here & (owner_row != dp), owner_row, -2)
    total_rows = NY * NZ * 8
    at_dest = iota((total_rows, LANES), 0)
    pair = at_dest >> 3
    sub = at_dest & 7
    result = None
    for k in range(3):
        dest = jnp.where(sub == k, 2 * pair, jnp.where(sub == 3 + k, 2 * pair + 1, -1))
        onehot = jnp.where(dest == leaving, 1.0, 0.0).astype(BF16)
        got = pick(onehot, [p[:, k * 128:(k + 1) * 128] for p in parts])
        result = got if result is None else result + got
    out_ref[...] = result

    staying = jnp.where(here & (owner_row == dp), slot_row, -1)
    onehot = jnp.where(iota((blk, LANES), 0) == staying, 1.0, 0.0).astype(BF16)
    got = pick(onehot, parts)
    for k in range(3):
        stay_ref[k * blk:(k + 1) * blk, :] = got[:, k * 128:(k + 1) * 128]

    group_rows = 2 * NZ * blk // LANES
    from_y = (x - y + NX) % NX
    at = pl.ds(pl.multiple_of(from_y * group_rows, group_rows), group_rows)
    block = (from_y * group_rows + iota((group_rows, LANES), 0)) * LANES + iota((group_rows, LANES), 1)
    coming = (owner_ref[at, :] == dp) & ((block >> log2(blk)) != dp)
    named = jnp.where(coming, slot_ref[at, :] + 1, 0).astype(F32)
    cols = 2 * NZ * 8
    def source_of(shape):
        col = iota(shape, 1)
        core = jnp.where(col >= NZ * 8, 1 - c, c)
        return ((col & (NZ * 8 - 1)) >> 3) * 2 + core
    spread = jnp.where(
        (iota((LANES, cols), 0) >> log2(blk)) == (source_of((LANES, cols)) & (segs - 1)), 1.0, 0.0)
    if group_rows < 8:
        named = jnp.concatenate([named, jnp.zeros((8 - group_rows, LANES), F32)], axis=0)
    table = jnp.dot(named.astype(BF16), spread.astype(BF16), preferred_element_type=F32)
    row_of = source_of((8, cols)) >> log2(segs)
    slots = jnp.sum(jnp.where(iota((8, cols), 0) == row_of, table, 0.0), axis=0, keepdims=True)
    at_row = iota((3 * blk, cols), 0)
    kind = at_row >> log2(blk)
    sub = iota((3 * blk, cols), 1) & 7
    wanted = ((at_row & (blk - 1)) + 1).astype(F32)
    wsel_ref[...] = jnp.where((slots == wanted) & (sub == 3 * c + kind), 1.0, 0.0)


def exchange(order, grad_hbm, out_ref, wsel_ref, stay_ref, aux_ref,
             first_ref, second_ref, weight_ref,
             grad, csend, crecv, own, rx0, rx1, t0, t1, ry0, ry1, u, rz, gfull,
             srecv, ssum, r1, r2, r3, pbuf, precv,
             grad_sem, csend_sem, crecv_sem, send_sem, recv_sem):
    blk = NX * JR
    zh = NZ // 2
    chunk = NY * zh * JR
    piece = zh * JR
    x = lax.axis_index("replica")
    dp = lax.axis_index("dp")
    y = dp // (2 * NZ)
    z = (dp // 2) % NZ
    c = dp % 2

    def device(dx=0, dy=0, dz=0, dc=0):
        to_y = (y + dy) % NY
        to_z = (z + dz) % NZ
        to_c = (c + dc) % 2
        return ((to_y * NZ + to_z) * 2 + to_c, (x + dx) % NX)

    load = pltpu.make_async_copy(grad_hbm, grad, grad_sem)
    load.start()

    barrier = pltpu.get_barrier_semaphore()
    peers = ([dict(dc=1)] + [dict(dx=k) for k in range(1, NX)]
             + [dict(dy=k) for k in range(1, NY)])
    for peer in peers:
        pl.semaphore_signal(barrier, inc=1, device_id=device(**peer), device_id_type=MESH)

    def greet(k, carry):
        pl.semaphore_signal(barrier, inc=1, device_id=device(dz=k), device_id_type=MESH)
        return carry

    lax.fori_loop(1, NZ, greet, 0)

    def send(src, dst, to, s_sem, r_sem):
        pltpu.make_async_remote_copy(
            src_ref=src, dst_ref=dst, send_sem=s_sem, recv_sem=r_sem,
            device_id=to, device_id_type=MESH).start()

    def await_bytes(ref, sem):
        pltpu.make_async_copy(ref, ref, sem).wait()

    def gather(dst, dst_base, base):
        def step(i, carry):
            at = base + i * UNROLL
            values = [grad[pl.ds(order[at + k], 1), :] for k in range(UNROLL)]
            tile = dst.at[pl.ds(pl.multiple_of(dst_base + i * UNROLL, UNROLL), UNROLL)]
            for k in range(UNROLL):
                tile[k:k + 1, :] = values[k]
            return carry
        lax.fori_loop(0, chunk // UNROLL, step, 0)

    chunks = []
    for k in [2, 1, 3, 0] if NX == 4 else [1, 0]:
        chunks.append((0, k, pl.multiple_of(((x + k) % NX) * chunk, chunk)))
        chunks.append((1, k, pl.multiple_of((NX + (y + k) % NY) * chunk, chunk)))

    load.wait()
    core_rows = 2 * NX * chunk
    for i, (h, k, base) in enumerate(chunks):
        gather(csend, base, (1 - c) * core_rows + base)
        if i == 0:
            pl.semaphore_wait(barrier, len(peers) + NZ - 1)
            for dx in range(1, NX):
                to_y = (x + dx - y + NX) % NX
                send(out_ref.at[pl.ds(pl.multiple_of(to_y * NZ * 8, NZ * 8), NZ * 8)],
                     srecv.at[dx - 1], device(dx=dx), send_sem.at[0], recv_sem.at[0])
        rows = pl.ds(base, chunk)
        send(csend.at[rows], crecv.at[rows], device(dc=1), csend_sem, crecv_sem.at[i])

    alive_mine = aux_ref[0:1, :]
    alive_other = aux_ref[8:9, :]
    partner_y = (x - y + NX) % NX
    for i, (h, k, base) in enumerate(chunks):
        gather(own, base, c * core_rows + base)
        rows = pl.ds(base, chunk)
        await_bytes(crecv.at[rows], crecv_sem.at[i])
        own[rows, :] = own[rows, :] * alive_mine + crecv[rows, :] * alive_other
        if k > 0:
            to = device(dx=k) if h == 0 else device(dy=k)
            send(own.at[rows], (rx0 if h == 0 else rx1).at[k - 1], to,
                 send_sem.at[1 + h], recv_sem.at[1 + h])
        if i == len(chunks) // 2:
            await_bytes(srecv, recv_sem.at[0])
            total = out_ref[pl.ds(pl.multiple_of(partner_y * NZ * 8, NZ * 8), NZ * 8), :]
            for dx in range(NX - 1):
                total = total + srecv[dx]
            ssum[...] = total
            r1[z] = ssum[pl.ds(pl.multiple_of(z * 8, 8), 8), :]

            def spread(kz, carry):
                to_z = (z + kz) % NZ
                send(ssum.at[pl.ds(pl.multiple_of(to_z * 8, 8), 8)], r1.at[z],
                     device(dz=kz), send_sem.at[3], recv_sem.at[3])
                return carry

            lax.fori_loop(1, NZ, spread, 0)

    own0 = pl.multiple_of(x * chunk, chunk)
    own1 = pl.multiple_of((NX + y) * chunk, chunk)
    await_bytes(rx0, recv_sem.at[1])
    total = own[pl.ds(own0, chunk), :]
    for k in range(NX - 1):
        total = total + rx0[k]
    t0[...] = total
    for k in range(1, NY):
        at = pl.ds(pl.multiple_of(((y + k) % NY) * piece, piece), piece)
        send(t0.at[at], ry0.at[k - 1], device(dy=k), send_sem.at[4], recv_sem.at[4])
    await_bytes(rx1, recv_sem.at[2])
    total = own[pl.ds(own1, chunk), :]
    for k in range(NY - 1):
        total = total + rx1[k]
    t1[...] = total
    for k in range(1, NX):
        at = pl.ds(pl.multiple_of(((x + k) % NX) * piece, piece), piece)
        send(t1.at[at], ry1.at[k - 1], device(dx=k), send_sem.at[5], recv_sem.at[5])

    await_bytes(r1.at[0:NZ - 1], recv_sem.at[3])
    partner = ((partner_y * NZ + z) * 2 + c, x)

    @pl.when(partner_y != y)
    def _():
        send(r1, r2, partner, send_sem.at[6], recv_sem.at[6])

    @pl.when(partner_y == y)
    def _():
        r2[...] = r1[...]

    await_bytes(ry0, recv_sem.at[4])
    total = t0[pl.ds(pl.multiple_of(y * piece, piece), piece), :]
    for k in range(NY - 1):
        total = total + ry0[k]
    u[0:piece, :] = total
    await_bytes(ry1, recv_sem.at[5])
    total = t1[pl.ds(pl.multiple_of(x * piece, piece), piece), :]
    for k in range(NX - 1):
        total = total + ry1[k]
    u[piece:2 * piece, :] = total

    def scatter(kz, carry):
        to_z = (z + kz) % NZ
        send(u.at[pl.ds(pl.multiple_of(to_z * JR, JR), JR)], rz.at[kz - 1],
             device(dz=kz), send_sem.at[7], recv_sem.at[7])
        return carry

    lax.fori_loop(1, NZ, scatter, 0)

    @pl.when(partner_y != y)
    def _():
        await_bytes(r2, recv_sem.at[6])

    send(r2, r3, device(dc=1), send_sem.at[8], recv_sem.at[8])
    half = NZ * 8
    near = three_parts(r2[...].reshape(half, LANES))
    total = stay_ref[...] + pick(wsel_ref[:, 0:half].astype(BF16), near)
    await_bytes(r3, recv_sem.at[8])
    far = three_parts(r3[...].reshape(half, LANES))
    pbuf[...] = total + pick(wsel_ref[:, half:2 * half].astype(BF16), far)
    for k in range(1, NX):
        send(pbuf, precv.at[k - 1], device(dx=k), send_sem.at[9], recv_sem.at[9])

    await_bytes(rz, recv_sem.at[7])
    total = u[pl.ds(pl.multiple_of(z * JR, JR), JR), :]
    for k in range(NZ - 1):
        total = total + rz[k]
    gfull[x] = total
    for k in range(1, NX):
        send(gfull.at[x], gfull.at[x], device(dx=k), send_sem.at[10], recv_sem.at[10])

    await_bytes(precv, recv_sem.at[9])
    state = pbuf[...]
    for k in range(NX - 1):
        state = state + precv[k]
    await_bytes(gfull.at[0:NX - 1], recv_sem.at[10])
    gradient = gfull[...].reshape(blk, LANES) / aux_ref[16:17, :]
    first = BETA_ONE * state[0:blk] + (1.0 - BETA_ONE) * gradient
    second = BETA_TWO * state[blk:2 * blk] + (1.0 - BETA_TWO) * gradient * gradient
    weight = state[2 * blk:3 * blk]
    update = first / BIAS_FIRST / (jnp.sqrt(second / BIAS_SECOND) + EPSILON)
    first_ref[...] = first
    second_ref[...] = second
    weight_ref[...] = weight - LEARN_RATE * (update + DECAY_RATE * weight)

    await_bytes(csend, csend_sem)
    for ref, n in ((srecv, 0), (rx0, 1), (rx1, 2), (r1.at[0:NZ - 1], 3), (ry0, 4), (ry1, 5),
                   (rz, 7), (r3, 8), (precv, 9), (gfull.at[0:NX - 1], 10)):
        await_bytes(ref, send_sem.at[n])

    @pl.when(partner_y != y)
    def _():
        await_bytes(r1, send_sem.at[6])


def on_device(grad_local, first_moment, second_moment, master_weight, lost_rows, source,
              new_owner, new_slot):
    blk = NX * JR
    nblk = new_owner.shape[0]
    rows = nblk // LANES
    half_z = NZ * 8
    vmem = pl.BlockSpec(memory_space=pltpu.VMEM)
    order, out, wsel, stay, aux = pl.pallas_call(
        prepare,
        out_shape=(
            jax.ShapeDtypeStruct((rows, LANES), I32),
            jax.ShapeDtypeStruct((NY * half_z, LANES), F32),
            jax.ShapeDtypeStruct((3 * blk, 2 * half_z), F32),
            jax.ShapeDtypeStruct((3 * blk, LANES), F32),
            jax.ShapeDtypeStruct((24, LANES), F32),
        ),
        in_specs=[vmem] * 7,
        out_specs=[vmem] * 5,
        scratch_shapes=[pltpu.VMEM((LANES, 3 * LANES), F32)],
        compiler_params=pltpu.CompilerParams(vmem_limit_bytes=24 * 2**20),
    )(new_owner.reshape(rows, LANES), new_slot.reshape(rows, LANES), source.reshape(rows, LANES),
      first_moment[0], second_moment[0], master_weight[0], lost_rows)

    zh = NZ // 2
    chunk = NY * zh * JR
    piece = zh * JR
    half_rows = 2 * NX * chunk

    def buf(*shape):
        return pltpu.VMEM(shape + (LANES,), F32)

    dma = pltpu.SemaphoreType.DMA
    result = jax.ShapeDtypeStruct((blk, LANES), F32)
    return pl.pallas_call(
        exchange,
        out_shape=(result,) * 3,
        in_specs=[pl.BlockSpec(memory_space=pltpu.SMEM), pl.BlockSpec(memory_space=pl.ANY)]
        + [vmem] * 4,
        out_specs=[vmem] * 3,
        scratch_shapes=[
            buf(nblk), buf(half_rows), buf(half_rows), buf(half_rows),
            buf(NX - 1, chunk), buf(NY - 1, chunk), buf(chunk), buf(chunk),
            buf(NY - 1, piece), buf(NX - 1, piece), buf(2 * piece),
            buf(NZ - 1, JR), buf(NX, JR),
            buf(NX - 1, half_z), buf(half_z), buf(NZ, 8), buf(NZ, 8), buf(NZ, 8),
            buf(3 * blk), buf(NX - 1, 3 * blk),
            dma, dma, dma((2 * NX,)), dma((11,)), dma((11,)),
        ],
        compiler_params=pltpu.CompilerParams(
            collective_id=0, has_side_effects=True, vmem_limit_bytes=32 * 2**20),
        cost_estimate=pl.CostEstimate(
            flops=nblk * LANES, bytes_accessed=nblk * LANES * 4, transcendentals=0),
    )(order.reshape(nblk), grad_local[0, 0], out, wsel, stay, aux)


def solution(mesh):
    return jax.shard_map(
        on_device,
        mesh=mesh,
        in_specs=(
            P("replica", "dp", None, None),
            P("replica", "dp", None),
            P("replica", "dp", None),
            P("replica", "dp", None),
            P(),
            P(),
            P(),
            P(),
        ),
        out_specs=(P("dp", None), P("dp", None), P("dp", None)),
        check_vma=False,
    )
```

```python
import functools
import math

import jax
import jax.numpy as jnp
from jax import lax
from jax.experimental import pallas as pl
from jax.experimental.pallas import tpu as pltpu
from jax.sharding import PartitionSpec as P

BETA_ONE = 0.9
BETA_TWO = 0.95
BIAS_FIRST = 1.0 - 0.9**10
BIAS_SECOND = 1.0 - 0.95**10
EPSILON = 1e-08
LEARN_RATE = 0.1
DECAY_RATE = 0.1

NX = 4
NY = 4
NZ = 16
JR = 8
LANES = 128
UNROLL = 32
VMEM_BYTES = 63 * 2**20

MESH = pl.DeviceIdType.MESH
F32 = jnp.float32
BF16 = jnp.bfloat16
I32 = jnp.int32


def log2(n):
    return int(math.log2(n))


def iota(shape, dim):
    return lax.broadcasted_iota(I32, shape, dim)


def three_parts(value):
    one = value.astype(BF16)
    rest = value - one.astype(F32)
    two = rest.astype(BF16)
    three = (rest - two.astype(F32)).astype(BF16)
    return one, two, three


def pick(onehot, parts):
    total = jnp.dot(onehot, parts[2], preferred_element_type=F32)
    total = total + jnp.dot(onehot, parts[1], preferred_element_type=F32)
    return total + jnp.dot(onehot, parts[0], preferred_element_type=F32)


def prepare_order(owner_ref, slot_ref, order_ref):
    rows = owner_ref.shape[0]
    zh = NZ // 2
    owner = owner_ref[...]
    slot = slot_ref[...]
    oy = owner >> log2(2 * NZ)
    oz = (owner >> 1) & (NZ - 1)
    oc = owner & 1
    ox = slot >> log2(JR)
    oj = slot & (JR - 1)
    half = oz >> log2(zh)
    zl = oz & (zh - 1)
    first = jnp.where(half == 0, ox, oy)
    second = jnp.where(half == 0, oy, ox)
    pos = ((((oc * 2 + half) * NX + first) * NY + second) * zh + zl) * JR + oj
    pos_row = pos >> 7
    pos_col = pos & 127
    row_pad = max(rows, 8)
    sub_row = iota((row_pad, LANES), 0)
    sub_col = iota((LANES, LANES), 0)
    lane = iota((1, LANES), 1)
    left, right = [], []
    for r in range(rows):
        hit = sub_row == pos_row[r:r + 1, :]
        high = (2 * r + (lane >> 6)).astype(F32)
        low = (lane & 63).astype(F32)
        left.append(jnp.concatenate(
            [jnp.where(hit, high, 0.0), jnp.where(hit, low, 0.0)], axis=0).astype(BF16))
        right.append(jnp.where(sub_col == pos_col[r:r + 1, :], 1.0, 0.0).astype(BF16))
    both = lax.dot_general(
        jnp.concatenate(left, axis=1), jnp.concatenate(right, axis=1),
        (((1,), (1,)), ((), ())), preferred_element_type=F32)
    order = both[:row_pad] * 64.0 + both[row_pad:]
    order_ref[...] = order[:rows].astype(I32)


def prepare_state(owner_ref, slot_ref, source_ref, m_ref, v_ref, w_ref, lost_ref,
                  out_ref, wsel_ref, stay_ref, aux_ref, held):
    blk = NX * JR
    segs = LANES // blk
    x = lax.axis_index("replica")
    dp = lax.axis_index("dp")
    y = dp // (2 * NZ)
    c = dp % 2
    partner = dp + 1 - 2 * c
    lane = iota((1, LANES), 1)

    living = (1 - lost_ref[...]).astype(F32)
    at_row = iota(living.shape, 0)
    at_col = iota(living.shape, 1)
    mine = jnp.sum(jnp.where((at_row == x) & (at_col == dp), living, 0.0))
    other = jnp.sum(jnp.where((at_row == x) & (at_col == partner), living, 0.0))
    aux_ref[0:8, :] = jnp.full((8, LANES), mine, F32)
    aux_ref[8:16, :] = jnp.full((8, LANES), other, F32)
    aux_ref[16:24, :] = jnp.full((8, LANES), jnp.sum(living), F32)

    seg = dp % segs
    held[...] = jnp.zeros_like(held)
    at = pl.ds(pl.multiple_of(seg * blk, 8), blk)
    keep = jnp.full((blk, LANES), mine, F32) > 0.5
    held[at, 0:128] = jnp.where(keep, m_ref[...], 0.0)
    held[at, 128:256] = jnp.where(keep, v_ref[...], 0.0)
    held[at, 256:384] = jnp.where(keep, w_ref[...], 0.0)
    parts = three_parts(held[...])
    own_row = dp // segs
    owner_row = owner_ref[pl.ds(own_row, 1), :]
    slot_row = slot_ref[pl.ds(own_row, 1), :]
    source_row = source_ref[pl.ds(own_row, 1), :]
    here = ((lane >> log2(blk)) == seg) & (source_row == x)

    leaving = jnp.where(here & (owner_row != dp), owner_row, -2)
    total_rows = NY * NZ * 8
    at_dest = iota((total_rows, LANES), 0)
    pair = at_dest >> 3
    sub = at_dest & 7
    result = None
    for k in range(3):
        dest = jnp.where(sub == k, 2 * pair, jnp.where(sub == 3 + k, 2 * pair + 1, -1))
        onehot = jnp.where(dest == leaving, 1.0, 0.0).astype(BF16)
        got = pick(onehot, [p[:, k * 128:(k + 1) * 128] for p in parts])
        result = got if result is None else result + got
    out_ref[...] = result

    staying = jnp.where(here & (owner_row == dp), slot_row, -1)
    onehot = jnp.where(iota((blk, LANES), 0) == staying, 1.0, 0.0).astype(BF16)
    got = pick(onehot, parts)
    for k in range(3):
        stay_ref[k * blk:(k + 1) * blk, :] = got[:, k * 128:(k + 1) * 128]

    group_rows = 2 * NZ * blk // LANES
    from_y = (x - y + NX) % NX
    at = pl.ds(pl.multiple_of(from_y * group_rows, group_rows), group_rows)
    block = (from_y * group_rows + iota((group_rows, LANES), 0)) * LANES + iota((group_rows, LANES), 1)
    coming = (owner_ref[at, :] == dp) & ((block >> log2(blk)) != dp)
    named = jnp.where(coming, slot_ref[at, :] + 1, 0).astype(F32)
    cols = 2 * NZ * 8
    def source_of(shape):
        col = iota(shape, 1)
        core = jnp.where(col >= NZ * 8, 1 - c, c)
        return ((col & (NZ * 8 - 1)) >> 3) * 2 + core
    spread = jnp.where(
        (iota((LANES, cols), 0) >> log2(blk)) == (source_of((LANES, cols)) & (segs - 1)), 1.0, 0.0)
    if group_rows < 8:
        named = jnp.concatenate([named, jnp.zeros((8 - group_rows, LANES), F32)], axis=0)
    table = jnp.dot(named.astype(BF16), spread.astype(BF16), preferred_element_type=F32)
    row_of = source_of((8, cols)) >> log2(segs)
    slots = jnp.sum(jnp.where(iota((8, cols), 0) == row_of, table, 0.0), axis=0, keepdims=True)
    at_row = iota((3 * blk, cols), 0)
    kind = at_row >> log2(blk)
    sub = iota((3 * blk, cols), 1) & 7
    wanted = ((at_row & (blk - 1)) + 1).astype(F32)
    wsel_ref[...] = jnp.where((slots == wanted) & (sub == 3 * c + kind), 1.0, 0.0)


def prepare(owner_ref, slot_ref, source_ref, m_ref, v_ref, w_ref, lost_ref,
            order_ref, out_ref, wsel_ref, stay_ref, aux_ref, held):
    prepare_order(owner_ref, slot_ref, order_ref)
    prepare_state(owner_ref, slot_ref, source_ref, m_ref, v_ref, w_ref, lost_ref,
                  out_ref, wsel_ref, stay_ref, aux_ref, held)


def exchange(order_hbm, out_hbm, wsel_hbm, stay_hbm, aux_hbm, grad_hbm, result_ref,
             order, out_ref, wsel_ref, stay_ref, aux_ref,
             grad, csend, crecv, own, rl0, rl1, rx0, rx1, t0, t1, ry0, ry1, u, rz, gfull,
             srecv, ssum, r1, r2, r3, pbuf, precv,
             grad_sem, in_sem, csend_sem, crecv_sem, send_sem, recv_sem):
    blk = NX * JR
    zh = NZ // 2
    chunk = NY * zh * JR
    piece = zh * JR
    x = lax.axis_index("replica")
    dp = lax.axis_index("dp")
    y = dp // (2 * NZ)
    z = (dp // 2) % NZ
    c = dp % 2

    def device(dx=0, dy=0, dz=0, dc=0):
        to_y = (y + dy) % NY
        to_z = (z + dz) % NZ
        to_c = (c + dc) % 2
        return ((to_y * NZ + to_z) * 2 + to_c, (x + dx) % NX)

    pairs = ((order_hbm, order), (out_hbm, out_ref), (wsel_hbm, wsel_ref),
             (stay_hbm, stay_ref), (aux_hbm, aux_ref))
    small = [pltpu.make_async_copy(src, dst, in_sem.at[i]) for i, (src, dst) in enumerate(pairs)]
    for copy in small:
        copy.start()
    load = pltpu.make_async_copy(grad_hbm, grad, grad_sem)
    load.start()

    barrier = pltpu.get_barrier_semaphore()
    peers = ([dict(dc=1)] + [dict(dx=k) for k in range(1, NX)]
             + [dict(dy=k) for k in range(1, NY)])
    for peer in peers:
        pl.semaphore_signal(barrier, inc=1, device_id=device(**peer), device_id_type=MESH)

    def greet(k, carry):
        pl.semaphore_signal(barrier, inc=1, device_id=device(dz=k), device_id_type=MESH)
        return carry

    lax.fori_loop(1, NZ, greet, 0)

    def send(src, dst, to, s_sem, r_sem):
        pltpu.make_async_remote_copy(
            src_ref=src, dst_ref=dst, send_sem=s_sem, recv_sem=r_sem,
            device_id=to, device_id_type=MESH).start()

    def await_bytes(ref, sem):
        pltpu.make_async_copy(ref, ref, sem).wait()

    def gather(dst, dst_base, base):
        def step(i, carry):
            at = base + i * UNROLL
            row, col = at // LANES, at % LANES
            values = [grad[pl.ds(order[row, col + k], 1), :] for k in range(UNROLL)]
            tile = dst.at[pl.ds(pl.multiple_of(dst_base + i * UNROLL, UNROLL), UNROLL)]
            for k in range(UNROLL):
                tile[k:k + 1, :] = values[k]
            return carry
        lax.fori_loop(0, chunk // UNROLL, step, 0)

    chunks = []
    for k in (2, 1, 3, 0):
        chunks.append((0, k, pl.multiple_of(((x + k) % NX) * chunk, chunk)))
        chunks.append((1, k, pl.multiple_of((NX + (y + k) % NY) * chunk, chunk)))

    for copy in small:
        copy.wait()
    load.wait()
    core_rows = 2 * NX * chunk
    for i, (h, k, base) in enumerate(chunks):
        gather(csend, base, (1 - c) * core_rows + base)
        if i == 0:
            pl.semaphore_wait(barrier, len(peers) + NZ - 1)
            for dx in range(1, NX):
                to_y = (x + dx - y + NX) % NX
                send(out_ref.at[pl.ds(pl.multiple_of(to_y * NZ * 8, NZ * 8), NZ * 8)],
                     srecv.at[dx - 1], device(dx=dx), send_sem.at[0], recv_sem.at[0])
        rows = pl.ds(base, chunk)
        send(csend.at[rows], crecv.at[rows], device(dc=1), csend_sem, crecv_sem.at[i])

    alive_mine = aux_ref[0:1, :]
    alive_other = aux_ref[8:9, :]
    partner_y = (x - y + NX) % NX
    for i, (h, k, base) in enumerate(chunks):
        gather(own, base, c * core_rows + base)
        rows = pl.ds(base, chunk)
        await_bytes(crecv.at[rows], crecv_sem.at[i])
        own[rows, :] = own[rows, :] * alive_mine + crecv[rows, :] * alive_other
        relay, landing = (rl0, rx0) if h == 0 else (rl1, rx1)
        up = device(dx=1) if h == 0 else device(dy=1)
        down = device(dx=-1) if h == 0 else device(dy=-1)
        part = chunk // 2
        low, high = pl.ds(base, part), pl.ds(pl.multiple_of(base + part, part), part)
        if k == 2:
            send(own.at[low], relay.at[0], up, send_sem.at[11 + 2 * h], recv_sem.at[11 + 2 * h])
            send(own.at[high], relay.at[1], down, send_sem.at[12 + 2 * h], recv_sem.at[12 + 2 * h])
        elif k == 1:
            send(own.at[high], landing.at[0, part:chunk], up, send_sem.at[1 + h], recv_sem.at[1 + h])
            await_bytes(relay.at[0], recv_sem.at[11 + 2 * h])
            own[low, :] = own[low, :] + relay[0]
            send(own.at[low], landing.at[0, 0:part], up, send_sem.at[1 + h], recv_sem.at[1 + h])
        elif k == 3:
            send(own.at[low], landing.at[1, 0:part], down, send_sem.at[1 + h], recv_sem.at[1 + h])
            await_bytes(relay.at[1], recv_sem.at[12 + 2 * h])
            own[high, :] = own[high, :] + relay[1]
            send(own.at[high], landing.at[1, part:chunk], down, send_sem.at[1 + h], recv_sem.at[1 + h])
        if i == len(chunks) // 2:
            await_bytes(srecv, recv_sem.at[0])
            total = out_ref[pl.ds(pl.multiple_of(partner_y * NZ * 8, NZ * 8), NZ * 8), :]
            for dx in range(NX - 1):
                total = total + srecv[dx]
            ssum[...] = total
            r1[z] = ssum[pl.ds(pl.multiple_of(z * 8, 8), 8), :]

            def spread(kz, carry):
                to_z = (z + kz) % NZ
                send(ssum.at[pl.ds(pl.multiple_of(to_z * 8, 8), 8)], r1.at[z],
                     device(dz=kz), send_sem.at[3], recv_sem.at[3])
                return carry

            lax.fori_loop(1, NZ, spread, 0)

    own0 = pl.multiple_of(x * chunk, chunk)
    own1 = pl.multiple_of((NX + y) * chunk, chunk)
    await_bytes(rx0, recv_sem.at[1])
    t0[...] = own[pl.ds(own0, chunk), :] + rx0[0] + rx0[1]
    for k in range(1, NY):
        at = pl.ds(pl.multiple_of(((y + k) % NY) * piece, piece), piece)
        send(t0.at[at], ry0.at[k - 1], device(dy=k), send_sem.at[4], recv_sem.at[4])
    await_bytes(rx1, recv_sem.at[2])
    t1[...] = own[pl.ds(own1, chunk), :] + rx1[0] + rx1[1]
    for k in range(1, NX):
        at = pl.ds(pl.multiple_of(((x + k) % NX) * piece, piece), piece)
        send(t1.at[at], ry1.at[k - 1], device(dx=k), send_sem.at[5], recv_sem.at[5])

    await_bytes(r1.at[0:NZ - 1], recv_sem.at[3])
    partner = ((partner_y * NZ + z) * 2 + c, x)

    @pl.when(partner_y != y)
    def _():
        send(r1, r2, partner, send_sem.at[6], recv_sem.at[6])

    @pl.when(partner_y == y)
    def _():
        r2[...] = r1[...]

    await_bytes(ry0, recv_sem.at[4])
    total = t0[pl.ds(pl.multiple_of(y * piece, piece), piece), :]
    for k in range(NY - 1):
        total = total + ry0[k]
    u[0:piece, :] = total
    await_bytes(ry1, recv_sem.at[5])
    total = t1[pl.ds(pl.multiple_of(x * piece, piece), piece), :]
    for k in range(NX - 1):
        total = total + ry1[k]
    u[piece:2 * piece, :] = total

    def scatter(kz, carry):
        to_z = (z + kz) % NZ
        send(u.at[pl.ds(pl.multiple_of(to_z * JR, JR), JR)], rz.at[kz - 1],
             device(dz=kz), send_sem.at[7], recv_sem.at[7])
        return carry

    lax.fori_loop(1, NZ, scatter, 0)

    @pl.when(partner_y != y)
    def _():
        await_bytes(r2, recv_sem.at[6])

    send(r2, r3, device(dc=1), send_sem.at[8], recv_sem.at[8])
    half = NZ * 8
    near = three_parts(r2[...].reshape(half, LANES))
    total = stay_ref[...] + pick(wsel_ref[:, 0:half].astype(BF16), near)
    await_bytes(r3, recv_sem.at[8])
    far = three_parts(r3[...].reshape(half, LANES))
    pbuf[...] = total + pick(wsel_ref[:, half:2 * half].astype(BF16), far)
    for k in range(1, NX):
        send(pbuf, precv.at[k - 1], device(dx=k), send_sem.at[9], recv_sem.at[9])

    await_bytes(rz, recv_sem.at[7])
    total = u[pl.ds(pl.multiple_of(z * JR, JR), JR), :]
    for k in range(NZ - 1):
        total = total + rz[k]
    gfull[x] = total
    for k in range(1, NX):
        send(gfull.at[x], gfull.at[x], device(dx=k), send_sem.at[10], recv_sem.at[10])

    await_bytes(precv, recv_sem.at[9])
    state = pbuf[...]
    for k in range(NX - 1):
        state = state + precv[k]
    await_bytes(gfull.at[0:NX - 1], recv_sem.at[10])
    result_ref[0:3 * blk, :] = state
    result_ref[3 * blk:4 * blk, :] = gfull[...].reshape(blk, LANES) / aux_ref[16:17, :]

    await_bytes(csend, csend_sem)
    for ref, n in ((srecv, 0), (rx0, 1), (rx1, 2),
                   (rl0.at[0], 11), (rl0.at[1], 12), (rl1.at[0], 13), (rl1.at[1], 14), (r1.at[0:NZ - 1], 3), (ry0, 4), (ry1, 5),
                   (rz, 7), (r3, 8), (precv, 9), (gfull.at[0:NX - 1], 10)):
        await_bytes(ref, send_sem.at[n])

    @pl.when(partner_y != y)
    def _():
        await_bytes(r1, send_sem.at[6])


def adamw_update(moment_one, moment_two, weight, gradient_rows):
    first = BETA_ONE * moment_one + (1.0 - BETA_ONE) * gradient_rows
    second = BETA_TWO * moment_two + (1.0 - BETA_TWO) * gradient_rows * gradient_rows
    update = first / BIAS_FIRST / (jnp.sqrt(second / BIAS_SECOND) + EPSILON)
    return (first, second, weight - LEARN_RATE * (update + DECAY_RATE * weight))


def on_device(grad_local, first_moment, second_moment, master_weight, lost_rows, source,
              new_owner, new_slot):
    blk = NX * JR
    nblk = new_owner.shape[0]
    rows = nblk // LANES
    half_z = NZ * 8
    zh = NZ // 2
    chunk = NY * zh * JR
    piece = zh * JR
    half_rows = 2 * NX * chunk

    def buf(*shape):
        return pltpu.VMEM(shape + (LANES,), F32)

    def whole(*shape):
        return pl.BlockSpec(shape, lambda i: (0, 0))

    table = (rows, LANES)
    shapes = ((NY * half_z, LANES), (3 * blk, 2 * half_z), (3 * blk, LANES), (24, LANES))
    prepared = pl.pallas_call(
        prepare,
        grid=(1,),
        out_shape=[jax.ShapeDtypeStruct(table, I32)]
        + [jax.ShapeDtypeStruct(shape, F32) for shape in shapes],
        in_specs=[whole(*table)] * 3 + [whole(blk, LANES)] * 3 + [whole(*lost_rows.shape)],
        out_specs=[whole(*table)] + [whole(*shape) for shape in shapes],
        scratch_shapes=[pltpu.VMEM((LANES, 3 * LANES), F32)],
        compiler_params=pltpu.CompilerParams(vmem_limit_bytes=VMEM_BYTES),
    )(new_owner.reshape(table), new_slot.reshape(table), source.reshape(table),
      first_moment[0], second_moment[0], master_weight[0], lost_rows)
    dma = pltpu.SemaphoreType.DMA
    result = pl.pallas_call(
        exchange,
        out_shape=jax.ShapeDtypeStruct((4 * blk, LANES), F32),
        in_specs=[pl.BlockSpec(memory_space=pl.ANY)] * 6,
        out_specs=pl.BlockSpec(memory_space=pltpu.VMEM),
        scratch_shapes=[
            pltpu.SMEM(table, I32), *[pltpu.VMEM(shape, F32) for shape in shapes],
            buf(nblk), buf(half_rows), buf(half_rows), buf(half_rows),
            buf(2, chunk // 2), buf(2, chunk // 2),
            buf(2, chunk), buf(2, chunk), buf(chunk), buf(chunk),
            buf(NY - 1, piece), buf(NX - 1, piece), buf(2 * piece),
            buf(NZ - 1, JR), buf(NX, JR),
            buf(NX - 1, half_z), buf(half_z), buf(NZ, 8), buf(NZ, 8), buf(NZ, 8),
            buf(3 * blk), buf(NX - 1, 3 * blk),
            dma, dma((5,)), dma, dma((2 * NX,)), dma((15,)), dma((15,)),
        ],
        compiler_params=pltpu.CompilerParams(
            collective_id=0, has_side_effects=True, vmem_limit_bytes=VMEM_BYTES),
        cost_estimate=pl.CostEstimate(
            flops=nblk * LANES, bytes_accessed=nblk * LANES * 4, transcendentals=0),
    )(*prepared, grad_local[0, 0])
    return adamw_update(result[0:blk], result[blk:2 * blk], result[2 * blk:3 * blk],
                        result[3 * blk:4 * blk])


def solution(mesh):
    return jax.shard_map(
        on_device,
        mesh=mesh,
        in_specs=(
            P("replica", "dp", None, None),
            P("replica", "dp", None),
            P("replica", "dp", None),
            P("replica", "dp", None),
            P(),
            P(),
            P(),
            P(),
        ),
        out_specs=(P("dp", None), P("dp", None), P("dp", None)),
        check_vma=False,
    )
```

```python
import functools
import math

import jax
import jax.numpy as jnp
from jax import lax
from jax.experimental import pallas as pl
from jax.experimental.pallas import tpu as pltpu
from jax.sharding import PartitionSpec as P

BETA_ONE = 0.9
BETA_TWO = 0.95
BIAS_FIRST = 1.0 - 0.9**10
BIAS_SECOND = 1.0 - 0.95**10
EPSILON = 1e-08
LEARN_RATE = 0.1
DECAY_RATE = 0.1

NX = 4
NY = 4
NZ = 16
JR = 8
LANES = 128
UNROLL = 32
VMEM_BYTES = 63 * 2**20

MESH = pl.DeviceIdType.MESH
F32 = jnp.float32
BF16 = jnp.bfloat16
I32 = jnp.int32


def log2(n):
    return int(math.log2(n))


def iota(shape, dim):
    return lax.broadcasted_iota(I32, shape, dim)


def three_parts(value):
    one = value.astype(BF16)
    rest = value - one.astype(F32)
    two = rest.astype(BF16)
    three = (rest - two.astype(F32)).astype(BF16)
    return one, two, three


def pick(onehot, parts):
    total = jnp.dot(onehot, parts[2], preferred_element_type=F32)
    total = total + jnp.dot(onehot, parts[1], preferred_element_type=F32)
    return total + jnp.dot(onehot, parts[0], preferred_element_type=F32)


def prepare_order(owner_ref, slot_ref, order_ref):
    rows = owner_ref.shape[0]
    zh = NZ // 2
    owner = owner_ref[...]
    slot = slot_ref[...]
    oy = owner >> log2(2 * NZ)
    oz = (owner >> 1) & (NZ - 1)
    oc = owner & 1
    ox = slot >> log2(JR)
    oj = slot & (JR - 1)
    half = oz >> log2(zh)
    zl = oz & (zh - 1)
    first = jnp.where(half == 0, ox, oy)
    second = jnp.where(half == 0, oy, ox)
    pos = ((((oc * 2 + half) * NX + first) * NY + second) * zh + zl) * JR + oj
    pos_row = pos >> 7
    pos_col = pos & 127
    row_pad = max(rows, 8)
    sub_row = iota((row_pad, LANES), 0)
    sub_col = iota((LANES, LANES), 0)
    lane = iota((1, LANES), 1)
    left, right = [], []
    for r in range(rows):
        hit = sub_row == pos_row[r:r + 1, :]
        high = (2 * r + (lane >> 6)).astype(F32)
        low = (lane & 63).astype(F32)
        left.append(jnp.concatenate(
            [jnp.where(hit, high, 0.0), jnp.where(hit, low, 0.0)], axis=0).astype(BF16))
        right.append(jnp.where(sub_col == pos_col[r:r + 1, :], 1.0, 0.0).astype(BF16))
    both = lax.dot_general(
        jnp.concatenate(left, axis=1), jnp.concatenate(right, axis=1),
        (((1,), (1,)), ((), ())), preferred_element_type=F32)
    order = both[:row_pad] * 64.0 + both[row_pad:]
    order_ref[...] = order[:rows].astype(I32)


def prepare_state(owner_ref, slot_ref, source_ref, m_ref, v_ref, w_ref, lost_ref,
                  out_ref, wsel_ref, stay_ref, aux_ref, held):
    blk = NX * JR
    segs = LANES // blk
    x = lax.axis_index("replica")
    dp = lax.axis_index("dp")
    y = dp // (2 * NZ)
    c = dp % 2
    partner = dp + 1 - 2 * c
    lane = iota((1, LANES), 1)

    living = (1 - lost_ref[...]).astype(F32)
    at_row = iota(living.shape, 0)
    at_col = iota(living.shape, 1)
    mine = jnp.sum(jnp.where((at_row == x) & (at_col == dp), living, 0.0))
    other = jnp.sum(jnp.where((at_row == x) & (at_col == partner), living, 0.0))
    aux_ref[0:8, :] = jnp.full((8, LANES), mine, F32)
    aux_ref[8:16, :] = jnp.full((8, LANES), other, F32)
    aux_ref[16:24, :] = jnp.full((8, LANES), jnp.sum(living), F32)

    seg = dp % segs
    held[...] = jnp.zeros_like(held)
    at = pl.ds(pl.multiple_of(seg * blk, 8), blk)
    keep = jnp.full((blk, LANES), mine, F32) > 0.5
    held[at, 0:128] = jnp.where(keep, m_ref[...], 0.0)
    held[at, 128:256] = jnp.where(keep, v_ref[...], 0.0)
    held[at, 256:384] = jnp.where(keep, w_ref[...], 0.0)
    parts = three_parts(held[...])
    own_row = dp // segs
    owner_row = owner_ref[pl.ds(own_row, 1), :]
    slot_row = slot_ref[pl.ds(own_row, 1), :]
    source_row = source_ref[pl.ds(own_row, 1), :]
    here = ((lane >> log2(blk)) == seg) & (source_row == x)

    leaving = jnp.where(here & (owner_row != dp), owner_row, -2)
    total_rows = NY * NZ * 8
    at_dest = iota((total_rows, LANES), 0)
    pair = at_dest >> 3
    sub = at_dest & 7
    result = None
    for k in range(3):
        dest = jnp.where(sub == k, 2 * pair, jnp.where(sub == 3 + k, 2 * pair + 1, -1))
        onehot = jnp.where(dest == leaving, 1.0, 0.0).astype(BF16)
        got = pick(onehot, [p[:, k * 128:(k + 1) * 128] for p in parts])
        result = got if result is None else result + got
    out_ref[...] = result

    staying = jnp.where(here & (owner_row == dp), slot_row, -1)
    onehot = jnp.where(iota((blk, LANES), 0) == staying, 1.0, 0.0).astype(BF16)
    got = pick(onehot, parts)
    for k in range(3):
        stay_ref[k * blk:(k + 1) * blk, :] = got[:, k * 128:(k + 1) * 128]

    group_rows = 2 * NZ * blk // LANES
    from_y = (x - y + NX) % NX
    at = pl.ds(pl.multiple_of(from_y * group_rows, group_rows), group_rows)
    block = (from_y * group_rows + iota((group_rows, LANES), 0)) * LANES + iota((group_rows, LANES), 1)
    coming = (owner_ref[at, :] == dp) & ((block >> log2(blk)) != dp)
    named = jnp.where(coming, slot_ref[at, :] + 1, 0).astype(F32)
    cols = 2 * NZ * 8
    def source_of(shape):
        col = iota(shape, 1)
        core = jnp.where(col >= NZ * 8, 1 - c, c)
        return ((col & (NZ * 8 - 1)) >> 3) * 2 + core
    spread = jnp.where(
        (iota((LANES, cols), 0) >> log2(blk)) == (source_of((LANES, cols)) & (segs - 1)), 1.0, 0.0)
    if group_rows < 8:
        named = jnp.concatenate([named, jnp.zeros((8 - group_rows, LANES), F32)], axis=0)
    table = jnp.dot(named.astype(BF16), spread.astype(BF16), preferred_element_type=F32)
    row_of = source_of((8, cols)) >> log2(segs)
    slots = jnp.sum(jnp.where(iota((8, cols), 0) == row_of, table, 0.0), axis=0, keepdims=True)
    at_row = iota((3 * blk, cols), 0)
    kind = at_row >> log2(blk)
    sub = iota((3 * blk, cols), 1) & 7
    wanted = ((at_row & (blk - 1)) + 1).astype(F32)
    wsel_ref[...] = jnp.where((slots == wanted) & (sub == 3 * c + kind), 1.0, 0.0)


def prepare(owner_ref, slot_ref, source_ref, m_ref, v_ref, w_ref, lost_ref,
            order_ref, out_ref, wsel_ref, stay_ref, aux_ref, held):
    prepare_order(owner_ref, slot_ref, order_ref)
    prepare_state(owner_ref, slot_ref, source_ref, m_ref, v_ref, w_ref, lost_ref,
                  out_ref, wsel_ref, stay_ref, aux_ref, held)


def exchange(order_hbm, out_hbm, wsel_hbm, stay_hbm, aux_hbm, grad_hbm, result_ref,
             order, out_ref, wsel_ref, stay_ref, aux_ref,
             grad, csend, crecv, own, rl0, rl1, rx0, rx1, t0, t1, ry0, ry1, u, rz, gfull,
             srecv, ssum, r1, r2, r3, pbuf, precv,
             grad_sem, in_sem, csend_sem, crecv_sem, send_sem, recv_sem):
    blk = NX * JR
    zh = NZ // 2
    chunk = NY * zh * JR
    piece = zh * JR
    x = lax.axis_index("replica")
    dp = lax.axis_index("dp")
    y = dp // (2 * NZ)
    z = (dp // 2) % NZ
    c = dp % 2

    def device(dx=0, dy=0, dz=0, dc=0):
        to_y = (y + dy) % NY
        to_z = (z + dz) % NZ
        to_c = (c + dc) % 2
        return ((to_y * NZ + to_z) * 2 + to_c, (x + dx) % NX)

    pairs = ((order_hbm, order), (out_hbm, out_ref), (wsel_hbm, wsel_ref),
             (stay_hbm, stay_ref), (aux_hbm, aux_ref))
    small = [pltpu.make_async_copy(src, dst, in_sem.at[i]) for i, (src, dst) in enumerate(pairs)]
    for copy in small:
        copy.start()
    load = pltpu.make_async_copy(grad_hbm, grad, grad_sem)
    load.start()

    barrier = pltpu.get_barrier_semaphore()
    peers = ([dict(dc=1)] + [dict(dx=k) for k in range(1, NX)]
             + [dict(dy=k) for k in range(1, NY)])
    for peer in peers:
        pl.semaphore_signal(barrier, inc=1, device_id=device(**peer), device_id_type=MESH)

    def greet(k, carry):
        pl.semaphore_signal(barrier, inc=1, device_id=device(dz=k), device_id_type=MESH)
        return carry

    lax.fori_loop(1, NZ, greet, 0)

    def send(src, dst, to, s_sem, r_sem):
        pltpu.make_async_remote_copy(
            src_ref=src, dst_ref=dst, send_sem=s_sem, recv_sem=r_sem,
            device_id=to, device_id_type=MESH).start()

    def await_bytes(ref, sem):
        pltpu.make_async_copy(ref, ref, sem).wait()

    grad_rows = grad.reshape(grad.shape[0], 1, LANES)

    def gather(dst, dst_base, base):
        dst_rows = dst.reshape(dst.shape[0], 1, LANES)

        def step(i, carry):
            at = i * UNROLL
            values = [grad_rows[order[base + at + k]] for k in range(UNROLL)]
            for k in range(UNROLL):
                dst_rows[dst_base + at + k] = values[k]
            return carry

        lax.fori_loop(0, chunk // UNROLL, step, 0)

    chunks = []
    for k in (2, 1, 3, 0):
        chunks.append((0, k, pl.multiple_of(((x + k) % NX) * chunk, chunk)))
        chunks.append((1, k, pl.multiple_of((NX + (y + k) % NY) * chunk, chunk)))

    for copy in small:
        copy.wait()
    load.wait()
    core_rows = 2 * NX * chunk
    for i, (h, k, base) in enumerate(chunks):
        gather(csend, base, (1 - c) * core_rows + base)
        if i == 0:
            pl.semaphore_wait(barrier, len(peers) + NZ - 1)
            for dx in range(1, NX):
                to_y = (x + dx - y + NX) % NX
                send(out_ref.at[pl.ds(pl.multiple_of(to_y * NZ * 8, NZ * 8), NZ * 8)],
                     srecv.at[dx - 1], device(dx=dx), send_sem.at[0], recv_sem.at[0])
        rows = pl.ds(base, chunk)
        send(csend.at[rows], crecv.at[rows], device(dc=1), csend_sem, crecv_sem.at[i])

    alive_mine = aux_ref[0:1, :]
    alive_other = aux_ref[8:9, :]
    partner_y = (x - y + NX) % NX
    part = chunk // 2
    relays, landings = (rl0, rl1), (rx0, rx1)

    def pass_on(i):
        h, k, base = chunks[i]
        axis = "dx" if h == 0 else "dy"
        side = 0 if k == 1 else 1
        rows = pl.ds(pl.multiple_of(base + side * part, part), part)
        await_bytes(relays[h].at[side], recv_sem.at[11 + 2 * h + side])
        own[rows, :] = own[rows, :] + relays[h][side]
        send(own.at[rows], landings[h].at[side, side * part:(side + 1) * part],
             device(**{axis: 1 - 2 * side}), send_sem.at[1 + h], recv_sem.at[1 + h])

    for i, (h, k, base) in enumerate(chunks):
        gather(own, base, c * core_rows + base)
        rows = pl.ds(base, chunk)
        await_bytes(crecv.at[rows], crecv_sem.at[i])
        own[rows, :] = own[rows, :] * alive_mine + crecv[rows, :] * alive_other
        axis = "dx" if h == 0 else "dy"
        low = pl.ds(base, part)
        high = pl.ds(pl.multiple_of(base + part, part), part)
        up, down = device(**{axis: 1}), device(**{axis: -1})
        relay, landing = relays[h], landings[h]
        straight = (send_sem.at[1 + h], recv_sem.at[1 + h])
        if k == 2:
            send(own.at[low], relay.at[0], up, send_sem.at[11 + 2 * h], recv_sem.at[11 + 2 * h])
            send(own.at[high], relay.at[1], down, send_sem.at[12 + 2 * h], recv_sem.at[12 + 2 * h])
        elif k == 1:
            send(own.at[high], landing.at[0, part:chunk], up, *straight)
        elif k == 3:
            send(own.at[low], landing.at[1, 0:part], down, *straight)
        if i >= 4:
            pass_on(i - 2)
        if i == len(chunks) // 2:
            await_bytes(srecv, recv_sem.at[0])
            total = out_ref[pl.ds(pl.multiple_of(partner_y * NZ * 8, NZ * 8), NZ * 8), :]
            for dx in range(NX - 1):
                total = total + srecv[dx]
            ssum[...] = total
            r1[z] = ssum[pl.ds(pl.multiple_of(z * 8, 8), 8), :]

            def spread(kz, carry):
                to_z = (z + kz) % NZ
                send(ssum.at[pl.ds(pl.multiple_of(to_z * 8, 8), 8)], r1.at[z],
                     device(dz=kz), send_sem.at[3], recv_sem.at[3])
                return carry

            lax.fori_loop(1, NZ, spread, 0)

    own0 = pl.multiple_of(x * chunk, chunk)
    own1 = pl.multiple_of((NX + y) * chunk, chunk)
    await_bytes(rx0, recv_sem.at[1])
    t0[...] = own[pl.ds(own0, chunk), :] + rx0[0] + rx0[1]
    for k in range(1, NY):
        at = pl.ds(pl.multiple_of(((y + k) % NY) * piece, piece), piece)
        send(t0.at[at], ry0.at[k - 1], device(dy=k), send_sem.at[4], recv_sem.at[4])
    await_bytes(rx1, recv_sem.at[2])
    t1[...] = own[pl.ds(own1, chunk), :] + rx1[0] + rx1[1]
    for k in range(1, NX):
        at = pl.ds(pl.multiple_of(((x + k) % NX) * piece, piece), piece)
        send(t1.at[at], ry1.at[k - 1], device(dx=k), send_sem.at[5], recv_sem.at[5])

    await_bytes(r1.at[0:NZ - 1], recv_sem.at[3])
    partner = ((partner_y * NZ + z) * 2 + c, x)

    @pl.when(partner_y != y)
    def _():
        send(r1, r2, partner, send_sem.at[6], recv_sem.at[6])

    @pl.when(partner_y == y)
    def _():
        r2[...] = r1[...]

    await_bytes(ry0, recv_sem.at[4])
    total = t0[pl.ds(pl.multiple_of(y * piece, piece), piece), :]
    for k in range(NY - 1):
        total = total + ry0[k]
    u[0:piece, :] = total
    await_bytes(ry1, recv_sem.at[5])
    total = t1[pl.ds(pl.multiple_of(x * piece, piece), piece), :]
    for k in range(NX - 1):
        total = total + ry1[k]
    u[piece:2 * piece, :] = total

    def scatter(kz, carry):
        to_z = (z + kz) % NZ
        send(u.at[pl.ds(pl.multiple_of(to_z * JR, JR), JR)], rz.at[kz - 1],
             device(dz=kz), send_sem.at[7], recv_sem.at[7])
        return carry

    lax.fori_loop(1, NZ, scatter, 0)

    @pl.when(partner_y != y)
    def _():
        await_bytes(r2, recv_sem.at[6])

    send(r2, r3, device(dc=1), send_sem.at[8], recv_sem.at[8])
    half = NZ * 8
    near = three_parts(r2[...].reshape(half, LANES))
    total = stay_ref[...] + pick(wsel_ref[:, 0:half].astype(BF16), near)
    await_bytes(r3, recv_sem.at[8])
    far = three_parts(r3[...].reshape(half, LANES))
    pbuf[...] = total + pick(wsel_ref[:, half:2 * half].astype(BF16), far)
    for k in range(1, NX):
        send(pbuf, precv.at[k - 1], device(dx=k), send_sem.at[9], recv_sem.at[9])

    await_bytes(rz, recv_sem.at[7])
    total = u[pl.ds(pl.multiple_of(z * JR, JR), JR), :]
    for k in range(NZ - 1):
        total = total + rz[k]
    gfull[x] = total
    for k in range(1, NX):
        send(gfull.at[x], gfull.at[x], device(dx=k), send_sem.at[10], recv_sem.at[10])

    await_bytes(precv, recv_sem.at[9])
    state = pbuf[...]
    for k in range(NX - 1):
        state = state + precv[k]
    await_bytes(gfull.at[0:NX - 1], recv_sem.at[10])
    result_ref[0:3 * blk, :] = state
    result_ref[3 * blk:4 * blk, :] = gfull[...].reshape(blk, LANES) / aux_ref[16:17, :]

    await_bytes(csend, csend_sem)
    for ref, n in ((srecv, 0), (rx0, 1), (rx1, 2),
                   (rl0.at[0], 11), (rl0.at[1], 12), (rl1.at[0], 13), (rl1.at[1], 14), (r1.at[0:NZ - 1], 3), (ry0, 4), (ry1, 5),
                   (rz, 7), (r3, 8), (precv, 9), (gfull.at[0:NX - 1], 10)):
        await_bytes(ref, send_sem.at[n])

    @pl.when(partner_y != y)
    def _():
        await_bytes(r1, send_sem.at[6])


def adamw_update(moment_one, moment_two, weight, gradient_rows):
    first = BETA_ONE * moment_one + (1.0 - BETA_ONE) * gradient_rows
    second = BETA_TWO * moment_two + (1.0 - BETA_TWO) * gradient_rows * gradient_rows
    update = first / BIAS_FIRST / (jnp.sqrt(second / BIAS_SECOND) + EPSILON)
    return (first, second, weight - LEARN_RATE * (update + DECAY_RATE * weight))


def on_device(grad_local, first_moment, second_moment, master_weight, lost_rows, source,
              new_owner, new_slot):
    blk = NX * JR
    nblk = new_owner.shape[0]
    rows = nblk // LANES
    half_z = NZ * 8
    zh = NZ // 2
    chunk = NY * zh * JR
    piece = zh * JR
    half_rows = 2 * NX * chunk

    def buf(*shape):
        return pltpu.VMEM(shape + (LANES,), F32)

    def whole(*shape):
        return pl.BlockSpec(shape, lambda i: (0, 0))

    table = (rows, LANES)
    shapes = ((NY * half_z, LANES), (3 * blk, 2 * half_z), (3 * blk, LANES), (24, LANES))
    prepared = pl.pallas_call(
        prepare,
        grid=(1,),
        out_shape=[jax.ShapeDtypeStruct(table, I32)]
        + [jax.ShapeDtypeStruct(shape, F32) for shape in shapes],
        in_specs=[whole(*table)] * 3 + [whole(blk, LANES)] * 3 + [whole(*lost_rows.shape)],
        out_specs=[whole(*table)] + [whole(*shape) for shape in shapes],
        scratch_shapes=[pltpu.VMEM((LANES, 3 * LANES), F32)],
        compiler_params=pltpu.CompilerParams(vmem_limit_bytes=VMEM_BYTES),
    )(new_owner.reshape(table), new_slot.reshape(table), source.reshape(table),
      first_moment[0], second_moment[0], master_weight[0], lost_rows)
    dma = pltpu.SemaphoreType.DMA
    result = pl.pallas_call(
        exchange,
        out_shape=jax.ShapeDtypeStruct((4 * blk, LANES), F32),
        in_specs=[pl.BlockSpec(memory_space=pl.ANY)] * 6,
        out_specs=pl.BlockSpec(memory_space=pltpu.VMEM),
        scratch_shapes=[
            pltpu.SMEM((nblk,), I32), *[pltpu.VMEM(shape, F32) for shape in shapes],
            buf(nblk), buf(half_rows), buf(half_rows), buf(half_rows),
            buf(2, chunk // 2), buf(2, chunk // 2),
            buf(2, chunk), buf(2, chunk), buf(chunk), buf(chunk),
            buf(NY - 1, piece), buf(NX - 1, piece), buf(2 * piece),
            buf(NZ - 1, JR), buf(NX, JR),
            buf(NX - 1, half_z), buf(half_z), buf(NZ, 8), buf(NZ, 8), buf(NZ, 8),
            buf(3 * blk), buf(NX - 1, 3 * blk),
            dma, dma((5,)), dma, dma((2 * NX,)), dma((15,)), dma((15,)),
        ],
        compiler_params=pltpu.CompilerParams(
            collective_id=0, has_side_effects=True, vmem_limit_bytes=VMEM_BYTES),
        cost_estimate=pl.CostEstimate(
            flops=nblk * LANES, bytes_accessed=nblk * LANES * 4, transcendentals=0),
    )(prepared[0].reshape(nblk), *prepared[1:], grad_local[0, 0])
    return adamw_update(result[0:blk], result[blk:2 * blk], result[2 * blk:3 * blk],
                        result[3 * blk:4 * blk])


def solution(mesh):
    return jax.shard_map(
        on_device,
        mesh=mesh,
        in_specs=(
            P("replica", "dp", None, None),
            P("replica", "dp", None),
            P("replica", "dp", None),
            P("replica", "dp", None),
            P(),
            P(),
            P(),
            P(),
        ),
        out_specs=(P("dp", None), P("dp", None), P("dp", None)),
        check_vma=False,
    )
```

```python
import functools
import math

import jax
import jax.numpy as jnp
from jax import lax
from jax.experimental import pallas as pl
from jax.experimental.pallas import tpu as pltpu
from jax.sharding import PartitionSpec as P

BETA_ONE = 0.9
BETA_TWO = 0.95
BIAS_FIRST = 1.0 - 0.9**10
BIAS_SECOND = 1.0 - 0.95**10
EPSILON = 1e-08
LEARN_RATE = 0.1
DECAY_RATE = 0.1

NX = 4
NY = 4
NZ = 16
JR = 8
LANES = 128
UNROLL = 32
VMEM_BYTES = 63 * 2**20

MESH = pl.DeviceIdType.MESH
F32 = jnp.float32
BF16 = jnp.bfloat16
I32 = jnp.int32


def log2(n):
    return int(math.log2(n))


def iota(shape, dim):
    return lax.broadcasted_iota(I32, shape, dim)


def three_parts(value):
    one = value.astype(BF16)
    rest = value - one.astype(F32)
    two = rest.astype(BF16)
    three = (rest - two.astype(F32)).astype(BF16)
    return one, two, three


def pick(onehot, parts):
    total = jnp.dot(onehot, parts[2], preferred_element_type=F32)
    total = total + jnp.dot(onehot, parts[1], preferred_element_type=F32)
    return total + jnp.dot(onehot, parts[0], preferred_element_type=F32)


def prepare_order(owner_ref, slot_ref, order_ref):
    rows = owner_ref.shape[0]
    zh = NZ // 2
    owner = owner_ref[...]
    slot = slot_ref[...]
    oy = owner >> log2(2 * NZ)
    oz = (owner >> 1) & (NZ - 1)
    oc = owner & 1
    ox = slot >> log2(JR)
    oj = slot & (JR - 1)
    half = oz >> log2(zh)
    zl = oz & (zh - 1)
    first = jnp.where(half == 0, ox, oy)
    second = jnp.where(half == 0, oy, ox)
    pos = ((((oc * 2 + half) * NX + first) * NY + second) * zh + zl) * JR + oj
    pos_row = pos >> 7
    pos_col = pos & 127
    row_pad = max(rows, 8)
    sub_row = iota((row_pad, LANES), 0)
    sub_col = iota((LANES, LANES), 0)
    lane = iota((1, LANES), 1)
    left, right = [], []
    for r in range(rows):
        hit = sub_row == pos_row[r:r + 1, :]
        high = (2 * r + (lane >> 6)).astype(F32)
        low = (lane & 63).astype(F32)
        left.append(jnp.concatenate(
            [jnp.where(hit, high, 0.0), jnp.where(hit, low, 0.0)], axis=0).astype(BF16))
        right.append(jnp.where(sub_col == pos_col[r:r + 1, :], 1.0, 0.0).astype(BF16))
    both = lax.dot_general(
        jnp.concatenate(left, axis=1), jnp.concatenate(right, axis=1),
        (((1,), (1,)), ((), ())), preferred_element_type=F32)
    order = both[:row_pad] * 64.0 + both[row_pad:]
    order_ref[...] = order[:rows].astype(I32)


def prepare_state(owner_ref, slot_ref, source_ref, m_ref, v_ref, w_ref, lost_ref,
                  out_ref, wsel_ref, stay_ref, aux_ref, held):
    blk = NX * JR
    segs = LANES // blk
    x = lax.axis_index("replica")
    dp = lax.axis_index("dp")
    y = dp // (2 * NZ)
    c = dp % 2
    partner = dp + 1 - 2 * c
    lane = iota((1, LANES), 1)

    living = (1 - lost_ref[...]).astype(F32)
    at_row = iota(living.shape, 0)
    at_col = iota(living.shape, 1)
    mine = jnp.sum(jnp.where((at_row == x) & (at_col == dp), living, 0.0))
    other = jnp.sum(jnp.where((at_row == x) & (at_col == partner), living, 0.0))
    aux_ref[0:8, :] = jnp.full((8, LANES), mine, F32)
    aux_ref[8:16, :] = jnp.full((8, LANES), other, F32)
    aux_ref[16:24, :] = jnp.full((8, LANES), jnp.sum(living), F32)

    seg = dp % segs
    held[...] = jnp.zeros_like(held)
    at = pl.ds(pl.multiple_of(seg * blk, 8), blk)
    keep = jnp.full((blk, LANES), mine, F32) > 0.5
    held[at, 0:128] = jnp.where(keep, m_ref[...], 0.0)
    held[at, 128:256] = jnp.where(keep, v_ref[...], 0.0)
    held[at, 256:384] = jnp.where(keep, w_ref[...], 0.0)
    parts = three_parts(held[...])
    own_row = dp // segs
    owner_row = owner_ref[pl.ds(own_row, 1), :]
    slot_row = slot_ref[pl.ds(own_row, 1), :]
    source_row = source_ref[pl.ds(own_row, 1), :]
    here = ((lane >> log2(blk)) == seg) & (source_row == x)

    leaving = jnp.where(here & (owner_row != dp), owner_row, -2)
    total_rows = NY * NZ * 8
    at_dest = iota((total_rows, LANES), 0)
    pair = at_dest >> 3
    sub = at_dest & 7
    result = None
    for k in range(3):
        dest = jnp.where(sub == k, 2 * pair, jnp.where(sub == 3 + k, 2 * pair + 1, -1))
        onehot = jnp.where(dest == leaving, 1.0, 0.0).astype(BF16)
        got = pick(onehot, [p[:, k * 128:(k + 1) * 128] for p in parts])
        result = got if result is None else result + got
    out_ref[...] = result

    staying = jnp.where(here & (owner_row == dp), slot_row, -1)
    onehot = jnp.where(iota((blk, LANES), 0) == staying, 1.0, 0.0).astype(BF16)
    got = pick(onehot, parts)
    for k in range(3):
        stay_ref[k * blk:(k + 1) * blk, :] = got[:, k * 128:(k + 1) * 128]

    group_rows = 2 * NZ * blk // LANES
    from_y = (x - y + NX) % NX
    at = pl.ds(pl.multiple_of(from_y * group_rows, group_rows), group_rows)
    block = (from_y * group_rows + iota((group_rows, LANES), 0)) * LANES + iota((group_rows, LANES), 1)
    coming = (owner_ref[at, :] == dp) & ((block >> log2(blk)) != dp)
    named = jnp.where(coming, slot_ref[at, :] + 1, 0).astype(F32)
    cols = 2 * NZ * 8
    def source_of(shape):
        col = iota(shape, 1)
        core = jnp.where(col >= NZ * 8, 1 - c, c)
        return ((col & (NZ * 8 - 1)) >> 3) * 2 + core
    spread = jnp.where(
        (iota((LANES, cols), 0) >> log2(blk)) == (source_of((LANES, cols)) & (segs - 1)), 1.0, 0.0)
    if group_rows < 8:
        named = jnp.concatenate([named, jnp.zeros((8 - group_rows, LANES), F32)], axis=0)
    table = jnp.dot(named.astype(BF16), spread.astype(BF16), preferred_element_type=F32)
    row_of = source_of((8, cols)) >> log2(segs)
    slots = jnp.sum(jnp.where(iota((8, cols), 0) == row_of, table, 0.0), axis=0, keepdims=True)
    at_row = iota((3 * blk, cols), 0)
    kind = at_row >> log2(blk)
    sub = iota((3 * blk, cols), 1) & 7
    wanted = ((at_row & (blk - 1)) + 1).astype(F32)
    wsel_ref[...] = jnp.where((slots == wanted) & (sub == 3 * c + kind), 1.0, 0.0)


def prepare(owner_ref, slot_ref, source_ref, m_ref, v_ref, w_ref, lost_ref,
            order_ref, out_ref, wsel_ref, stay_ref, aux_ref, held):
    prepare_order(owner_ref, slot_ref, order_ref)
    prepare_state(owner_ref, slot_ref, source_ref, m_ref, v_ref, w_ref, lost_ref,
                  out_ref, wsel_ref, stay_ref, aux_ref, held)


def exchange(order_hbm, out_hbm, wsel_hbm, stay_hbm, aux_hbm, grad_hbm, result_ref,
             order, out_ref, wsel_ref, stay_ref, aux_ref,
             grad, csend, crecv, own, rl0, rl1, rx0, rx1, t0, t1, ry0, ry1, u, rz, gfull,
             srecv, ssum, r1, r2, r3, pbuf, precv,
             grad_sem, in_sem, csend_sem, crecv_sem, send_sem, recv_sem):
    blk = NX * JR
    zh = NZ // 2
    chunk = NY * zh * JR
    piece = zh * JR
    x = lax.axis_index("replica")
    dp = lax.axis_index("dp")
    y = dp // (2 * NZ)
    z = (dp // 2) % NZ
    c = dp % 2

    def device(dx=0, dy=0, dz=0, dc=0):
        to_y = (y + dy) % NY
        to_z = (z + dz) % NZ
        to_c = (c + dc) % 2
        return ((to_y * NZ + to_z) * 2 + to_c, (x + dx) % NX)

    pairs = ((order_hbm, order), (out_hbm, out_ref), (wsel_hbm, wsel_ref),
             (stay_hbm, stay_ref), (aux_hbm, aux_ref))
    small = [pltpu.make_async_copy(src, dst, in_sem.at[i]) for i, (src, dst) in enumerate(pairs)]
    for copy in small:
        copy.start()
    load = pltpu.make_async_copy(grad_hbm, grad, grad_sem)
    load.start()

    barrier = pltpu.get_barrier_semaphore()
    peers = ([dict(dc=1)] + [dict(dx=k) for k in range(1, NX)]
             + [dict(dy=k) for k in range(1, NY)])
    for peer in peers:
        pl.semaphore_signal(barrier, inc=1, device_id=device(**peer), device_id_type=MESH)

    def greet(k, carry):
        pl.semaphore_signal(barrier, inc=1, device_id=device(dz=k), device_id_type=MESH)
        return carry

    lax.fori_loop(1, NZ, greet, 0)

    def send(src, dst, to, s_sem, r_sem):
        pltpu.make_async_remote_copy(
            src_ref=src, dst_ref=dst, send_sem=s_sem, recv_sem=r_sem,
            device_id=to, device_id_type=MESH).start()

    def await_bytes(ref, sem):
        pltpu.make_async_copy(ref, ref, sem).wait()

    grad_rows = grad.reshape(grad.shape[0], 1, LANES)

    def gather(dst, dst_base, base):
        dst_rows = dst.reshape(dst.shape[0], 1, LANES)

        def step(i, carry):
            at = i * UNROLL
            values = [grad_rows[order[base + at + k]] for k in range(UNROLL)]
            for k in range(UNROLL):
                dst_rows[dst_base + at + k] = values[k]
            return carry

        lax.fori_loop(0, chunk // UNROLL, step, 0)

    chunks = []
    for k in (2, 1, 3, 0):
        chunks.append((0, k, pl.multiple_of(((x + k) % NX) * chunk, chunk)))
        chunks.append((1, k, pl.multiple_of((NX + (y + k) % NY) * chunk, chunk)))

    for copy in small:
        copy.wait()
    load.wait()
    core_rows = 2 * NX * chunk

    def for_partner(i):
        base = chunks[i][2]
        gather(csend, base, (1 - c) * core_rows + base)
        if i == 0:
            pl.semaphore_wait(barrier, len(peers) + NZ - 1)
            for dx in range(1, NX):
                to_y = (x + dx - y + NX) % NX
                send(out_ref.at[pl.ds(pl.multiple_of(to_y * NZ * 8, NZ * 8), NZ * 8)],
                     srecv.at[dx - 1], device(dx=dx), send_sem.at[0], recv_sem.at[0])
        rows = pl.ds(base, chunk)
        send(csend.at[rows], crecv.at[rows], device(dc=1), csend_sem, crecv_sem.at[i])

    alive_mine = aux_ref[0:1, :]
    alive_other = aux_ref[8:9, :]
    partner_y = (x - y + NX) % NX
    part = chunk // 2
    relays, landings = (rl0, rl1), (rx0, rx1)

    def pass_on(i):
        h, k, base = chunks[i]
        axis = "dx" if h == 0 else "dy"
        side = 0 if k == 1 else 1
        rows = pl.ds(pl.multiple_of(base + side * part, part), part)
        await_bytes(relays[h].at[side], recv_sem.at[11 + 2 * h + side])
        own[rows, :] = own[rows, :] + relays[h][side]
        send(own.at[rows], landings[h].at[side, side * part:(side + 1) * part],
             device(**{axis: 1 - 2 * side}), send_sem.at[1 + h], recv_sem.at[1 + h])

    def for_me(i):
        h, k, base = chunks[i]
        gather(own, base, c * core_rows + base)
        rows = pl.ds(base, chunk)
        await_bytes(crecv.at[rows], crecv_sem.at[i])
        own[rows, :] = own[rows, :] * alive_mine + crecv[rows, :] * alive_other
        axis = "dx" if h == 0 else "dy"
        low = pl.ds(base, part)
        high = pl.ds(pl.multiple_of(base + part, part), part)
        up, down = device(**{axis: 1}), device(**{axis: -1})
        relay, landing = relays[h], landings[h]
        straight = (send_sem.at[1 + h], recv_sem.at[1 + h])
        if k == 2:
            send(own.at[low], relay.at[0], up, send_sem.at[11 + 2 * h], recv_sem.at[11 + 2 * h])
            send(own.at[high], relay.at[1], down, send_sem.at[12 + 2 * h], recv_sem.at[12 + 2 * h])
        elif k == 1:
            send(own.at[high], landing.at[0, part:chunk], up, *straight)
        elif k == 3:
            send(own.at[low], landing.at[1, 0:part], down, *straight)
        for earlier in {3: [2], 4: [3], 5: [4, 5]}.get(i, []):
            pass_on(earlier)
        if i == 3:
            await_bytes(srecv, recv_sem.at[0])
            total = out_ref[pl.ds(pl.multiple_of(partner_y * NZ * 8, NZ * 8), NZ * 8), :]
            for dx in range(NX - 1):
                total = total + srecv[dx]
            ssum[...] = total
            r1[z] = ssum[pl.ds(pl.multiple_of(z * 8, 8), 8), :]

            def spread(kz, carry):
                to_z = (z + kz) % NZ
                send(ssum.at[pl.ds(pl.multiple_of(to_z * 8, 8), 8)], r1.at[z],
                     device(dz=kz), send_sem.at[3], recv_sem.at[3])
                return carry

            lax.fori_loop(1, NZ, spread, 0)

    lag = 3
    for i in range(len(chunks) + lag):
        if i < len(chunks):
            for_partner(i)
        if i >= lag:
            for_me(i - lag)

    own0 = pl.multiple_of(x * chunk, chunk)
    own1 = pl.multiple_of((NX + y) * chunk, chunk)
    await_bytes(rx0, recv_sem.at[1])
    t0[...] = own[pl.ds(own0, chunk), :] + rx0[0] + rx0[1]
    for k in range(1, NY):
        at = pl.ds(pl.multiple_of(((y + k) % NY) * piece, piece), piece)
        send(t0.at[at], ry0.at[k - 1], device(dy=k), send_sem.at[4], recv_sem.at[4])
    await_bytes(rx1, recv_sem.at[2])
    t1[...] = own[pl.ds(own1, chunk), :] + rx1[0] + rx1[1]
    for k in range(1, NX):
        at = pl.ds(pl.multiple_of(((x + k) % NX) * piece, piece), piece)
        send(t1.at[at], ry1.at[k - 1], device(dx=k), send_sem.at[5], recv_sem.at[5])

    await_bytes(r1.at[0:NZ - 1], recv_sem.at[3])
    partner = ((partner_y * NZ + z) * 2 + c, x)

    @pl.when(partner_y != y)
    def _():
        send(r1, r2, partner, send_sem.at[6], recv_sem.at[6])

    @pl.when(partner_y == y)
    def _():
        r2[...] = r1[...]

    await_bytes(ry0, recv_sem.at[4])
    total = t0[pl.ds(pl.multiple_of(y * piece, piece), piece), :]
    for k in range(NY - 1):
        total = total + ry0[k]
    u[0:piece, :] = total
    await_bytes(ry1, recv_sem.at[5])
    total = t1[pl.ds(pl.multiple_of(x * piece, piece), piece), :]
    for k in range(NX - 1):
        total = total + ry1[k]
    u[piece:2 * piece, :] = total

    def scatter(kz, carry):
        to_z = (z + kz) % NZ
        send(u.at[pl.ds(pl.multiple_of(to_z * JR, JR), JR)], rz.at[kz - 1],
             device(dz=kz), send_sem.at[7], recv_sem.at[7])
        return carry

    lax.fori_loop(1, NZ, scatter, 0)

    @pl.when(partner_y != y)
    def _():
        await_bytes(r2, recv_sem.at[6])

    send(r2, r3, device(dc=1), send_sem.at[8], recv_sem.at[8])
    half = NZ * 8
    near = three_parts(r2[...].reshape(half, LANES))
    total = stay_ref[...] + pick(wsel_ref[:, 0:half].astype(BF16), near)
    await_bytes(r3, recv_sem.at[8])
    far = three_parts(r3[...].reshape(half, LANES))
    pbuf[...] = total + pick(wsel_ref[:, half:2 * half].astype(BF16), far)
    for k in range(1, NX):
        send(pbuf, precv.at[k - 1], device(dx=k), send_sem.at[9], recv_sem.at[9])

    await_bytes(rz, recv_sem.at[7])
    total = u[pl.ds(pl.multiple_of(z * JR, JR), JR), :]
    for k in range(NZ - 1):
        total = total + rz[k]
    gfull[x] = total
    for k in range(1, NX):
        send(gfull.at[x], gfull.at[x], device(dx=k), send_sem.at[10], recv_sem.at[10])

    await_bytes(precv, recv_sem.at[9])
    state = pbuf[...]
    for k in range(NX - 1):
        state = state + precv[k]
    await_bytes(gfull.at[0:NX - 1], recv_sem.at[10])
    result_ref[0:3 * blk, :] = state
    result_ref[3 * blk:4 * blk, :] = gfull[...].reshape(blk, LANES) / aux_ref[16:17, :]

    await_bytes(csend, csend_sem)
    for ref, n in ((srecv, 0), (rx0, 1), (rx1, 2),
                   (rl0.at[0], 11), (rl0.at[1], 12), (rl1.at[0], 13), (rl1.at[1], 14), (r1.at[0:NZ - 1], 3), (ry0, 4), (ry1, 5),
                   (rz, 7), (r3, 8), (precv, 9), (gfull.at[0:NX - 1], 10)):
        await_bytes(ref, send_sem.at[n])

    @pl.when(partner_y != y)
    def _():
        await_bytes(r1, send_sem.at[6])


def adamw_update(moment_one, moment_two, weight, gradient_rows):
    first = BETA_ONE * moment_one + (1.0 - BETA_ONE) * gradient_rows
    second = BETA_TWO * moment_two + (1.0 - BETA_TWO) * gradient_rows * gradient_rows
    update = first / BIAS_FIRST / (jnp.sqrt(second / BIAS_SECOND) + EPSILON)
    return (first, second, weight - LEARN_RATE * (update + DECAY_RATE * weight))


def on_device(grad_local, first_moment, second_moment, master_weight, lost_rows, source,
              new_owner, new_slot):
    blk = NX * JR
    nblk = new_owner.shape[0]
    rows = nblk // LANES
    half_z = NZ * 8
    zh = NZ // 2
    chunk = NY * zh * JR
    piece = zh * JR
    half_rows = 2 * NX * chunk

    def buf(*shape):
        return pltpu.VMEM(shape + (LANES,), F32)

    def whole(*shape):
        return pl.BlockSpec(shape, lambda i: (0, 0))

    table = (rows, LANES)
    shapes = ((NY * half_z, LANES), (3 * blk, 2 * half_z), (3 * blk, LANES), (24, LANES))
    prepared = pl.pallas_call(
        prepare,
        grid=(1,),
        out_shape=[jax.ShapeDtypeStruct(table, I32)]
        + [jax.ShapeDtypeStruct(shape, F32) for shape in shapes],
        in_specs=[whole(*table)] * 3 + [whole(blk, LANES)] * 3 + [whole(*lost_rows.shape)],
        out_specs=[whole(*table)] + [whole(*shape) for shape in shapes],
        scratch_shapes=[pltpu.VMEM((LANES, 3 * LANES), F32)],
        compiler_params=pltpu.CompilerParams(vmem_limit_bytes=VMEM_BYTES),
    )(new_owner.reshape(table), new_slot.reshape(table), source.reshape(table),
      first_moment[0], second_moment[0], master_weight[0], lost_rows)
    dma = pltpu.SemaphoreType.DMA
    result = pl.pallas_call(
        exchange,
        out_shape=jax.ShapeDtypeStruct((4 * blk, LANES), F32),
        in_specs=[pl.BlockSpec(memory_space=pl.ANY)] * 6,
        out_specs=pl.BlockSpec(memory_space=pltpu.VMEM),
        scratch_shapes=[
            pltpu.SMEM((nblk,), I32), *[pltpu.VMEM(shape, F32) for shape in shapes],
            buf(nblk), buf(half_rows), buf(half_rows), buf(half_rows),
            buf(2, chunk // 2), buf(2, chunk // 2),
            buf(2, chunk), buf(2, chunk), buf(chunk), buf(chunk),
            buf(NY - 1, piece), buf(NX - 1, piece), buf(2 * piece),
            buf(NZ - 1, JR), buf(NX, JR),
            buf(NX - 1, half_z), buf(half_z), buf(NZ, 8), buf(NZ, 8), buf(NZ, 8),
            buf(3 * blk), buf(NX - 1, 3 * blk),
            dma, dma((5,)), dma, dma((2 * NX,)), dma((15,)), dma((15,)),
        ],
        compiler_params=pltpu.CompilerParams(
            collective_id=0, has_side_effects=True, vmem_limit_bytes=VMEM_BYTES),
        cost_estimate=pl.CostEstimate(
            flops=nblk * LANES, bytes_accessed=nblk * LANES * 4, transcendentals=0),
    )(prepared[0].reshape(nblk), *prepared[1:], grad_local[0, 0])
    return adamw_update(result[0:blk], result[blk:2 * blk], result[2 * blk:3 * blk],
                        result[3 * blk:4 * blk])


def solution(mesh):
    return jax.shard_map(
        on_device,
        mesh=mesh,
        in_specs=(
            P("replica", "dp", None, None),
            P("replica", "dp", None),
            P("replica", "dp", None),
            P("replica", "dp", None),
            P(),
            P(),
            P(),
            P(),
        ),
        out_specs=(P("dp", None), P("dp", None), P("dp", None)),
        check_vma=False,
    )
```

```python
import functools
import math

import jax
import jax.numpy as jnp
from jax import lax
from jax.experimental import pallas as pl
from jax.experimental.pallas import tpu as pltpu
from jax.sharding import PartitionSpec as P

BETA_ONE = 0.9
BETA_TWO = 0.95
BIAS_FIRST = 1.0 - 0.9**10
BIAS_SECOND = 1.0 - 0.95**10
EPSILON = 1e-08
LEARN_RATE = 0.1
DECAY_RATE = 0.1

NX = 4
NY = 4
NZ = 16
JR = 8
LANES = 128
UNROLL = 32
VMEM_BYTES = 63 * 2**20

MESH = pl.DeviceIdType.MESH
F32 = jnp.float32
BF16 = jnp.bfloat16
I32 = jnp.int32


def log2(n):
    return int(math.log2(n))


def iota(shape, dim):
    return lax.broadcasted_iota(I32, shape, dim)


def three_parts(value):
    one = value.astype(BF16)
    rest = value - one.astype(F32)
    two = rest.astype(BF16)
    three = (rest - two.astype(F32)).astype(BF16)
    return one, two, three


def pick(onehot, parts):
    total = jnp.dot(onehot, parts[2], preferred_element_type=F32)
    total = total + jnp.dot(onehot, parts[1], preferred_element_type=F32)
    return total + jnp.dot(onehot, parts[0], preferred_element_type=F32)


def prepare_order(owner_ref, slot_ref, order_ref):
    rows = owner_ref.shape[0]
    zh = NZ // 2
    owner = owner_ref[...]
    slot = slot_ref[...]
    oy = owner >> log2(2 * NZ)
    oz = (owner >> 1) & (NZ - 1)
    oc = owner & 1
    ox = slot >> log2(JR)
    oj = slot & (JR - 1)
    half = oz >> log2(zh)
    zl = oz & (zh - 1)
    first = jnp.where(half == 0, ox, oy)
    second = jnp.where(half == 0, oy, ox)
    pos = ((((oc * 2 + half) * NX + first) * NY + second) * zh + zl) * JR + oj
    pos_row = pos >> 7
    pos_col = pos & 127
    row_pad = max(rows, 8)
    sub_row = iota((row_pad, LANES), 0)
    sub_col = iota((LANES, LANES), 0)
    lane = iota((1, LANES), 1)
    left, right = [], []
    for r in range(rows):
        hit = sub_row == pos_row[r:r + 1, :]
        high = (2 * r + (lane >> 6)).astype(F32)
        low = (lane & 63).astype(F32)
        left.append(jnp.concatenate(
            [jnp.where(hit, high, 0.0), jnp.where(hit, low, 0.0)], axis=0).astype(BF16))
        right.append(jnp.where(sub_col == pos_col[r:r + 1, :], 1.0, 0.0).astype(BF16))
    both = lax.dot_general(
        jnp.concatenate(left, axis=1), jnp.concatenate(right, axis=1),
        (((1,), (1,)), ((), ())), preferred_element_type=F32)
    order = both[:row_pad] * 64.0 + both[row_pad:]
    order_ref[...] = order[:rows].astype(I32)


def prepare_state(owner_ref, slot_ref, source_ref, m_ref, v_ref, w_ref, lost_ref,
                  masked_ref, wout_ref, wsel_ref, wstay_ref, aux_ref):
    blk = NX * JR
    segs = LANES // blk
    x = lax.axis_index("replica")
    dp = lax.axis_index("dp")
    y = dp // (2 * NZ)
    c = dp % 2
    partner = dp + 1 - 2 * c
    lane = iota((1, LANES), 1)
    from_y = (x - y + NX) % NX

    living = (1 - lost_ref[...]).astype(F32)
    at_row = iota(living.shape, 0)
    at_col = iota(living.shape, 1)
    mine = jnp.sum(jnp.where((at_row == x) & (at_col == dp), living, 0.0))
    other = jnp.sum(jnp.where((at_row == x) & (at_col == partner), living, 0.0))
    aux_ref[0:8, :] = jnp.full((8, LANES), mine, F32)
    aux_ref[8:16, :] = jnp.full((8, LANES), other, F32)
    aux_ref[16:24, :] = jnp.full((8, LANES), jnp.sum(living), F32)

    seg = dp % segs
    own_row = dp // segs
    owner_row = owner_ref[pl.ds(own_row, 1), :]
    slot_row = slot_ref[pl.ds(own_row, 1), :]
    source_row = source_ref[pl.ds(own_row, 1), :]
    hit = (iota((blk, LANES), 0) + seg * blk == lane) & (source_row == x)
    mask = jnp.dot(jnp.where(hit, 1.0, 0.0).astype(BF16), jnp.ones((LANES, LANES), BF16),
                   preferred_element_type=F32)
    for k, ref in enumerate((m_ref, v_ref, w_ref)):
        chosen = jnp.where(mask > 0.5, ref[...], 0.0)
        for q in range(NX):
            masked_ref[q * 3 * JR + k * JR:q * 3 * JR + (k + 1) * JR, :] = (
                chosen[q * JR:(q + 1) * JR])

    def quarter(index):
        return (index * 43) >> 10

    col = iota((LANES, LANES), 1)
    place = seg * blk + quarter(col) * JR + (col & (JR - 1))
    spread = jnp.where((iota((LANES, LANES), 0) == place) & (col < 3 * blk), 1.0, 0.0)
    both = jnp.where(iota((8, LANES), 0) == 0, owner_row + 1, slot_row + 1).astype(F32)
    both = jnp.dot(both.astype(BF16), spread.astype(BF16), preferred_element_type=F32)
    owner_at = both[0:1, :].astype(I32)
    slot_at = both[1:2, :].astype(I32)
    kind_at = (lane - 24 * quarter(lane)) >> log2(JR)

    leaving = jnp.where(owner_at == dp + 1, -5, owner_at)
    row = iota((NZ * 8, LANES), 0)
    sub = row & 7
    core = jnp.where(sub >= 3, 1, 0)
    dest = (from_y * NZ + (row >> 3)) * 2 + core + 1
    wanted = jnp.where(sub < 6, dest, -9)
    wout_ref[...] = jnp.where((wanted == leaving) & (sub - 3 * core == kind_at), 1.0, 0.0)

    row = iota((3 * JR, LANES), 0)
    wanted = x * JR + (row & (JR - 1)) + 1
    wstay_ref[...] = jnp.where(
        (owner_at == dp + 1) & (slot_at == wanted) & ((row >> log2(JR)) == kind_at), 1.0, 0.0)

    group_rows = 2 * NZ * blk // LANES
    at = pl.ds(pl.multiple_of(from_y * group_rows, group_rows), group_rows)
    block = (from_y * group_rows + iota((group_rows, LANES), 0)) * LANES + iota((group_rows, LANES), 1)
    coming = (owner_ref[at, :] == dp) & ((block >> log2(blk)) != dp)
    named = jnp.where(coming, slot_ref[at, :] + 1, 0).astype(F32)
    cols = 2 * NZ * 8

    def source_of(shape):
        col = iota(shape, 1)
        core = jnp.where(col >= NZ * 8, 1 - c, c)
        return ((col & (NZ * 8 - 1)) >> 3) * 2 + core

    spread = jnp.where(
        (iota((LANES, cols), 0) >> log2(blk)) == (source_of((LANES, cols)) & (segs - 1)), 1.0, 0.0)
    table = jnp.dot(named.astype(BF16), spread.astype(BF16), preferred_element_type=F32)
    row_of = source_of((8, cols)) >> log2(segs)
    slots = jnp.sum(jnp.where(iota((8, cols), 0) == row_of, table, 0.0), axis=0, keepdims=True)
    row = iota((3 * blk, cols), 0)
    kind = (row - 24 * quarter(row)) >> log2(JR)
    sub = iota((3 * blk, cols), 1) & 7
    wanted = (quarter(row) * JR + (row & (JR - 1)) + 1).astype(F32)
    wsel_ref[...] = jnp.where((slots == wanted) & (sub == 3 * c + kind), 1.0, 0.0)


def prepare(owner_ref, slot_ref, source_ref, m_ref, v_ref, w_ref, lost_ref,
            order_ref, masked_ref, wout_ref, wsel_ref, wstay_ref, aux_ref):
    prepare_order(owner_ref, slot_ref, order_ref)
    prepare_state(owner_ref, slot_ref, source_ref, m_ref, v_ref, w_ref, lost_ref,
                  masked_ref, wout_ref, wsel_ref, wstay_ref, aux_ref)


def exchange(order_hbm, masked_hbm, wout_hbm, wsel_hbm, wstay_hbm, aux_hbm, grad_hbm, result_ref,
             order, masked_ref, wout_ref, wsel_ref, wstay_ref, aux_ref,
             grad, csend, crecv, own, rl0, rl1, rx0, rx1, t0, t1, ry0, ry1, u, rz, gfull,
             srecv, state, ssum, r1, r2, r3, pbuf, precv, sfull,
             grad_sem, in_sem, csend_sem, crecv_sem, send_sem, recv_sem):
    blk = NX * JR
    zh = NZ // 2
    chunk = NY * zh * JR
    piece = zh * JR
    x = lax.axis_index("replica")
    dp = lax.axis_index("dp")
    y = dp // (2 * NZ)
    z = (dp // 2) % NZ
    c = dp % 2

    def device(dx=0, dy=0, dz=0, dc=0):
        to_y = (y + dy) % NY
        to_z = (z + dz) % NZ
        to_c = (c + dc) % 2
        return ((to_y * NZ + to_z) * 2 + to_c, (x + dx) % NX)

    pairs = ((order_hbm, order), (masked_hbm, masked_ref), (wout_hbm, wout_ref),
             (wsel_hbm, wsel_ref), (wstay_hbm, wstay_ref), (aux_hbm, aux_ref))
    small = [pltpu.make_async_copy(src, dst, in_sem.at[i]) for i, (src, dst) in enumerate(pairs)]
    for copy in small:
        copy.start()
    load = pltpu.make_async_copy(grad_hbm, grad, grad_sem)
    load.start()

    barrier = pltpu.get_barrier_semaphore()
    peers = ([dict(dc=1)] + [dict(dx=k) for k in range(1, NX)]
             + [dict(dy=k) for k in range(1, NY)])
    for peer in peers:
        pl.semaphore_signal(barrier, inc=1, device_id=device(**peer), device_id_type=MESH)

    def greet(k, carry):
        pl.semaphore_signal(barrier, inc=1, device_id=device(dz=k), device_id_type=MESH)
        return carry

    lax.fori_loop(1, NZ, greet, 0)

    def send(src, dst, to, s_sem, r_sem):
        pltpu.make_async_remote_copy(
            src_ref=src, dst_ref=dst, send_sem=s_sem, recv_sem=r_sem,
            device_id=to, device_id_type=MESH).start()

    def await_bytes(ref, sem):
        pltpu.make_async_copy(ref, ref, sem).wait()

    grad_rows = grad.reshape(grad.shape[0], 1, LANES)

    def gather(dst, dst_base, base):
        dst_rows = dst.reshape(dst.shape[0], 1, LANES)

        def step(i, carry):
            at = i * UNROLL
            values = [grad_rows[order[base + at + k]] for k in range(UNROLL)]
            for k in range(UNROLL):
                dst_rows[dst_base + at + k] = values[k]
            return carry

        lax.fori_loop(0, chunk // UNROLL, step, 0)

    chunks = []
    for k in (2, 1, 3, 0):
        chunks.append((0, k, pl.multiple_of(((x + k) % NX) * chunk, chunk)))
        chunks.append((1, k, pl.multiple_of((NX + (y + k) % NY) * chunk, chunk)))

    for copy in small:
        copy.wait()
    load.wait()
    core_rows = 2 * NX * chunk
    share = 3 * JR
    my_share = pl.ds(pl.multiple_of(x * share, share), share)

    def for_partner(i):
        base = chunks[i][2]
        gather(csend, base, (1 - c) * core_rows + base)
        if i == 0:
            pl.semaphore_wait(barrier, len(peers) + NZ - 1)
            for dx in range(1, NX):
                at = pl.ds(pl.multiple_of(((x + dx) % NX) * share, share), share)
                send(masked_ref.at[at], srecv.at[dx - 1], device(dx=dx), send_sem.at[0], recv_sem.at[0])
        rows = pl.ds(base, chunk)
        send(csend.at[rows], crecv.at[rows], device(dc=1), csend_sem, crecv_sem.at[i])

    alive_mine = aux_ref[0:1, :]
    alive_other = aux_ref[8:9, :]
    partner_y = (x - y + NX) % NX
    part = chunk // 2
    relays, landings = (rl0, rl1), (rx0, rx1)

    def pass_on(i):
        h, k, base = chunks[i]
        axis = "dx" if h == 0 else "dy"
        side = 0 if k == 1 else 1
        rows = pl.ds(pl.multiple_of(base + side * part, part), part)
        await_bytes(relays[h].at[side], recv_sem.at[11 + 2 * h + side])
        own[rows, :] = own[rows, :] + relays[h][side]
        send(own.at[rows], landings[h].at[side, side * part:(side + 1) * part],
             device(**{axis: 1 - 2 * side}), send_sem.at[1 + h], recv_sem.at[1 + h])

    def for_me(i):
        h, k, base = chunks[i]
        gather(own, base, c * core_rows + base)
        rows = pl.ds(base, chunk)
        await_bytes(crecv.at[rows], crecv_sem.at[i])
        own[rows, :] = own[rows, :] * alive_mine + crecv[rows, :] * alive_other
        axis = "dx" if h == 0 else "dy"
        low = pl.ds(base, part)
        high = pl.ds(pl.multiple_of(base + part, part), part)
        up, down = device(**{axis: 1}), device(**{axis: -1})
        relay, landing = relays[h], landings[h]
        straight = (send_sem.at[1 + h], recv_sem.at[1 + h])
        if k == 2:
            send(own.at[low], relay.at[0], up, send_sem.at[11 + 2 * h], recv_sem.at[11 + 2 * h])
            send(own.at[high], relay.at[1], down, send_sem.at[12 + 2 * h], recv_sem.at[12 + 2 * h])
        elif k == 1:
            send(own.at[high], landing.at[0, part:chunk], up, *straight)
        elif k == 3:
            send(own.at[low], landing.at[1, 0:part], down, *straight)
        for earlier in {3: [2], 4: [3], 5: [4, 5]}.get(i, []):
            pass_on(earlier)
        if i == 0:
            await_bytes(srecv, recv_sem.at[0])
            state[x] = masked_ref[my_share, :] + srecv[0] + srecv[1] + srecv[2]
            for dx in range(1, NX):
                send(state.at[x], state.at[x], device(dx=dx), send_sem.at[15], recv_sem.at[15])
        if i == 2:
            await_bytes(state.at[0:NX - 1], recv_sem.at[15])
            parts = three_parts(state[...].reshape(3 * blk, LANES))
            ssum[...] = pick(wout_ref[:, 0:3 * blk].astype(BF16), parts)
            sfull[x] = pick(wstay_ref[:, 0:3 * blk].astype(BF16), parts)
            r1[z] = ssum[pl.ds(pl.multiple_of(z * 8, 8), 8), :]

            def spread(kz, carry):
                to_z = (z + kz) % NZ
                send(ssum.at[pl.ds(pl.multiple_of(to_z * 8, 8), 8)], r1.at[z],
                     device(dz=kz), send_sem.at[3], recv_sem.at[3])
                return carry

            lax.fori_loop(1, NZ, spread, 0)

    lag = 3
    for i in range(len(chunks) + lag):
        if i < len(chunks):
            for_partner(i)
        if i >= lag:
            for_me(i - lag)

    own0 = pl.multiple_of(x * chunk, chunk)
    own1 = pl.multiple_of((NX + y) * chunk, chunk)
    await_bytes(rx0, recv_sem.at[1])
    t0[...] = own[pl.ds(own0, chunk), :] + rx0[0] + rx0[1]
    for k in range(1, NY):
        at = pl.ds(pl.multiple_of(((y + k) % NY) * piece, piece), piece)
        send(t0.at[at], ry0.at[k - 1], device(dy=k), send_sem.at[4], recv_sem.at[4])
    await_bytes(rx1, recv_sem.at[2])
    t1[...] = own[pl.ds(own1, chunk), :] + rx1[0] + rx1[1]
    for k in range(1, NX):
        at = pl.ds(pl.multiple_of(((x + k) % NX) * piece, piece), piece)
        send(t1.at[at], ry1.at[k - 1], device(dx=k), send_sem.at[5], recv_sem.at[5])

    await_bytes(r1.at[0:NZ - 1], recv_sem.at[3])
    partner = ((partner_y * NZ + z) * 2 + c, x)

    @pl.when(partner_y != y)
    def _():
        send(r1, r2, partner, send_sem.at[6], recv_sem.at[6])

    @pl.when(partner_y == y)
    def _():
        r2[...] = r1[...]

    await_bytes(ry0, recv_sem.at[4])
    total = t0[pl.ds(pl.multiple_of(y * piece, piece), piece), :]
    for k in range(NY - 1):
        total = total + ry0[k]
    u[0:piece, :] = total
    await_bytes(ry1, recv_sem.at[5])
    total = t1[pl.ds(pl.multiple_of(x * piece, piece), piece), :]
    for k in range(NX - 1):
        total = total + ry1[k]
    u[piece:2 * piece, :] = total

    def scatter(kz, carry):
        to_z = (z + kz) % NZ
        send(u.at[pl.ds(pl.multiple_of(to_z * JR, JR), JR)], rz.at[kz - 1],
             device(dz=kz), send_sem.at[7], recv_sem.at[7])
        return carry

    lax.fori_loop(1, NZ, scatter, 0)

    @pl.when(partner_y != y)
    def _():
        await_bytes(r2, recv_sem.at[6])

    send(r2, r3, device(dc=1), send_sem.at[8], recv_sem.at[8])
    half = NZ * 8
    near = three_parts(r2[...].reshape(half, LANES))
    total = pick(wsel_ref[:, 0:half].astype(BF16), near)
    await_bytes(r3, recv_sem.at[8])
    far = three_parts(r3[...].reshape(half, LANES))
    pbuf[...] = total + pick(wsel_ref[:, half:2 * half].astype(BF16), far)
    for k in range(1, NX):
        at = pl.ds(pl.multiple_of(((x + k) % NX) * share, share), share)
        send(pbuf.at[at], precv.at[k - 1], device(dx=k), send_sem.at[9], recv_sem.at[9])
    await_bytes(precv, recv_sem.at[9])
    sfull[x] = sfull[x] + pbuf[my_share, :] + precv[0] + precv[1] + precv[2]
    for k in range(1, NX):
        send(sfull.at[x], sfull.at[x], device(dx=k), send_sem.at[16], recv_sem.at[16])

    await_bytes(rz, recv_sem.at[7])
    total = u[pl.ds(pl.multiple_of(z * JR, JR), JR), :]
    for k in range(NZ - 1):
        total = total + rz[k]
    gfull[x] = total
    for k in range(1, NX):
        send(gfull.at[x], gfull.at[x], device(dx=k), send_sem.at[10], recv_sem.at[10])

    await_bytes(sfull.at[0:NX - 1], recv_sem.at[16])
    for q in range(NX):
        for k in range(3):
            result_ref[k * blk + q * JR:k * blk + (q + 1) * JR, :] = sfull[q, k * JR:(k + 1) * JR, :]
    await_bytes(gfull.at[0:NX - 1], recv_sem.at[10])
    result_ref[3 * blk:4 * blk, :] = gfull[...].reshape(blk, LANES) / aux_ref[16:17, :]

    await_bytes(csend, csend_sem)
    for ref, n in ((srecv, 0), (rx0, 1), (rx1, 2),
                   (rl0.at[0], 11), (rl0.at[1], 12), (rl1.at[0], 13), (rl1.at[1], 14), (r1.at[0:NZ - 1], 3), (ry0, 4), (ry1, 5),
                   (rz, 7), (r3, 8), (precv, 9), (gfull.at[0:NX - 1], 10),
                   (state.at[0:NX - 1], 15), (sfull.at[0:NX - 1], 16)):
        await_bytes(ref, send_sem.at[n])

    @pl.when(partner_y != y)
    def _():
        await_bytes(r1, send_sem.at[6])


def adamw_update(moment_one, moment_two, weight, gradient_rows):
    first = BETA_ONE * moment_one + (1.0 - BETA_ONE) * gradient_rows
    second = BETA_TWO * moment_two + (1.0 - BETA_TWO) * gradient_rows * gradient_rows
    update = first / BIAS_FIRST / (jnp.sqrt(second / BIAS_SECOND) + EPSILON)
    return (first, second, weight - LEARN_RATE * (update + DECAY_RATE * weight))


def on_device(grad_local, first_moment, second_moment, master_weight, lost_rows, source,
              new_owner, new_slot):
    blk = NX * JR
    nblk = new_owner.shape[0]
    rows = nblk // LANES
    half_z = NZ * 8
    zh = NZ // 2
    chunk = NY * zh * JR
    piece = zh * JR
    half_rows = 2 * NX * chunk

    def buf(*shape):
        return pltpu.VMEM(shape + (LANES,), F32)

    def whole(*shape):
        return pl.BlockSpec(shape, lambda i: (0, 0))

    table = (rows, LANES)
    shapes = ((3 * blk, LANES), (half_z, LANES), (3 * blk, 2 * half_z), (3 * JR, LANES), (24, LANES))
    prepared = pl.pallas_call(
        prepare,
        grid=(1,),
        out_shape=[jax.ShapeDtypeStruct(table, I32)]
        + [jax.ShapeDtypeStruct(shape, F32) for shape in shapes],
        in_specs=[whole(*table)] * 3 + [whole(blk, LANES)] * 3 + [whole(*lost_rows.shape)],
        out_specs=[whole(*table)] + [whole(*shape) for shape in shapes],
        compiler_params=pltpu.CompilerParams(vmem_limit_bytes=VMEM_BYTES),
    )(new_owner.reshape(table), new_slot.reshape(table), source.reshape(table),
      first_moment[0], second_moment[0], master_weight[0], lost_rows)
    dma = pltpu.SemaphoreType.DMA
    result = pl.pallas_call(
        exchange,
        out_shape=jax.ShapeDtypeStruct((4 * blk, LANES), F32),
        in_specs=[pl.BlockSpec(memory_space=pl.ANY)] * 7,
        out_specs=pl.BlockSpec(memory_space=pltpu.VMEM),
        scratch_shapes=[
            pltpu.SMEM((nblk,), I32), *[pltpu.VMEM(shape, F32) for shape in shapes],
            buf(nblk), buf(half_rows), buf(half_rows), buf(half_rows),
            buf(2, chunk // 2), buf(2, chunk // 2),
            buf(2, chunk), buf(2, chunk), buf(chunk), buf(chunk),
            buf(NY - 1, piece), buf(NX - 1, piece), buf(2 * piece),
            buf(NZ - 1, JR), buf(NX, JR),
            buf(NX - 1, 3 * JR), buf(NX, 3 * JR), buf(half_z), buf(NZ, 8), buf(NZ, 8), buf(NZ, 8),
            buf(3 * blk), buf(NX - 1, 3 * JR), buf(NX, 3 * JR),
            dma, dma((6,)), dma, dma((2 * NX,)), dma((17,)), dma((17,)),
        ],
        compiler_params=pltpu.CompilerParams(
            collective_id=0, has_side_effects=True, vmem_limit_bytes=VMEM_BYTES),
        cost_estimate=pl.CostEstimate(
            flops=nblk * LANES, bytes_accessed=nblk * LANES * 4, transcendentals=0),
    )(prepared[0].reshape(nblk), *prepared[1:], grad_local[0, 0])
    return adamw_update(result[0:blk], result[blk:2 * blk], result[2 * blk:3 * blk],
                        result[3 * blk:4 * blk])


def solution(mesh):
    return jax.shard_map(
        on_device,
        mesh=mesh,
        in_specs=(
            P("replica", "dp", None, None),
            P("replica", "dp", None),
            P("replica", "dp", None),
            P("replica", "dp", None),
            P(),
            P(),
            P(),
            P(),
        ),
        out_specs=(P("dp", None), P("dp", None), P("dp", None)),
        check_vma=False,
    )
```

```python
import functools
import math

import jax
import jax.numpy as jnp
from jax import lax
from jax.experimental import pallas as pl
from jax.experimental.pallas import tpu as pltpu
from jax.sharding import PartitionSpec as P

BETA_ONE = 0.9
BETA_TWO = 0.95
BIAS_FIRST = 1.0 - 0.9**10
BIAS_SECOND = 1.0 - 0.95**10
EPSILON = 1e-08
LEARN_RATE = 0.1
DECAY_RATE = 0.1

NX = 4
NY = 4
NZ = 16
JR = 8
LANES = 128
UNROLL = 32
VMEM_BYTES = 63 * 2**20

MESH = pl.DeviceIdType.MESH
F32 = jnp.float32
BF16 = jnp.bfloat16
I32 = jnp.int32


def log2(n):
    return int(math.log2(n))


def iota(shape, dim):
    return lax.broadcasted_iota(I32, shape, dim)


def three_parts(value):
    one = value.astype(BF16)
    rest = value - one.astype(F32)
    two = rest.astype(BF16)
    three = (rest - two.astype(F32)).astype(BF16)
    return one, two, three


def pick(onehot, parts):
    total = jnp.dot(onehot, parts[2], preferred_element_type=F32)
    total = total + jnp.dot(onehot, parts[1], preferred_element_type=F32)
    return total + jnp.dot(onehot, parts[0], preferred_element_type=F32)


def prepare_order(owner_ref, slot_ref, order_ref):
    rows = owner_ref.shape[0]
    zh = NZ // 2
    owner = owner_ref[...]
    slot = slot_ref[...]
    oy = owner >> log2(2 * NZ)
    oz = (owner >> 1) & (NZ - 1)
    oc = owner & 1
    ox = slot >> log2(JR)
    oj = slot & (JR - 1)
    half = oz >> log2(zh)
    zl = oz & (zh - 1)
    first = jnp.where(half == 0, ox, oy)
    second = jnp.where(half == 0, oy, ox)
    pos = ((((oc * 2 + half) * NX + first) * NY + second) * zh + zl) * JR + oj
    pos_row = pos >> 7
    pos_col = pos & 127
    row_pad = max(rows, 8)
    sub_row = iota((row_pad, LANES), 0)
    sub_col = iota((LANES, LANES), 0)
    lane = iota((1, LANES), 1)
    left, right = [], []
    for r in range(rows):
        hit = sub_row == pos_row[r:r + 1, :]
        high = (2 * r + (lane >> 6)).astype(F32)
        low = (lane & 63).astype(F32)
        left.append(jnp.concatenate(
            [jnp.where(hit, high, 0.0), jnp.where(hit, low, 0.0)], axis=0).astype(BF16))
        right.append(jnp.where(sub_col == pos_col[r:r + 1, :], 1.0, 0.0).astype(BF16))
    both = lax.dot_general(
        jnp.concatenate(left, axis=1), jnp.concatenate(right, axis=1),
        (((1,), (1,)), ((), ())), preferred_element_type=F32)
    order = both[:row_pad] * 64.0 + both[row_pad:]
    order_ref[...] = order[:rows].astype(I32)


def prepare_state(owner_ref, slot_ref, source_ref, m_ref, v_ref, w_ref, lost_ref,
                  masked_ref, wout_ref, wsel_ref, wstay_ref, aux_ref):
    blk = NX * JR
    segs = LANES // blk
    x = lax.axis_index("replica")
    dp = lax.axis_index("dp")
    y = dp // (2 * NZ)
    c = dp % 2
    partner = dp + 1 - 2 * c
    lane = iota((1, LANES), 1)
    from_y = (x - y + NX) % NX

    living = (1 - lost_ref[...]).astype(F32)
    at_row = iota(living.shape, 0)
    at_col = iota(living.shape, 1)
    mine = jnp.sum(jnp.where((at_row == x) & (at_col == dp), living, 0.0))
    other = jnp.sum(jnp.where((at_row == x) & (at_col == partner), living, 0.0))
    aux_ref[0:8, :] = jnp.full((8, LANES), mine, F32)
    aux_ref[8:16, :] = jnp.full((8, LANES), other, F32)
    aux_ref[16:24, :] = jnp.full((8, LANES), jnp.sum(living), F32)

    seg = dp % segs
    own_row = dp // segs
    owner_row = owner_ref[pl.ds(own_row, 1), :]
    slot_row = slot_ref[pl.ds(own_row, 1), :]
    source_row = source_ref[pl.ds(own_row, 1), :]
    hit = (iota((blk, LANES), 0) + seg * blk == lane) & (source_row == x)
    mask = jnp.dot(jnp.where(hit, 1.0, 0.0).astype(BF16), jnp.ones((LANES, LANES), BF16),
                   preferred_element_type=F32)
    for k, ref in enumerate((m_ref, v_ref, w_ref)):
        chosen = jnp.where(mask > 0.5, ref[...], 0.0)
        for q in range(NX):
            masked_ref[q * 3 * JR + k * JR:q * 3 * JR + (k + 1) * JR, :] = (
                chosen[q * JR:(q + 1) * JR])

    def quarter(index):
        return (index * 43) >> 10

    col = iota((LANES, LANES), 1)
    place = seg * blk + quarter(col) * JR + (col & (JR - 1))
    spread = jnp.where((iota((LANES, LANES), 0) == place) & (col < 3 * blk), 1.0, 0.0)
    both = jnp.where(iota((8, LANES), 0) == 0, owner_row + 1, slot_row + 1).astype(F32)
    both = jnp.dot(both.astype(BF16), spread.astype(BF16), preferred_element_type=F32)
    owner_at = both[0:1, :].astype(I32)
    slot_at = both[1:2, :].astype(I32)
    kind_at = (lane - 24 * quarter(lane)) >> log2(JR)

    leaving = jnp.where(owner_at == dp + 1, -5, owner_at)
    row = iota((NZ * 8, LANES), 0)
    sub = row & 7
    core = jnp.where(sub >= 3, 1, 0)
    dest = (from_y * NZ + (row >> 3)) * 2 + core + 1
    wanted = jnp.where(sub < 6, dest, -9)
    wout_ref[...] = jnp.where((wanted == leaving) & (sub - 3 * core == kind_at), 1.0, 0.0)

    row = iota((3 * JR, LANES), 0)
    wanted = x * JR + (row & (JR - 1)) + 1
    wstay_ref[...] = jnp.where(
        (owner_at == dp + 1) & (slot_at == wanted) & ((row >> log2(JR)) == kind_at), 1.0, 0.0)

    group_rows = 2 * NZ * blk // LANES
    at = pl.ds(pl.multiple_of(from_y * group_rows, group_rows), group_rows)
    block = (from_y * group_rows + iota((group_rows, LANES), 0)) * LANES + iota((group_rows, LANES), 1)
    coming = (owner_ref[at, :] == dp) & ((block >> log2(blk)) != dp)
    named = jnp.where(coming, slot_ref[at, :] + 1, 0).astype(F32)
    cols = 2 * NZ * 8

    def source_of(shape):
        col = iota(shape, 1)
        core = jnp.where(col >= NZ * 8, 1 - c, c)
        return ((col & (NZ * 8 - 1)) >> 3) * 2 + core

    spread = jnp.where(
        (iota((LANES, cols), 0) >> log2(blk)) == (source_of((LANES, cols)) & (segs - 1)), 1.0, 0.0)
    table = jnp.dot(named.astype(BF16), spread.astype(BF16), preferred_element_type=F32)
    row_of = source_of((8, cols)) >> log2(segs)
    slots = jnp.sum(jnp.where(iota((8, cols), 0) == row_of, table, 0.0), axis=0, keepdims=True)
    row = iota((3 * blk, cols), 0)
    kind = (row - 24 * quarter(row)) >> log2(JR)
    sub = iota((3 * blk, cols), 1) & 7
    wanted = (quarter(row) * JR + (row & (JR - 1)) + 1).astype(F32)
    wsel_ref[...] = jnp.where((slots == wanted) & (sub == 3 * c + kind), 1.0, 0.0)


def prepare(owner_ref, slot_ref, source_ref, m_ref, v_ref, w_ref, lost_ref,
            order_ref, masked_ref, wout_ref, wsel_ref, wstay_ref, aux_ref):
    prepare_order(owner_ref, slot_ref, order_ref)
    prepare_state(owner_ref, slot_ref, source_ref, m_ref, v_ref, w_ref, lost_ref,
                  masked_ref, wout_ref, wsel_ref, wstay_ref, aux_ref)


def exchange(order_hbm, masked_hbm, wout_hbm, wsel_hbm, wstay_hbm, aux_hbm, grad_hbm, result_ref,
             order, masked_ref, wout_ref, wsel_ref, wstay_ref, aux_ref,
             grad, csend, crecv, own, rl0, rl1, rx0, rx1, t0, t1, ry0, ry1, u, rz, gfull,
             srecv, state, ssum, r2, r3, pbuf, precv, sfull,
             grad_sem, in_sem, csend_sem, crecv_sem, send_sem, recv_sem):
    blk = NX * JR
    zh = NZ // 2
    chunk = NY * zh * JR
    piece = zh * JR
    x = lax.axis_index("replica")
    dp = lax.axis_index("dp")
    y = dp // (2 * NZ)
    z = (dp // 2) % NZ
    c = dp % 2

    def device(dx=0, dy=0, dz=0, dc=0):
        to_y = (y + dy) % NY
        to_z = (z + dz) % NZ
        to_c = (c + dc) % 2
        return ((to_y * NZ + to_z) * 2 + to_c, (x + dx) % NX)

    pairs = ((order_hbm, order), (masked_hbm, masked_ref), (wout_hbm, wout_ref),
             (wsel_hbm, wsel_ref), (wstay_hbm, wstay_ref), (aux_hbm, aux_ref))
    small = [pltpu.make_async_copy(src, dst, in_sem.at[i]) for i, (src, dst) in enumerate(pairs)]
    for copy in small:
        copy.start()
    load = pltpu.make_async_copy(grad_hbm, grad, grad_sem)
    load.start()

    barrier = pltpu.get_barrier_semaphore()
    peers = ([dict(dc=1)] + [dict(dx=k) for k in range(1, NX)]
             + [dict(dy=k) for k in range(1, NY)])
    for peer in peers:
        pl.semaphore_signal(barrier, inc=1, device_id=device(**peer), device_id_type=MESH)

    def greet(k, carry):
        pl.semaphore_signal(barrier, inc=1, device_id=device(dz=k), device_id_type=MESH)
        return carry

    lax.fori_loop(1, NZ, greet, 0)
    partner_y = (x - y + NX) % NX

    @pl.when(partner_y != y)
    def _():
        def greet_far(to_z, carry):
            pl.semaphore_signal(barrier, inc=1, device_id=((partner_y * NZ + to_z) * 2 + c, x),
                                device_id_type=MESH)
            return carry

        lax.fori_loop(0, NZ, greet_far, 0)

    def send(src, dst, to, s_sem, r_sem):
        pltpu.make_async_remote_copy(
            src_ref=src, dst_ref=dst, send_sem=s_sem, recv_sem=r_sem,
            device_id=to, device_id_type=MESH).start()

    def await_bytes(ref, sem):
        pltpu.make_async_copy(ref, ref, sem).wait()

    grad_rows = grad.reshape(grad.shape[0], 1, LANES)

    def gather(dst, dst_base, base):
        dst_rows = dst.reshape(dst.shape[0], 1, LANES)

        def step(i, carry):
            at = i * UNROLL
            values = [grad_rows[order[base + at + k]] for k in range(UNROLL)]
            for k in range(UNROLL):
                dst_rows[dst_base + at + k] = values[k]
            return carry

        lax.fori_loop(0, chunk // UNROLL, step, 0)

    chunks = []
    for k in (2, 1, 3, 0):
        chunks.append((0, k, pl.multiple_of(((x + k) % NX) * chunk, chunk)))
        chunks.append((1, k, pl.multiple_of((NX + (y + k) % NY) * chunk, chunk)))

    for copy in small:
        copy.wait()
    load.wait()
    core_rows = 2 * NX * chunk
    share = 3 * JR
    my_share = pl.ds(pl.multiple_of(x * share, share), share)

    def for_partner(i):
        base = chunks[i][2]
        gather(csend, base, (1 - c) * core_rows + base)
        if i == 0:
            pl.semaphore_wait(
                barrier, len(peers) + NZ - 1 + jnp.where(partner_y != y, NZ, 0).astype(I32))
            for dx in range(1, NX):
                at = pl.ds(pl.multiple_of(((x + dx) % NX) * share, share), share)
                send(masked_ref.at[at], srecv.at[dx - 1], device(dx=dx), send_sem.at[0], recv_sem.at[0])
        rows = pl.ds(base, chunk)
        send(csend.at[rows], crecv.at[rows], device(dc=1), csend_sem, crecv_sem.at[i])

    alive_mine = aux_ref[0:1, :]
    alive_other = aux_ref[8:9, :]
    part = chunk // 2
    relays, landings = (rl0, rl1), (rx0, rx1)

    def pass_on(i):
        h, k, base = chunks[i]
        axis = "dx" if h == 0 else "dy"
        side = 0 if k == 1 else 1
        rows = pl.ds(pl.multiple_of(base + side * part, part), part)
        await_bytes(relays[h].at[side], recv_sem.at[11 + 2 * h + side])
        own[rows, :] = own[rows, :] + relays[h][side]
        send(own.at[rows], landings[h].at[side, side * part:(side + 1) * part],
             device(**{axis: 1 - 2 * side}), send_sem.at[1 + h], recv_sem.at[1 + h])

    def for_me(i):
        h, k, base = chunks[i]
        gather(own, base, c * core_rows + base)
        rows = pl.ds(base, chunk)
        await_bytes(crecv.at[rows], crecv_sem.at[i])
        own[rows, :] = own[rows, :] * alive_mine + crecv[rows, :] * alive_other
        axis = "dx" if h == 0 else "dy"
        low = pl.ds(base, part)
        high = pl.ds(pl.multiple_of(base + part, part), part)
        up, down = device(**{axis: 1}), device(**{axis: -1})
        relay, landing = relays[h], landings[h]
        straight = (send_sem.at[1 + h], recv_sem.at[1 + h])
        if k == 2:
            send(own.at[low], relay.at[0], up, send_sem.at[11 + 2 * h], recv_sem.at[11 + 2 * h])
            send(own.at[high], relay.at[1], down, send_sem.at[12 + 2 * h], recv_sem.at[12 + 2 * h])
        elif k == 1:
            send(own.at[high], landing.at[0, part:chunk], up, *straight)
        elif k == 3:
            send(own.at[low], landing.at[1, 0:part], down, *straight)
        for earlier in {3: [2], 4: [3], 5: [4, 5]}.get(i, []):
            pass_on(earlier)
        if i == 2:
            await_bytes(srecv, recv_sem.at[0])
            state[x] = masked_ref[my_share, :] + srecv[0] + srecv[1] + srecv[2]
            for dx in range(1, NX):
                send(state.at[x], state.at[x], device(dx=dx), send_sem.at[15], recv_sem.at[15])
        if i == 5:
            await_bytes(state.at[0:NX - 1], recv_sem.at[15])
            parts = three_parts(state[...].reshape(3 * blk, LANES))
            ssum[...] = pick(wout_ref[:, 0:3 * blk].astype(BF16), parts)
            sfull[x] = pick(wstay_ref[:, 0:3 * blk].astype(BF16), parts)

            def spread(kz, carry):
                to_z = (z + kz) % NZ
                send(ssum.at[pl.ds(pl.multiple_of(to_z * 8, 8), 8)], r2.at[z],
                     ((partner_y * NZ + to_z) * 2 + c, x), send_sem.at[3], recv_sem.at[3])
                return carry

            lax.fori_loop(1, NZ, spread, 0)

            @pl.when(partner_y != y)
            def _():
                spread(0, 0)

            @pl.when(partner_y == y)
            def _():
                r2[z] = ssum[pl.ds(pl.multiple_of(z * 8, 8), 8), :]

    lag = 3
    for i in range(len(chunks) + lag):
        if i < len(chunks):
            for_partner(i)
        if i >= lag:
            for_me(i - lag)

    own0 = pl.multiple_of(x * chunk, chunk)
    own1 = pl.multiple_of((NX + y) * chunk, chunk)
    await_bytes(rx0, recv_sem.at[1])
    t0[...] = own[pl.ds(own0, chunk), :] + rx0[0] + rx0[1]
    for k in range(1, NY):
        at = pl.ds(pl.multiple_of(((y + k) % NY) * piece, piece), piece)
        send(t0.at[at], ry0.at[k - 1], device(dy=k), send_sem.at[4], recv_sem.at[4])
    await_bytes(rx1, recv_sem.at[2])
    t1[...] = own[pl.ds(own1, chunk), :] + rx1[0] + rx1[1]
    for k in range(1, NX):
        at = pl.ds(pl.multiple_of(((x + k) % NX) * piece, piece), piece)
        send(t1.at[at], ry1.at[k - 1], device(dx=k), send_sem.at[5], recv_sem.at[5])

    await_bytes(ry0, recv_sem.at[4])
    total = t0[pl.ds(pl.multiple_of(y * piece, piece), piece), :]
    for k in range(NY - 1):
        total = total + ry0[k]
    u[0:piece, :] = total
    await_bytes(ry1, recv_sem.at[5])
    total = t1[pl.ds(pl.multiple_of(x * piece, piece), piece), :]
    for k in range(NX - 1):
        total = total + ry1[k]
    u[piece:2 * piece, :] = total

    def scatter(kz, carry):
        to_z = (z + kz) % NZ
        send(u.at[pl.ds(pl.multiple_of(to_z * JR, JR), JR)], rz.at[kz - 1],
             device(dz=kz), send_sem.at[7], recv_sem.at[7])
        return carry

    lax.fori_loop(1, NZ, scatter, 0)

    @pl.when(partner_y != y)
    def _():
        await_bytes(r2, recv_sem.at[3])

    @pl.when(partner_y == y)
    def _():
        await_bytes(r2.at[0:NZ - 1], recv_sem.at[3])

    send(r2, r3, device(dc=1), send_sem.at[8], recv_sem.at[8])
    half = NZ * 8
    near = three_parts(r2[...].reshape(half, LANES))
    total = pick(wsel_ref[:, 0:half].astype(BF16), near)
    await_bytes(r3, recv_sem.at[8])
    far = three_parts(r3[...].reshape(half, LANES))
    pbuf[...] = total + pick(wsel_ref[:, half:2 * half].astype(BF16), far)
    for k in range(1, NX):
        at = pl.ds(pl.multiple_of(((x + k) % NX) * share, share), share)
        send(pbuf.at[at], precv.at[k - 1], device(dx=k), send_sem.at[9], recv_sem.at[9])

    await_bytes(rz, recv_sem.at[7])
    total = u[pl.ds(pl.multiple_of(z * JR, JR), JR), :]
    for k in range(NZ - 1):
        total = total + rz[k]
    gfull[x] = total
    for k in range(1, NX):
        send(gfull.at[x], gfull.at[x], device(dx=k), send_sem.at[10], recv_sem.at[10])

    await_bytes(precv, recv_sem.at[9])
    sfull[x] = sfull[x] + pbuf[my_share, :] + precv[0] + precv[1] + precv[2]
    for k in range(1, NX):
        send(sfull.at[x], sfull.at[x], device(dx=k), send_sem.at[16], recv_sem.at[16])
    await_bytes(sfull.at[0:NX - 1], recv_sem.at[16])
    for q in range(NX):
        for k in range(3):
            result_ref[k * blk + q * JR:k * blk + (q + 1) * JR, :] = sfull[q, k * JR:(k + 1) * JR, :]
    await_bytes(gfull.at[0:NX - 1], recv_sem.at[10])
    result_ref[3 * blk:4 * blk, :] = gfull[...].reshape(blk, LANES) / aux_ref[16:17, :]

    await_bytes(csend, csend_sem)
    for ref, n in ((srecv, 0), (rx0, 1), (rx1, 2),
                   (rl0.at[0], 11), (rl0.at[1], 12), (rl1.at[0], 13), (rl1.at[1], 14), (ry0, 4), (ry1, 5),
                   (rz, 7), (r3, 8), (precv, 9), (gfull.at[0:NX - 1], 10),
                   (state.at[0:NX - 1], 15), (sfull.at[0:NX - 1], 16)):
        await_bytes(ref, send_sem.at[n])

    @pl.when(partner_y != y)
    def _():
        await_bytes(r2, send_sem.at[3])

    @pl.when(partner_y == y)
    def _():
        await_bytes(r2.at[0:NZ - 1], send_sem.at[3])


def adamw_update(moment_one, moment_two, weight, gradient_rows):
    first = BETA_ONE * moment_one + (1.0 - BETA_ONE) * gradient_rows
    second = BETA_TWO * moment_two + (1.0 - BETA_TWO) * gradient_rows * gradient_rows
    update = first / BIAS_FIRST / (jnp.sqrt(second / BIAS_SECOND) + EPSILON)
    return (first, second, weight - LEARN_RATE * (update + DECAY_RATE * weight))


def on_device(grad_local, first_moment, second_moment, master_weight, lost_rows, source,
              new_owner, new_slot):
    blk = NX * JR
    nblk = new_owner.shape[0]
    rows = nblk // LANES
    half_z = NZ * 8
    zh = NZ // 2
    chunk = NY * zh * JR
    piece = zh * JR
    half_rows = 2 * NX * chunk

    def buf(*shape):
        return pltpu.VMEM(shape + (LANES,), F32)

    def whole(*shape):
        return pl.BlockSpec(shape, lambda i: (0, 0))

    table = (rows, LANES)
    shapes = ((3 * blk, LANES), (half_z, LANES), (3 * blk, 2 * half_z), (3 * JR, LANES), (24, LANES))
    prepared = pl.pallas_call(
        prepare,
        grid=(1,),
        out_shape=[jax.ShapeDtypeStruct(table, I32)]
        + [jax.ShapeDtypeStruct(shape, F32) for shape in shapes],
        in_specs=[whole(*table)] * 3 + [whole(blk, LANES)] * 3 + [whole(*lost_rows.shape)],
        out_specs=[whole(*table)] + [whole(*shape) for shape in shapes],
        compiler_params=pltpu.CompilerParams(vmem_limit_bytes=VMEM_BYTES),
    )(new_owner.reshape(table), new_slot.reshape(table), source.reshape(table),
      first_moment[0], second_moment[0], master_weight[0], lost_rows)
    dma = pltpu.SemaphoreType.DMA
    result = pl.pallas_call(
        exchange,
        out_shape=jax.ShapeDtypeStruct((4 * blk, LANES), F32),
        in_specs=[pl.BlockSpec(memory_space=pl.ANY)] * 7,
        out_specs=pl.BlockSpec(memory_space=pltpu.VMEM),
        scratch_shapes=[
            pltpu.SMEM((nblk,), I32), *[pltpu.VMEM(shape, F32) for shape in shapes],
            buf(nblk), buf(half_rows), buf(half_rows), buf(half_rows),
            buf(2, chunk // 2), buf(2, chunk // 2),
            buf(2, chunk), buf(2, chunk), buf(chunk), buf(chunk),
            buf(NY - 1, piece), buf(NX - 1, piece), buf(2 * piece),
            buf(NZ - 1, JR), buf(NX, JR),
            buf(NX - 1, 3 * JR), buf(NX, 3 * JR), buf(half_z), buf(NZ, 8), buf(NZ, 8),
            buf(3 * blk), buf(NX - 1, 3 * JR), buf(NX, 3 * JR),
            dma, dma((6,)), dma, dma((2 * NX,)), dma((17,)), dma((17,)),
        ],
        compiler_params=pltpu.CompilerParams(
            collective_id=0, has_side_effects=True, vmem_limit_bytes=VMEM_BYTES),
        cost_estimate=pl.CostEstimate(
            flops=nblk * LANES, bytes_accessed=nblk * LANES * 4, transcendentals=0),
    )(prepared[0].reshape(nblk), *prepared[1:], grad_local[0, 0])
    return adamw_update(result[0:blk], result[blk:2 * blk], result[2 * blk:3 * blk],
                        result[3 * blk:4 * blk])


def solution(mesh):
    return jax.shard_map(
        on_device,
        mesh=mesh,
        in_specs=(
            P("replica", "dp", None, None),
            P("replica", "dp", None),
            P("replica", "dp", None),
            P("replica", "dp", None),
            P(),
            P(),
            P(),
            P(),
        ),
        out_specs=(P("dp", None), P("dp", None), P("dp", None)),
        check_vma=False,
    )
```

```python
import functools
import math

import jax
import jax.numpy as jnp
from jax import lax
from jax.experimental import pallas as pl
from jax.experimental.pallas import tpu as pltpu
from jax.sharding import PartitionSpec as P

BETA_ONE = 0.9
BETA_TWO = 0.95
BIAS_FIRST = 1.0 - 0.9**10
BIAS_SECOND = 1.0 - 0.95**10
EPSILON = 1e-08
LEARN_RATE = 0.1
DECAY_RATE = 0.1

NX = 4
NY = 4
NZ = 16
JR = 8
LANES = 128
UNROLL = 32
VMEM_BYTES = 63 * 2**20

MESH = pl.DeviceIdType.MESH
F32 = jnp.float32
BF16 = jnp.bfloat16
I32 = jnp.int32


def log2(n):
    return int(math.log2(n))


def iota(shape, dim):
    return lax.broadcasted_iota(I32, shape, dim)


def three_parts(value):
    one = value.astype(BF16)
    rest = value - one.astype(F32)
    two = rest.astype(BF16)
    three = (rest - two.astype(F32)).astype(BF16)
    return one, two, three


def pick(onehot, parts):
    total = jnp.dot(onehot, parts[2], preferred_element_type=F32)
    total = total + jnp.dot(onehot, parts[1], preferred_element_type=F32)
    return total + jnp.dot(onehot, parts[0], preferred_element_type=F32)


def prepare_order(owner_ref, slot_ref, order_ref):
    rows = owner_ref.shape[0]
    zh = NZ // 2
    owner = owner_ref[...]
    slot = slot_ref[...]
    oy = owner >> log2(2 * NZ)
    oz = (owner >> 1) & (NZ - 1)
    oc = owner & 1
    ox = slot >> log2(JR)
    oj = slot & (JR - 1)
    half = oz >> log2(zh)
    zl = oz & (zh - 1)
    first = jnp.where(half == 0, ox, oy)
    second = jnp.where(half == 0, oy, ox)
    pos = ((((oc * 2 + half) * NX + first) * NY + second) * zh + zl) * JR + oj
    pos_row = pos >> 7
    pos_col = pos & 127
    row_pad = max(rows, 8)
    sub_row = iota((row_pad, LANES), 0)
    sub_col = iota((LANES, LANES), 0)
    lane = iota((1, LANES), 1)
    left, right = [], []
    for r in range(rows):
        hit = sub_row == pos_row[r:r + 1, :]
        high = (2 * r + (lane >> 6)).astype(F32)
        low = (lane & 63).astype(F32)
        left.append(jnp.concatenate(
            [jnp.where(hit, high, 0.0), jnp.where(hit, low, 0.0)], axis=0).astype(BF16))
        right.append(jnp.where(sub_col == pos_col[r:r + 1, :], 1.0, 0.0).astype(BF16))
    both = lax.dot_general(
        jnp.concatenate(left, axis=1), jnp.concatenate(right, axis=1),
        (((1,), (1,)), ((), ())), preferred_element_type=F32)
    order = both[:row_pad] * 64.0 + both[row_pad:]
    order_ref[...] = order[:rows].astype(I32)


def prepare_state(owner_ref, slot_ref, source_ref, m_ref, v_ref, w_ref, lost_ref,
                  masked_ref, wout_ref, wsel_ref, wstay_ref, aux_ref):
    blk = NX * JR
    segs = LANES // blk
    x = lax.axis_index("replica")
    dp = lax.axis_index("dp")
    y = dp // (2 * NZ)
    c = dp % 2
    partner = dp + 1 - 2 * c
    lane = iota((1, LANES), 1)
    from_y = (x - y + NX) % NX

    living = (1 - lost_ref[...]).astype(F32)
    at_row = iota(living.shape, 0)
    at_col = iota(living.shape, 1)
    mine = jnp.sum(jnp.where((at_row == x) & (at_col == dp), living, 0.0))
    other = jnp.sum(jnp.where((at_row == x) & (at_col == partner), living, 0.0))
    aux_ref[0:8, :] = jnp.full((8, LANES), mine, F32)
    aux_ref[8:16, :] = jnp.full((8, LANES), other, F32)
    aux_ref[16:24, :] = jnp.full((8, LANES), jnp.sum(living), F32)

    seg = dp % segs
    own_row = dp // segs
    owner_row = owner_ref[pl.ds(own_row, 1), :]
    slot_row = slot_ref[pl.ds(own_row, 1), :]
    source_row = source_ref[pl.ds(own_row, 1), :]
    hit = (iota((blk, LANES), 0) + seg * blk == lane) & (source_row == x)
    mask = jnp.dot(jnp.where(hit, 1.0, 0.0).astype(BF16), jnp.ones((LANES, LANES), BF16),
                   preferred_element_type=F32)
    for k, ref in enumerate((m_ref, v_ref, w_ref)):
        chosen = jnp.where(mask > 0.5, ref[...], 0.0)
        for q in range(NX):
            masked_ref[q * 3 * JR + k * JR:q * 3 * JR + (k + 1) * JR, :] = (
                chosen[q * JR:(q + 1) * JR])

    def quarter(index):
        return (index * 43) >> 10

    col = iota((LANES, LANES), 1)
    place = seg * blk + quarter(col) * JR + (col & (JR - 1))
    spread = jnp.where((iota((LANES, LANES), 0) == place) & (col < 3 * blk), 1.0, 0.0)
    both = jnp.where(iota((8, LANES), 0) == 0, owner_row + 1, slot_row + 1).astype(F32)
    both = jnp.dot(both.astype(BF16), spread.astype(BF16), preferred_element_type=F32)
    owner_at = both[0:1, :].astype(I32)
    slot_at = both[1:2, :].astype(I32)
    kind_at = (lane - 24 * quarter(lane)) >> log2(JR)

    leaving = jnp.where(owner_at == dp + 1, -5, owner_at)
    row = iota((NZ * 8, LANES), 0)
    sub = row & 7
    core = jnp.where(sub >= 3, 1, 0)
    dest = (from_y * NZ + (row >> 3)) * 2 + core + 1
    wanted = jnp.where(sub < 6, dest, -9)
    wout_ref[...] = jnp.where((wanted == leaving) & (sub - 3 * core == kind_at), 1.0, 0.0)

    row = iota((3 * JR, LANES), 0)
    wanted = x * JR + (row & (JR - 1)) + 1
    wstay_ref[...] = jnp.where(
        (owner_at == dp + 1) & (slot_at == wanted) & ((row >> log2(JR)) == kind_at), 1.0, 0.0)

    group_rows = 2 * NZ * blk // LANES
    at = pl.ds(pl.multiple_of(from_y * group_rows, group_rows), group_rows)
    block = (from_y * group_rows + iota((group_rows, LANES), 0)) * LANES + iota((group_rows, LANES), 1)
    coming = (owner_ref[at, :] == dp) & ((block >> log2(blk)) != dp)
    named = jnp.where(coming, slot_ref[at, :] + 1, 0).astype(F32)
    cols = 2 * NZ * 8

    def source_of(shape):
        col = iota(shape, 1)
        core = jnp.where(col >= NZ * 8, 1 - c, c)
        return ((col & (NZ * 8 - 1)) >> 3) * 2 + core

    spread = jnp.where(
        (iota((LANES, cols), 0) >> log2(blk)) == (source_of((LANES, cols)) & (segs - 1)), 1.0, 0.0)
    table = jnp.dot(named.astype(BF16), spread.astype(BF16), preferred_element_type=F32)
    row_of = source_of((8, cols)) >> log2(segs)
    slots = jnp.sum(jnp.where(iota((8, cols), 0) == row_of, table, 0.0), axis=0, keepdims=True)
    row = iota((3 * blk, cols), 0)
    kind = (row - 24 * quarter(row)) >> log2(JR)
    sub = iota((3 * blk, cols), 1) & 7
    wanted = (quarter(row) * JR + (row & (JR - 1)) + 1).astype(F32)
    wsel_ref[...] = jnp.where((slots == wanted) & (sub == 3 * c + kind), 1.0, 0.0)


def prepare(owner_ref, slot_ref, source_ref, m_ref, v_ref, w_ref, lost_ref,
            order_ref, masked_ref, wout_ref, wsel_ref, wstay_ref, aux_ref):
    prepare_order(owner_ref, slot_ref, order_ref)
    prepare_state(owner_ref, slot_ref, source_ref, m_ref, v_ref, w_ref, lost_ref,
                  masked_ref, wout_ref, wsel_ref, wstay_ref, aux_ref)


def exchange(order_hbm, masked_hbm, wout_hbm, wsel_hbm, wstay_hbm, aux_hbm, grad_hbm, result_ref,
             order, masked_ref, wout_ref, wsel_ref, wstay_ref, aux_ref,
             grad, csend, crecv, own, rl0, rl1, rx0, rx1, t0, t1, ry0, ry1, u, rz, gfull,
             srecv, state, ssum, r2, r3, pbuf, precv, sfull,
             grad_sem, in_sem, csend_sem, crecv_sem, send_sem, recv_sem):
    blk = NX * JR
    zh = NZ // 2
    chunk = NY * zh * JR
    piece = zh * JR
    x = lax.axis_index("replica")
    dp = lax.axis_index("dp")
    y = dp // (2 * NZ)
    z = (dp // 2) % NZ
    c = dp % 2

    def device(dx=0, dy=0, dz=0, dc=0):
        to_y = (y + dy) % NY
        to_z = (z + dz) % NZ
        to_c = (c + dc) % 2
        return ((to_y * NZ + to_z) * 2 + to_c, (x + dx) % NX)

    pairs = ((order_hbm, order), (masked_hbm, masked_ref), (wout_hbm, wout_ref),
             (wsel_hbm, wsel_ref), (wstay_hbm, wstay_ref), (aux_hbm, aux_ref))
    small = [pltpu.make_async_copy(src, dst, in_sem.at[i]) for i, (src, dst) in enumerate(pairs)]
    for copy in small:
        copy.start()
    load = pltpu.make_async_copy(grad_hbm, grad, grad_sem)
    load.start()

    barrier = pltpu.get_barrier_semaphore()
    peers = ([dict(dc=1)] + [dict(dx=k) for k in range(1, NX)]
             + [dict(dy=k) for k in range(1, NY)])
    for peer in peers:
        pl.semaphore_signal(barrier, inc=1, device_id=device(**peer), device_id_type=MESH)

    def greet(k, carry):
        pl.semaphore_signal(barrier, inc=1, device_id=device(dz=k), device_id_type=MESH)
        return carry

    lax.fori_loop(1, NZ, greet, 0)
    partner_y = (x - y + NX) % NX

    @pl.when(partner_y != y)
    def _():
        def greet_far(to_z, carry):
            pl.semaphore_signal(barrier, inc=1, device_id=((partner_y * NZ + to_z) * 2 + c, x),
                                device_id_type=MESH)
            return carry

        lax.fori_loop(0, NZ, greet_far, 0)

    def send(src, dst, to, s_sem, r_sem):
        pltpu.make_async_remote_copy(
            src_ref=src, dst_ref=dst, send_sem=s_sem, recv_sem=r_sem,
            device_id=to, device_id_type=MESH).start()

    def await_bytes(ref, sem):
        pltpu.make_async_copy(ref, ref, sem).wait()

    grad_rows = grad.reshape(grad.shape[0], 1, LANES)

    def gather(dst, dst_base, base):
        dst_rows = dst.reshape(dst.shape[0], 1, LANES)

        def step(i, carry):
            at = i * UNROLL
            values = [grad_rows[order[base + at + k]] for k in range(UNROLL)]
            for k in range(UNROLL):
                dst_rows[dst_base + at + k] = values[k]
            return carry

        lax.fori_loop(0, chunk // UNROLL, step, 0)

    chunks = []
    for k in (2, 1, 3, 0):
        chunks.append((0, k, pl.multiple_of(((x + k) % NX) * chunk, chunk)))
        chunks.append((1, k, pl.multiple_of((NX + (y + k) % NY) * chunk, chunk)))

    for copy in small:
        copy.wait()
    load.wait()
    core_rows = 2 * NX * chunk
    share = 3 * JR
    my_share = pl.ds(pl.multiple_of(x * share, share), share)

    def for_partner(i):
        base = chunks[i][2]
        gather(csend, base, (1 - c) * core_rows + base)
        if i == 0:
            pl.semaphore_wait(
                barrier, len(peers) + NZ - 1 + jnp.where(partner_y != y, NZ, 0).astype(I32))
            for dx in range(1, NX):
                at = pl.ds(pl.multiple_of(((x + dx) % NX) * share, share), share)
                send(masked_ref.at[at], srecv.at[dx - 1], device(dx=dx), send_sem.at[0], recv_sem.at[0])
        rows = pl.ds(base, chunk)
        send(csend.at[rows], crecv.at[rows], device(dc=1), csend_sem, crecv_sem.at[i])

    alive_mine = aux_ref[0:1, :]
    alive_other = aux_ref[8:9, :]
    part = chunk // 2
    relays, landings = (rl0, rl1), (rx0, rx1)

    def pass_on(i):
        h, k, base = chunks[i]
        axis = "dx" if h == 0 else "dy"
        side = 0 if k == 1 else 1
        rows = pl.ds(pl.multiple_of(base + side * part, part), part)
        await_bytes(relays[h].at[side], recv_sem.at[11 + 2 * h + side])
        own[rows, :] = own[rows, :] + relays[h][side]
        send(own.at[rows], landings[h].at[side, side * part:(side + 1) * part],
             device(**{axis: 1 - 2 * side}), send_sem.at[1 + h], recv_sem.at[1 + h])

    def for_me(i):
        h, k, base = chunks[i]
        gather(own, base, c * core_rows + base)
        rows = pl.ds(base, chunk)
        await_bytes(crecv.at[rows], crecv_sem.at[i])
        own[rows, :] = own[rows, :] * alive_mine + crecv[rows, :] * alive_other
        axis = "dx" if h == 0 else "dy"
        low = pl.ds(base, part)
        high = pl.ds(pl.multiple_of(base + part, part), part)
        up, down = device(**{axis: 1}), device(**{axis: -1})
        relay, landing = relays[h], landings[h]
        straight = (send_sem.at[1 + h], recv_sem.at[1 + h])
        if k == 2:
            send(own.at[low], relay.at[0], up, send_sem.at[11 + 2 * h], recv_sem.at[11 + 2 * h])
            send(own.at[high], relay.at[1], down, send_sem.at[12 + 2 * h], recv_sem.at[12 + 2 * h])
        elif k == 1:
            send(own.at[high], landing.at[0, part:chunk], up, *straight)
        elif k == 3:
            send(own.at[low], landing.at[1, 0:part], down, *straight)
        if i >= 4:
            pass_on(i - 2)
        if i == 2:
            await_bytes(srecv, recv_sem.at[0])
            state[x] = masked_ref[my_share, :] + srecv[0] + srecv[1] + srecv[2]
            for dx in range(1, NX):
                send(state.at[x], state.at[x], device(dx=dx), send_sem.at[15], recv_sem.at[15])
        if i == 5:
            await_bytes(state.at[0:NX - 1], recv_sem.at[15])
            parts = three_parts(state[...].reshape(3 * blk, LANES))
            ssum[...] = pick(wout_ref[:, 0:3 * blk].astype(BF16), parts)
            sfull[x] = pick(wstay_ref[:, 0:3 * blk].astype(BF16), parts)

            def spread(kz, carry):
                to_z = (z + kz) % NZ
                send(ssum.at[pl.ds(pl.multiple_of(to_z * 8, 8), 8)], r2.at[z],
                     ((partner_y * NZ + to_z) * 2 + c, x), send_sem.at[3], recv_sem.at[3])
                return carry

            lax.fori_loop(1, NZ, spread, 0)

            @pl.when(partner_y != y)
            def _():
                spread(0, 0)

            @pl.when(partner_y == y)
            def _():
                r2[z] = ssum[pl.ds(pl.multiple_of(z * 8, 8), 8), :]

    for i in range(len(chunks)):
        for_partner(i)
    for i in range(len(chunks)):
        for_me(i)

    own0 = pl.multiple_of(x * chunk, chunk)
    own1 = pl.multiple_of((NX + y) * chunk, chunk)
    await_bytes(rx0, recv_sem.at[1])
    t0[...] = own[pl.ds(own0, chunk), :] + rx0[0] + rx0[1]
    for k in range(1, NY):
        at = pl.ds(pl.multiple_of(((y + k) % NY) * piece, piece), piece)
        send(t0.at[at], ry0.at[k - 1], device(dy=k), send_sem.at[4], recv_sem.at[4])
    await_bytes(rx1, recv_sem.at[2])
    t1[...] = own[pl.ds(own1, chunk), :] + rx1[0] + rx1[1]
    for k in range(1, NX):
        at = pl.ds(pl.multiple_of(((x + k) % NX) * piece, piece), piece)
        send(t1.at[at], ry1.at[k - 1], device(dx=k), send_sem.at[5], recv_sem.at[5])

    await_bytes(ry0, recv_sem.at[4])
    total = t0[pl.ds(pl.multiple_of(y * piece, piece), piece), :]
    for k in range(NY - 1):
        total = total + ry0[k]
    u[0:piece, :] = total
    await_bytes(ry1, recv_sem.at[5])
    total = t1[pl.ds(pl.multiple_of(x * piece, piece), piece), :]
    for k in range(NX - 1):
        total = total + ry1[k]
    u[piece:2 * piece, :] = total

    def scatter(kz, carry):
        to_z = (z + kz) % NZ
        send(u.at[pl.ds(pl.multiple_of(to_z * JR, JR), JR)], rz.at[kz - 1],
             device(dz=kz), send_sem.at[7], recv_sem.at[7])
        return carry

    lax.fori_loop(1, NZ, scatter, 0)

    @pl.when(partner_y != y)
    def _():
        await_bytes(r2, recv_sem.at[3])

    @pl.when(partner_y == y)
    def _():
        await_bytes(r2.at[0:NZ - 1], recv_sem.at[3])

    send(r2, r3, device(dc=1), send_sem.at[8], recv_sem.at[8])
    half = NZ * 8
    near = three_parts(r2[...].reshape(half, LANES))
    total = pick(wsel_ref[:, 0:half].astype(BF16), near)
    await_bytes(r3, recv_sem.at[8])
    far = three_parts(r3[...].reshape(half, LANES))
    pbuf[...] = total + pick(wsel_ref[:, half:2 * half].astype(BF16), far)
    for k in range(1, NX):
        at = pl.ds(pl.multiple_of(((x + k) % NX) * share, share), share)
        send(pbuf.at[at], precv.at[k - 1], device(dx=k), send_sem.at[9], recv_sem.at[9])

    await_bytes(rz, recv_sem.at[7])
    total = u[pl.ds(pl.multiple_of(z * JR, JR), JR), :]
    for k in range(NZ - 1):
        total = total + rz[k]
    gfull[x] = total
    for k in range(1, NX):
        send(gfull.at[x], gfull.at[x], device(dx=k), send_sem.at[10], recv_sem.at[10])

    await_bytes(precv, recv_sem.at[9])
    sfull[x] = sfull[x] + pbuf[my_share, :] + precv[0] + precv[1] + precv[2]
    for k in range(1, NX):
        send(sfull.at[x], sfull.at[x], device(dx=k), send_sem.at[16], recv_sem.at[16])
    await_bytes(sfull.at[0:NX - 1], recv_sem.at[16])
    for q in range(NX):
        for k in range(3):
            result_ref[k * blk + q * JR:k * blk + (q + 1) * JR, :] = sfull[q, k * JR:(k + 1) * JR, :]
    await_bytes(gfull.at[0:NX - 1], recv_sem.at[10])
    result_ref[3 * blk:4 * blk, :] = gfull[...].reshape(blk, LANES) / aux_ref[16:17, :]

    await_bytes(csend, csend_sem)
    for ref, n in ((srecv, 0), (rx0, 1), (rx1, 2),
                   (rl0.at[0], 11), (rl0.at[1], 12), (rl1.at[0], 13), (rl1.at[1], 14), (ry0, 4), (ry1, 5),
                   (rz, 7), (r3, 8), (precv, 9), (gfull.at[0:NX - 1], 10),
                   (state.at[0:NX - 1], 15), (sfull.at[0:NX - 1], 16)):
        await_bytes(ref, send_sem.at[n])

    @pl.when(partner_y != y)
    def _():
        await_bytes(r2, send_sem.at[3])

    @pl.when(partner_y == y)
    def _():
        await_bytes(r2.at[0:NZ - 1], send_sem.at[3])


def adamw_update(moment_one, moment_two, weight, gradient_rows):
    first = BETA_ONE * moment_one + (1.0 - BETA_ONE) * gradient_rows
    second = BETA_TWO * moment_two + (1.0 - BETA_TWO) * gradient_rows * gradient_rows
    update = first / BIAS_FIRST / (jnp.sqrt(second / BIAS_SECOND) + EPSILON)
    return (first, second, weight - LEARN_RATE * (update + DECAY_RATE * weight))


def on_device(grad_local, first_moment, second_moment, master_weight, lost_rows, source,
              new_owner, new_slot):
    blk = NX * JR
    nblk = new_owner.shape[0]
    rows = nblk // LANES
    half_z = NZ * 8
    zh = NZ // 2
    chunk = NY * zh * JR
    piece = zh * JR
    half_rows = 2 * NX * chunk

    def buf(*shape):
        return pltpu.VMEM(shape + (LANES,), F32)

    def whole(*shape):
        return pl.BlockSpec(shape, lambda i: (0, 0))

    table = (rows, LANES)
    shapes = ((3 * blk, LANES), (half_z, LANES), (3 * blk, 2 * half_z), (3 * JR, LANES), (24, LANES))
    prepared = pl.pallas_call(
        prepare,
        grid=(1,),
        out_shape=[jax.ShapeDtypeStruct(table, I32)]
        + [jax.ShapeDtypeStruct(shape, F32) for shape in shapes],
        in_specs=[whole(*table)] * 3 + [whole(blk, LANES)] * 3 + [whole(*lost_rows.shape)],
        out_specs=[whole(*table)] + [whole(*shape) for shape in shapes],
        compiler_params=pltpu.CompilerParams(vmem_limit_bytes=VMEM_BYTES),
    )(new_owner.reshape(table), new_slot.reshape(table), source.reshape(table),
      first_moment[0], second_moment[0], master_weight[0], lost_rows)
    dma = pltpu.SemaphoreType.DMA
    result = pl.pallas_call(
        exchange,
        out_shape=jax.ShapeDtypeStruct((4 * blk, LANES), F32),
        in_specs=[pl.BlockSpec(memory_space=pl.ANY)] * 7,
        out_specs=pl.BlockSpec(memory_space=pltpu.VMEM),
        scratch_shapes=[
            pltpu.SMEM((nblk,), I32), *[pltpu.VMEM(shape, F32) for shape in shapes],
            buf(nblk), buf(half_rows), buf(half_rows), buf(half_rows),
            buf(2, chunk // 2), buf(2, chunk // 2),
            buf(2, chunk), buf(2, chunk), buf(chunk), buf(chunk),
            buf(NY - 1, piece), buf(NX - 1, piece), buf(2 * piece),
            buf(NZ - 1, JR), buf(NX, JR),
            buf(NX - 1, 3 * JR), buf(NX, 3 * JR), buf(half_z), buf(NZ, 8), buf(NZ, 8),
            buf(3 * blk), buf(NX - 1, 3 * JR), buf(NX, 3 * JR),
            dma, dma((6,)), dma, dma((2 * NX,)), dma((17,)), dma((17,)),
        ],
        compiler_params=pltpu.CompilerParams(
            collective_id=0, has_side_effects=True, vmem_limit_bytes=VMEM_BYTES),
        cost_estimate=pl.CostEstimate(
            flops=nblk * LANES, bytes_accessed=nblk * LANES * 4, transcendentals=0),
    )(prepared[0].reshape(nblk), *prepared[1:], grad_local[0, 0])
    return adamw_update(result[0:blk], result[blk:2 * blk], result[2 * blk:3 * blk],
                        result[3 * blk:4 * blk])


def solution(mesh):
    return jax.shard_map(
        on_device,
        mesh=mesh,
        in_specs=(
            P("replica", "dp", None, None),
            P("replica", "dp", None),
            P("replica", "dp", None),
            P("replica", "dp", None),
            P(),
            P(),
            P(),
            P(),
        ),
        out_specs=(P("dp", None), P("dp", None), P("dp", None)),
        check_vma=False,
    )
```

```python
import functools
import math

import jax
import jax.numpy as jnp
from jax import lax
from jax.experimental import pallas as pl
from jax.experimental.pallas import tpu as pltpu
from jax.sharding import PartitionSpec as P

BETA_ONE = 0.9
BETA_TWO = 0.95
BIAS_FIRST = 1.0 - 0.9**10
BIAS_SECOND = 1.0 - 0.95**10
EPSILON = 1e-08
LEARN_RATE = 0.1
DECAY_RATE = 0.1

NX = 4
NY = 4
NZ = 16
JR = 8
LANES = 128
UNROLL = 32
VMEM_BYTES = 63 * 2**20

MESH = pl.DeviceIdType.MESH
F32 = jnp.float32
BF16 = jnp.bfloat16
I32 = jnp.int32


def log2(n):
    return int(math.log2(n))


def iota(shape, dim):
    return lax.broadcasted_iota(I32, shape, dim)


def three_parts(value):
    one = value.astype(BF16)
    rest = value - one.astype(F32)
    two = rest.astype(BF16)
    three = (rest - two.astype(F32)).astype(BF16)
    return one, two, three


def pick(onehot, parts):
    total = jnp.dot(onehot, parts[2], preferred_element_type=F32)
    total = total + jnp.dot(onehot, parts[1], preferred_element_type=F32)
    return total + jnp.dot(onehot, parts[0], preferred_element_type=F32)


def prepare_order(owner_ref, slot_ref, order_ref):
    rows = owner_ref.shape[0]
    zh = NZ // 2
    owner = owner_ref[...]
    slot = slot_ref[...]
    oy = owner >> log2(2 * NZ)
    oz = (owner >> 1) & (NZ - 1)
    oc = owner & 1
    ox = slot >> log2(JR)
    oj = slot & (JR - 1)
    half = oz >> log2(zh)
    zl = oz & (zh - 1)
    first = jnp.where(half == 0, ox, oy)
    second = jnp.where(half == 0, oy, ox)
    pos = ((((oc * 2 + half) * NX + first) * NY + second) * zh + zl) * JR + oj
    pos_row = pos >> 7
    pos_col = pos & 127
    row_pad = max(rows, 8)
    sub_row = iota((row_pad, LANES), 0)
    sub_col = iota((LANES, LANES), 0)
    lane = iota((1, LANES), 1)
    left, right = [], []
    for r in range(rows):
        hit = sub_row == pos_row[r:r + 1, :]
        high = (2 * r + (lane >> 6)).astype(F32)
        low = (lane & 63).astype(F32)
        left.append(jnp.concatenate(
            [jnp.where(hit, high, 0.0), jnp.where(hit, low, 0.0)], axis=0).astype(BF16))
        right.append(jnp.where(sub_col == pos_col[r:r + 1, :], 1.0, 0.0).astype(BF16))
    both = lax.dot_general(
        jnp.concatenate(left, axis=1), jnp.concatenate(right, axis=1),
        (((1,), (1,)), ((), ())), preferred_element_type=F32)
    order = both[:row_pad] * 64.0 + both[row_pad:]
    order_ref[...] = order[:rows].astype(I32)


def prepare_state(owner_ref, slot_ref, source_ref, m_ref, v_ref, w_ref, lost_ref,
                  out_ref, wsel_ref, stay_ref, aux_ref, held):
    blk = NX * JR
    segs = LANES // blk
    x = lax.axis_index("replica")
    dp = lax.axis_index("dp")
    y = dp // (2 * NZ)
    c = dp % 2
    partner = dp + 1 - 2 * c
    lane = iota((1, LANES), 1)

    living = (1 - lost_ref[...]).astype(F32)
    at_row = iota(living.shape, 0)
    at_col = iota(living.shape, 1)
    mine = jnp.sum(jnp.where((at_row == x) & (at_col == dp), living, 0.0))
    other = jnp.sum(jnp.where((at_row == x) & (at_col == partner), living, 0.0))
    aux_ref[0:8, :] = jnp.full((8, LANES), mine, F32)
    aux_ref[8:16, :] = jnp.full((8, LANES), other, F32)
    aux_ref[16:24, :] = jnp.full((8, LANES), jnp.sum(living), F32)

    seg = dp % segs
    held[...] = jnp.zeros_like(held)
    at = pl.ds(pl.multiple_of(seg * blk, 8), blk)
    keep = jnp.full((blk, LANES), mine, F32) > 0.5
    held[at, 0:128] = jnp.where(keep, m_ref[...], 0.0)
    held[at, 128:256] = jnp.where(keep, v_ref[...], 0.0)
    held[at, 256:384] = jnp.where(keep, w_ref[...], 0.0)
    parts = three_parts(held[...])
    own_row = dp // segs
    owner_row = owner_ref[pl.ds(own_row, 1), :]
    slot_row = slot_ref[pl.ds(own_row, 1), :]
    source_row = source_ref[pl.ds(own_row, 1), :]
    here = ((lane >> log2(blk)) == seg) & (source_row == x)

    leaving = jnp.where(here & (owner_row != dp), owner_row, -2)
    total_rows = NY * NZ * 8
    at_dest = iota((total_rows, LANES), 0)
    pair = at_dest >> 3
    sub = at_dest & 7
    result = None
    for k in range(3):
        dest = jnp.where(sub == k, 2 * pair, jnp.where(sub == 3 + k, 2 * pair + 1, -1))
        onehot = jnp.where(dest == leaving, 1.0, 0.0).astype(BF16)
        got = pick(onehot, [p[:, k * 128:(k + 1) * 128] for p in parts])
        result = got if result is None else result + got
    out_ref[...] = result

    staying = jnp.where(here & (owner_row == dp), slot_row, -1)
    onehot = jnp.where(iota((blk, LANES), 0) == staying, 1.0, 0.0).astype(BF16)
    got = pick(onehot, parts)
    for k in range(3):
        stay_ref[k * blk:(k + 1) * blk, :] = got[:, k * 128:(k + 1) * 128]

    group_rows = 2 * NZ * blk // LANES
    from_y = (x - y + NX) % NX
    at = pl.ds(pl.multiple_of(from_y * group_rows, group_rows), group_rows)
    block = (from_y * group_rows + iota((group_rows, LANES), 0)) * LANES + iota((group_rows, LANES), 1)
    coming = (owner_ref[at, :] == dp) & ((block >> log2(blk)) != dp)
    named = jnp.where(coming, slot_ref[at, :] + 1, 0).astype(F32)
    cols = 2 * NZ * 8
    def source_of(shape):
        col = iota(shape, 1)
        core = jnp.where(col >= NZ * 8, 1 - c, c)
        return ((col & (NZ * 8 - 1)) >> 3) * 2 + core
    spread = jnp.where(
        (iota((LANES, cols), 0) >> log2(blk)) == (source_of((LANES, cols)) & (segs - 1)), 1.0, 0.0)
    if group_rows < 8:
        named = jnp.concatenate([named, jnp.zeros((8 - group_rows, LANES), F32)], axis=0)
    table = jnp.dot(named.astype(BF16), spread.astype(BF16), preferred_element_type=F32)
    row_of = source_of((8, cols)) >> log2(segs)
    slots = jnp.sum(jnp.where(iota((8, cols), 0) == row_of, table, 0.0), axis=0, keepdims=True)
    at_row = iota((3 * blk, cols), 0)
    kind = at_row >> log2(blk)
    sub = iota((3 * blk, cols), 1) & 7
    wanted = ((at_row & (blk - 1)) + 1).astype(F32)
    wsel_ref[...] = jnp.where((slots == wanted) & (sub == 3 * c + kind), 1.0, 0.0)


def prepare(owner_ref, slot_ref, source_ref, m_ref, v_ref, w_ref, lost_ref,
            order_ref, out_ref, wsel_ref, stay_ref, aux_ref, held):
    prepare_order(owner_ref, slot_ref, order_ref)
    prepare_state(owner_ref, slot_ref, source_ref, m_ref, v_ref, w_ref, lost_ref,
                  out_ref, wsel_ref, stay_ref, aux_ref, held)


def exchange(order_hbm, out_hbm, wsel_hbm, stay_hbm, aux_hbm, grad_hbm, result_ref,
             order, out_ref, wsel_ref, stay_ref, aux_ref,
             grad, csend, crecv, own, rl0, rl1, rx0, rx1, t0, t1, ry0, ry1, u, rz, gfull,
             srecv, ssum, r2, r3, pbuf, precv,
             grad_sem, in_sem, csend_sem, crecv_sem, send_sem, recv_sem):
    blk = NX * JR
    zh = NZ // 2
    chunk = NY * zh * JR
    piece = zh * JR
    x = lax.axis_index("replica")
    dp = lax.axis_index("dp")
    y = dp // (2 * NZ)
    z = (dp // 2) % NZ
    c = dp % 2

    def device(dx=0, dy=0, dz=0, dc=0):
        to_y = (y + dy) % NY
        to_z = (z + dz) % NZ
        to_c = (c + dc) % 2
        return ((to_y * NZ + to_z) * 2 + to_c, (x + dx) % NX)

    pairs = ((order_hbm, order), (out_hbm, out_ref), (wsel_hbm, wsel_ref),
             (stay_hbm, stay_ref), (aux_hbm, aux_ref))
    small = [pltpu.make_async_copy(src, dst, in_sem.at[i]) for i, (src, dst) in enumerate(pairs)]
    for copy in small:
        copy.start()
    load = pltpu.make_async_copy(grad_hbm, grad, grad_sem)
    load.start()

    barrier = pltpu.get_barrier_semaphore()
    peers = ([dict(dc=1)] + [dict(dx=k) for k in range(1, NX)]
             + [dict(dy=k) for k in range(1, NY)])
    for peer in peers:
        pl.semaphore_signal(barrier, inc=1, device_id=device(**peer), device_id_type=MESH)

    def greet(k, carry):
        pl.semaphore_signal(barrier, inc=1, device_id=device(dz=k), device_id_type=MESH)
        return carry

    lax.fori_loop(1, NZ, greet, 0)
    partner_y = (x - y + NX) % NX

    @pl.when(partner_y != y)
    def _():
        def greet_far(to_z, carry):
            pl.semaphore_signal(barrier, inc=1, device_id=((partner_y * NZ + to_z) * 2 + c, x),
                                device_id_type=MESH)
            return carry

        lax.fori_loop(0, NZ, greet_far, 0)

    def send(src, dst, to, s_sem, r_sem):
        pltpu.make_async_remote_copy(
            src_ref=src, dst_ref=dst, send_sem=s_sem, recv_sem=r_sem,
            device_id=to, device_id_type=MESH).start()

    def await_bytes(ref, sem):
        pltpu.make_async_copy(ref, ref, sem).wait()

    grad_rows = grad.reshape(grad.shape[0], 1, LANES)

    def gather(dst, dst_base, base):
        dst_rows = dst.reshape(dst.shape[0], 1, LANES)

        def step(i, carry):
            at = i * UNROLL
            values = [grad_rows[order[base + at + k]] for k in range(UNROLL)]
            for k in range(UNROLL):
                dst_rows[dst_base + at + k] = values[k]
            return carry

        lax.fori_loop(0, chunk // UNROLL, step, 0)

    chunks = []
    for k in (2, 1, 3, 0):
        chunks.append((0, k, pl.multiple_of(((x + k) % NX) * chunk, chunk)))
        chunks.append((1, k, pl.multiple_of((NX + (y + k) % NY) * chunk, chunk)))

    for copy in small:
        copy.wait()
    load.wait()
    core_rows = 2 * NX * chunk

    def for_partner(i):
        base = chunks[i][2]
        gather(csend, base, (1 - c) * core_rows + base)
        if i == 0:
            pl.semaphore_wait(
                barrier, len(peers) + NZ - 1 + jnp.where(partner_y != y, NZ, 0).astype(I32))
            for dx in range(1, NX):
                to_y = (x + dx - y + NX) % NX
                send(out_ref.at[pl.ds(pl.multiple_of(to_y * NZ * 8, NZ * 8), NZ * 8)],
                     srecv.at[dx - 1], device(dx=dx), send_sem.at[0], recv_sem.at[0])
        rows = pl.ds(base, chunk)
        send(csend.at[rows], crecv.at[rows], device(dc=1), csend_sem, crecv_sem.at[i])

    alive_mine = aux_ref[0:1, :]
    alive_other = aux_ref[8:9, :]
    part = chunk // 2
    relays, landings = (rl0, rl1), (rx0, rx1)

    def pass_on(i):
        h, k, base = chunks[i]
        axis = "dx" if h == 0 else "dy"
        side = 0 if k == 1 else 1
        rows = pl.ds(pl.multiple_of(base + side * part, part), part)
        await_bytes(relays[h].at[side], recv_sem.at[11 + 2 * h + side])
        own[rows, :] = own[rows, :] + relays[h][side]
        send(own.at[rows], landings[h].at[side, side * part:(side + 1) * part],
             device(**{axis: 1 - 2 * side}), send_sem.at[1 + h], recv_sem.at[1 + h])

    def for_me(i):
        h, k, base = chunks[i]
        gather(own, base, c * core_rows + base)
        rows = pl.ds(base, chunk)
        await_bytes(crecv.at[rows], crecv_sem.at[i])
        own[rows, :] = own[rows, :] * alive_mine + crecv[rows, :] * alive_other
        axis = "dx" if h == 0 else "dy"
        low = pl.ds(base, part)
        high = pl.ds(pl.multiple_of(base + part, part), part)
        up, down = device(**{axis: 1}), device(**{axis: -1})
        relay, landing = relays[h], landings[h]
        straight = (send_sem.at[1 + h], recv_sem.at[1 + h])
        if k == 2:
            send(own.at[low], relay.at[0], up, send_sem.at[11 + 2 * h], recv_sem.at[11 + 2 * h])
            send(own.at[high], relay.at[1], down, send_sem.at[12 + 2 * h], recv_sem.at[12 + 2 * h])
        elif k == 1:
            send(own.at[high], landing.at[0, part:chunk], up, *straight)
        elif k == 3:
            send(own.at[low], landing.at[1, 0:part], down, *straight)
        for earlier in {3: [2], 4: [3], 5: [4, 5]}.get(i, []):
            pass_on(earlier)
        if i == 5:
            await_bytes(srecv, recv_sem.at[0])
            total = out_ref[pl.ds(pl.multiple_of(partner_y * NZ * 8, NZ * 8), NZ * 8), :]
            for dx in range(NX - 1):
                total = total + srecv[dx]
            ssum[...] = total

            def spread(kz, carry):
                to_z = (z + kz) % NZ
                send(ssum.at[pl.ds(pl.multiple_of(to_z * 8, 8), 8)], r2.at[z],
                     ((partner_y * NZ + to_z) * 2 + c, x), send_sem.at[3], recv_sem.at[3])
                return carry

            lax.fori_loop(1, NZ, spread, 0)

            @pl.when(partner_y != y)
            def _():
                spread(0, 0)

            @pl.when(partner_y == y)
            def _():
                r2[z] = ssum[pl.ds(pl.multiple_of(z * 8, 8), 8), :]

    lag = 3
    for i in range(len(chunks) + lag):
        if i < len(chunks):
            for_partner(i)
        if i >= lag:
            for_me(i - lag)

    own0 = pl.multiple_of(x * chunk, chunk)
    own1 = pl.multiple_of((NX + y) * chunk, chunk)
    await_bytes(rx0, recv_sem.at[1])
    t0[...] = own[pl.ds(own0, chunk), :] + rx0[0] + rx0[1]
    for k in range(1, NY):
        at = pl.ds(pl.multiple_of(((y + k) % NY) * piece, piece), piece)
        send(t0.at[at], ry0.at[k - 1], device(dy=k), send_sem.at[4], recv_sem.at[4])
    await_bytes(rx1, recv_sem.at[2])
    t1[...] = own[pl.ds(own1, chunk), :] + rx1[0] + rx1[1]
    for k in range(1, NX):
        at = pl.ds(pl.multiple_of(((x + k) % NX) * piece, piece), piece)
        send(t1.at[at], ry1.at[k - 1], device(dx=k), send_sem.at[5], recv_sem.at[5])

    await_bytes(ry0, recv_sem.at[4])
    total = t0[pl.ds(pl.multiple_of(y * piece, piece), piece), :]
    for k in range(NY - 1):
        total = total + ry0[k]
    u[0:piece, :] = total
    await_bytes(ry1, recv_sem.at[5])
    total = t1[pl.ds(pl.multiple_of(x * piece, piece), piece), :]
    for k in range(NX - 1):
        total = total + ry1[k]
    u[piece:2 * piece, :] = total

    def scatter(kz, carry):
        to_z = (z + kz) % NZ
        send(u.at[pl.ds(pl.multiple_of(to_z * JR, JR), JR)], rz.at[kz - 1],
             device(dz=kz), send_sem.at[7], recv_sem.at[7])
        return carry

    lax.fori_loop(1, NZ, scatter, 0)

    @pl.when(partner_y != y)
    def _():
        await_bytes(r2, recv_sem.at[3])

    @pl.when(partner_y == y)
    def _():
        await_bytes(r2.at[0:NZ - 1], recv_sem.at[3])

    send(r2, r3, device(dc=1), send_sem.at[8], recv_sem.at[8])
    half = NZ * 8
    near = three_parts(r2[...].reshape(half, LANES))
    total = stay_ref[...] + pick(wsel_ref[:, 0:half].astype(BF16), near)
    await_bytes(r3, recv_sem.at[8])
    far = three_parts(r3[...].reshape(half, LANES))
    pbuf[...] = total + pick(wsel_ref[:, half:2 * half].astype(BF16), far)
    for k in range(1, NX):
        send(pbuf, precv.at[k - 1], device(dx=k), send_sem.at[9], recv_sem.at[9])

    await_bytes(rz, recv_sem.at[7])
    total = u[pl.ds(pl.multiple_of(z * JR, JR), JR), :]
    for k in range(NZ - 1):
        total = total + rz[k]
    gfull[x] = total
    for k in range(1, NX):
        send(gfull.at[x], gfull.at[x], device(dx=k), send_sem.at[10], recv_sem.at[10])

    await_bytes(precv, recv_sem.at[9])
    state = pbuf[...]
    for k in range(NX - 1):
        state = state + precv[k]
    await_bytes(gfull.at[0:NX - 1], recv_sem.at[10])
    result_ref[0:3 * blk, :] = state
    result_ref[3 * blk:4 * blk, :] = gfull[...].reshape(blk, LANES) / aux_ref[16:17, :]

    await_bytes(csend, csend_sem)
    for ref, n in ((srecv, 0), (rx0, 1), (rx1, 2),
                   (rl0.at[0], 11), (rl0.at[1], 12), (rl1.at[0], 13), (rl1.at[1], 14), (ry0, 4), (ry1, 5),
                   (rz, 7), (r3, 8), (precv, 9), (gfull.at[0:NX - 1], 10)):
        await_bytes(ref, send_sem.at[n])

    @pl.when(partner_y != y)
    def _():
        await_bytes(r2, send_sem.at[3])

    @pl.when(partner_y == y)
    def _():
        await_bytes(r2.at[0:NZ - 1], send_sem.at[3])


def adamw_update(moment_one, moment_two, weight, gradient_rows):
    first = BETA_ONE * moment_one + (1.0 - BETA_ONE) * gradient_rows
    second = BETA_TWO * moment_two + (1.0 - BETA_TWO) * gradient_rows * gradient_rows
    update = first / BIAS_FIRST / (jnp.sqrt(second / BIAS_SECOND) + EPSILON)
    return (first, second, weight - LEARN_RATE * (update + DECAY_RATE * weight))


def on_device(grad_local, first_moment, second_moment, master_weight, lost_rows, source,
              new_owner, new_slot):
    blk = NX * JR
    nblk = new_owner.shape[0]
    rows = nblk // LANES
    half_z = NZ * 8
    zh = NZ // 2
    chunk = NY * zh * JR
    piece = zh * JR
    half_rows = 2 * NX * chunk

    def buf(*shape):
        return pltpu.VMEM(shape + (LANES,), F32)

    def whole(*shape):
        return pl.BlockSpec(shape, lambda i: (0, 0))

    table = (rows, LANES)
    shapes = ((NY * half_z, LANES), (3 * blk, 2 * half_z), (3 * blk, LANES), (24, LANES))
    prepared = pl.pallas_call(
        prepare,
        grid=(1,),
        out_shape=[jax.ShapeDtypeStruct(table, I32)]
        + [jax.ShapeDtypeStruct(shape, F32) for shape in shapes],
        in_specs=[whole(*table)] * 3 + [whole(blk, LANES)] * 3 + [whole(*lost_rows.shape)],
        out_specs=[whole(*table)] + [whole(*shape) for shape in shapes],
        scratch_shapes=[pltpu.VMEM((LANES, 3 * LANES), F32)],
        compiler_params=pltpu.CompilerParams(vmem_limit_bytes=VMEM_BYTES),
    )(new_owner.reshape(table), new_slot.reshape(table), source.reshape(table),
      first_moment[0], second_moment[0], master_weight[0], lost_rows)
    dma = pltpu.SemaphoreType.DMA
    result = pl.pallas_call(
        exchange,
        out_shape=jax.ShapeDtypeStruct((4 * blk, LANES), F32),
        in_specs=[pl.BlockSpec(memory_space=pl.ANY)] * 6,
        out_specs=pl.BlockSpec(memory_space=pltpu.VMEM),
        scratch_shapes=[
            pltpu.SMEM((nblk,), I32), *[pltpu.VMEM(shape, F32) for shape in shapes],
            buf(nblk), buf(half_rows), buf(half_rows), buf(half_rows),
            buf(2, chunk // 2), buf(2, chunk // 2),
            buf(2, chunk), buf(2, chunk), buf(chunk), buf(chunk),
            buf(NY - 1, piece), buf(NX - 1, piece), buf(2 * piece),
            buf(NZ - 1, JR), buf(NX, JR),
            buf(NX - 1, half_z), buf(half_z), buf(NZ, 8), buf(NZ, 8),
            buf(3 * blk), buf(NX - 1, 3 * blk),
            dma, dma((5,)), dma, dma((2 * NX,)), dma((15,)), dma((15,)),
        ],
        compiler_params=pltpu.CompilerParams(
            collective_id=0, has_side_effects=True, vmem_limit_bytes=VMEM_BYTES),
        cost_estimate=pl.CostEstimate(
            flops=nblk * LANES, bytes_accessed=nblk * LANES * 4, transcendentals=0),
    )(prepared[0].reshape(nblk), *prepared[1:], grad_local[0, 0])
    return adamw_update(result[0:blk], result[blk:2 * blk], result[2 * blk:3 * blk],
                        result[3 * blk:4 * blk])


def solution(mesh):
    return jax.shard_map(
        on_device,
        mesh=mesh,
        in_specs=(
            P("replica", "dp", None, None),
            P("replica", "dp", None),
            P("replica", "dp", None),
            P("replica", "dp", None),
            P(),
            P(),
            P(),
            P(),
        ),
        out_specs=(P("dp", None), P("dp", None), P("dp", None)),
        check_vma=False,
    )
```

```python
import functools
import math

import jax
import jax.numpy as jnp
from jax import lax
from jax.experimental import pallas as pl
from jax.experimental.pallas import tpu as pltpu
from jax.sharding import PartitionSpec as P

BETA_ONE = 0.9
BETA_TWO = 0.95
BIAS_FIRST = 1.0 - 0.9**10
BIAS_SECOND = 1.0 - 0.95**10
EPSILON = 1e-08
LEARN_RATE = 0.1
DECAY_RATE = 0.1

NX = 4
NY = 4
NZ = 16
JR = 8
LANES = 128
UNROLL = 32
VMEM_BYTES = 63 * 2**20

MESH = pl.DeviceIdType.MESH
F32 = jnp.float32
BF16 = jnp.bfloat16
I32 = jnp.int32


def log2(n):
    return int(math.log2(n))


def iota(shape, dim):
    return lax.broadcasted_iota(I32, shape, dim)


def three_parts(value):
    one = value.astype(BF16)
    rest = value - one.astype(F32)
    two = rest.astype(BF16)
    three = (rest - two.astype(F32)).astype(BF16)
    return one, two, three


def pick(onehot, parts):
    total = jnp.dot(onehot, parts[2], preferred_element_type=F32)
    total = total + jnp.dot(onehot, parts[1], preferred_element_type=F32)
    return total + jnp.dot(onehot, parts[0], preferred_element_type=F32)


def prepare_order(owner_ref, slot_ref, order_ref):
    rows = owner_ref.shape[0]
    zh = NZ // 2
    owner = owner_ref[...]
    slot = slot_ref[...]
    oy = owner >> log2(2 * NZ)
    oz = (owner >> 1) & (NZ - 1)
    oc = owner & 1
    ox = slot >> log2(JR)
    oj = slot & (JR - 1)
    half = oz >> log2(zh)
    zl = oz & (zh - 1)
    first = jnp.where(half == 0, ox, oy)
    second = jnp.where(half == 0, oy, ox)
    pos = ((((oc * 2 + half) * NX + first) * NY + second) * zh + zl) * JR + oj
    pos_row = pos >> 7
    pos_col = pos & 127
    row_pad = max(rows, 8)
    sub_row = iota((row_pad, LANES), 0)
    sub_col = iota((LANES, LANES), 0)
    lane = iota((1, LANES), 1)
    left, right = [], []
    for r in range(rows):
        hit = sub_row == pos_row[r:r + 1, :]
        high = (2 * r + (lane >> 6)).astype(F32)
        low = (lane & 63).astype(F32)
        left.append(jnp.concatenate(
            [jnp.where(hit, high, 0.0), jnp.where(hit, low, 0.0)], axis=0).astype(BF16))
        right.append(jnp.where(sub_col == pos_col[r:r + 1, :], 1.0, 0.0).astype(BF16))
    both = lax.dot_general(
        jnp.concatenate(left, axis=1), jnp.concatenate(right, axis=1),
        (((1,), (1,)), ((), ())), preferred_element_type=F32)
    order = both[:row_pad] * 64.0 + both[row_pad:]
    order_ref[...] = order[:rows].astype(I32)


def prepare_state(owner_ref, slot_ref, source_ref, m_ref, v_ref, w_ref, lost_ref,
                  out_ref, wsel_ref, stay_ref, aux_ref, held):
    blk = NX * JR
    segs = LANES // blk
    x = lax.axis_index("replica")
    dp = lax.axis_index("dp")
    y = dp // (2 * NZ)
    c = dp % 2
    partner = dp + 1 - 2 * c
    lane = iota((1, LANES), 1)

    living = (1 - lost_ref[...]).astype(F32)
    at_row = iota(living.shape, 0)
    at_col = iota(living.shape, 1)
    mine = jnp.sum(jnp.where((at_row == x) & (at_col == dp), living, 0.0))
    other = jnp.sum(jnp.where((at_row == x) & (at_col == partner), living, 0.0))
    aux_ref[0:8, :] = jnp.full((8, LANES), mine, F32)
    aux_ref[8:16, :] = jnp.full((8, LANES), other, F32)
    aux_ref[16:24, :] = jnp.full((8, LANES), jnp.sum(living), F32)

    seg = dp % segs
    held[...] = jnp.zeros_like(held)
    at = pl.ds(pl.multiple_of(seg * blk, 8), blk)
    keep = jnp.full((blk, LANES), mine, F32) > 0.5
    held[at, 0:128] = jnp.where(keep, m_ref[...], 0.0)
    held[at, 128:256] = jnp.where(keep, v_ref[...], 0.0)
    held[at, 256:384] = jnp.where(keep, w_ref[...], 0.0)
    parts = three_parts(held[...])
    own_row = dp // segs
    owner_row = owner_ref[pl.ds(own_row, 1), :]
    slot_row = slot_ref[pl.ds(own_row, 1), :]
    source_row = source_ref[pl.ds(own_row, 1), :]
    here = ((lane >> log2(blk)) == seg) & (source_row == x)

    leaving = jnp.where(here & (owner_row != dp), owner_row, -2)
    total_rows = NY * NZ * 8
    at_dest = iota((total_rows, LANES), 0)
    pair = at_dest >> 3
    sub = at_dest & 7
    result = None
    for k in range(3):
        dest = jnp.where(sub == k, 2 * pair, jnp.where(sub == 3 + k, 2 * pair + 1, -1))
        onehot = jnp.where(dest == leaving, 1.0, 0.0).astype(BF16)
        got = pick(onehot, [p[:, k * 128:(k + 1) * 128] for p in parts])
        result = got if result is None else result + got
    out_ref[...] = result

    staying = jnp.where(here & (owner_row == dp), slot_row, -1)
    onehot = jnp.where(iota((blk, LANES), 0) == staying, 1.0, 0.0).astype(BF16)
    got = pick(onehot, parts)
    for k in range(3):
        stay_ref[k * blk:(k + 1) * blk, :] = got[:, k * 128:(k + 1) * 128]

    group_rows = 2 * NZ * blk // LANES
    from_y = (x - y + NX) % NX
    at = pl.ds(pl.multiple_of(from_y * group_rows, group_rows), group_rows)
    block = (from_y * group_rows + iota((group_rows, LANES), 0)) * LANES + iota((group_rows, LANES), 1)
    coming = (owner_ref[at, :] == dp) & ((block >> log2(blk)) != dp)
    named = jnp.where(coming, slot_ref[at, :] + 1, 0).astype(F32)
    cols = 2 * NZ * 8
    def source_of(shape):
        col = iota(shape, 1)
        core = jnp.where(col >= NZ * 8, 1 - c, c)
        return ((col & (NZ * 8 - 1)) >> 3) * 2 + core
    spread = jnp.where(
        (iota((LANES, cols), 0) >> log2(blk)) == (source_of((LANES, cols)) & (segs - 1)), 1.0, 0.0)
    if group_rows < 8:
        named = jnp.concatenate([named, jnp.zeros((8 - group_rows, LANES), F32)], axis=0)
    table = jnp.dot(named.astype(BF16), spread.astype(BF16), preferred_element_type=F32)
    row_of = source_of((8, cols)) >> log2(segs)
    slots = jnp.sum(jnp.where(iota((8, cols), 0) == row_of, table, 0.0), axis=0, keepdims=True)
    at_row = iota((3 * blk, cols), 0)
    kind = at_row >> log2(blk)
    sub = iota((3 * blk, cols), 1) & 7
    wanted = ((at_row & (blk - 1)) + 1).astype(F32)
    wsel_ref[...] = jnp.where((slots == wanted) & (sub == 3 * c + kind), 1.0, 0.0)


def prepare(owner_ref, slot_ref, source_ref, m_ref, v_ref, w_ref, lost_ref,
            order_ref, out_ref, wsel_ref, stay_ref, aux_ref, held):
    prepare_order(owner_ref, slot_ref, order_ref)
    prepare_state(owner_ref, slot_ref, source_ref, m_ref, v_ref, w_ref, lost_ref,
                  out_ref, wsel_ref, stay_ref, aux_ref, held)


def exchange(order_hbm, out_hbm, wsel_hbm, stay_hbm, aux_hbm, grad_hbm, result_ref,
             order, out_ref, wsel_ref, stay_ref, aux_ref,
             grad, csend, crecv, own, rl0, rl1, rx0, rx1, t0, t1, ry0, ry1, u, rz, gfull,
             srecv, ssum, r1, r2, r3, pbuf, precv,
             grad_sem, in_sem, csend_sem, crecv_sem, send_sem, recv_sem):
    blk = NX * JR
    zh = NZ // 2
    chunk = NY * zh * JR
    piece = zh * JR
    x = lax.axis_index("replica")
    dp = lax.axis_index("dp")
    y = dp // (2 * NZ)
    z = (dp // 2) % NZ
    c = dp % 2

    def device(dx=0, dy=0, dz=0, dc=0):
        to_y = (y + dy) % NY
        to_z = (z + dz) % NZ
        to_c = (c + dc) % 2
        return ((to_y * NZ + to_z) * 2 + to_c, (x + dx) % NX)

    pairs = ((order_hbm, order), (out_hbm, out_ref), (wsel_hbm, wsel_ref),
             (stay_hbm, stay_ref), (aux_hbm, aux_ref))
    small = [pltpu.make_async_copy(src, dst, in_sem.at[i]) for i, (src, dst) in enumerate(pairs)]
    for copy in small:
        copy.start()
    load = pltpu.make_async_copy(grad_hbm, grad, grad_sem)
    load.start()

    barrier = pltpu.get_barrier_semaphore()
    peers = ([dict(dc=1)] + [dict(dx=k) for k in range(1, NX)]
             + [dict(dy=k) for k in range(1, NY)])
    for peer in peers:
        pl.semaphore_signal(barrier, inc=1, device_id=device(**peer), device_id_type=MESH)

    def greet(k, carry):
        pl.semaphore_signal(barrier, inc=1, device_id=device(dz=k), device_id_type=MESH)
        return carry

    lax.fori_loop(1, NZ, greet, 0)

    def send(src, dst, to, s_sem, r_sem):
        pltpu.make_async_remote_copy(
            src_ref=src, dst_ref=dst, send_sem=s_sem, recv_sem=r_sem,
            device_id=to, device_id_type=MESH).start()

    def await_bytes(ref, sem):
        pltpu.make_async_copy(ref, ref, sem).wait()

    grad_rows = grad.reshape(grad.shape[0], 1, LANES)

    def gather(dst, dst_base, base):
        dst_rows = dst.reshape(dst.shape[0], 1, LANES)

        def step(i, carry):
            at = i * UNROLL
            values = [grad_rows[order[base + at + k]] for k in range(UNROLL)]
            for k in range(UNROLL):
                dst_rows[dst_base + at + k] = values[k]
            return carry

        lax.fori_loop(0, chunk // UNROLL, step, 0)

    chunks = []
    for k in (2, 1, 3, 0):
        chunks.append((0, k, pl.multiple_of(((x + k) % NX) * chunk, chunk)))
        chunks.append((1, k, pl.multiple_of((NX + (y + k) % NY) * chunk, chunk)))

    for copy in small:
        copy.wait()
    load.wait()
    core_rows = 2 * NX * chunk
    for i, (h, k, base) in enumerate(chunks):
        gather(csend, base, (1 - c) * core_rows + base)
        if i == 0:
            pl.semaphore_wait(barrier, len(peers) + NZ - 1)
            for dx in range(1, NX):
                to_y = (x + dx - y + NX) % NX
                send(out_ref.at[pl.ds(pl.multiple_of(to_y * NZ * 8, NZ * 8), NZ * 8)],
                     srecv.at[dx - 1], device(dx=dx), send_sem.at[0], recv_sem.at[0])
        rows = pl.ds(base, chunk)
        send(csend.at[rows], crecv.at[rows], device(dc=1), csend_sem, crecv_sem.at[i])

    alive_mine = aux_ref[0:1, :]
    alive_other = aux_ref[8:9, :]
    partner_y = (x - y + NX) % NX
    part = chunk // 2
    relays, landings = (rl0, rl1), (rx0, rx1)

    def pass_on(i):
        h, k, base = chunks[i]
        axis = "dx" if h == 0 else "dy"
        side = 0 if k == 1 else 1
        rows = pl.ds(pl.multiple_of(base + side * part, part), part)
        await_bytes(relays[h].at[side], recv_sem.at[11 + 2 * h + side])
        own[rows, :] = own[rows, :] + relays[h][side]
        send(own.at[rows], landings[h].at[side, side * part:(side + 1) * part],
             device(**{axis: 1 - 2 * side}), send_sem.at[1 + h], recv_sem.at[1 + h])

    for i, (h, k, base) in enumerate(chunks):
        gather(own, base, c * core_rows + base)
        rows = pl.ds(base, chunk)
        await_bytes(crecv.at[rows], crecv_sem.at[i])
        own[rows, :] = own[rows, :] * alive_mine + crecv[rows, :] * alive_other
        axis = "dx" if h == 0 else "dy"
        low = pl.ds(base, part)
        high = pl.ds(pl.multiple_of(base + part, part), part)
        up, down = device(**{axis: 1}), device(**{axis: -1})
        relay, landing = relays[h], landings[h]
        straight = (send_sem.at[1 + h], recv_sem.at[1 + h])
        if k == 2:
            send(own.at[low], relay.at[0], up, send_sem.at[11 + 2 * h], recv_sem.at[11 + 2 * h])
            send(own.at[high], relay.at[1], down, send_sem.at[12 + 2 * h], recv_sem.at[12 + 2 * h])
        elif k == 1:
            send(own.at[high], landing.at[0, part:chunk], up, *straight)
        elif k == 3:
            send(own.at[low], landing.at[1, 0:part], down, *straight)
        if i >= 4:
            pass_on(i - 2)
        if i == 1:
            await_bytes(srecv, recv_sem.at[0])
            total = out_ref[pl.ds(pl.multiple_of(partner_y * NZ * 8, NZ * 8), NZ * 8), :]
            for dx in range(NX - 1):
                total = total + srecv[dx]
            ssum[...] = total
            r1[z] = ssum[pl.ds(pl.multiple_of(z * 8, 8), 8), :]

            def spread(kz, carry):
                to_z = (z + kz) % NZ
                send(ssum.at[pl.ds(pl.multiple_of(to_z * 8, 8), 8)], r1.at[z],
                     device(dz=kz), send_sem.at[3], recv_sem.at[3])
                return carry

            lax.fori_loop(1, NZ, spread, 0)

    own0 = pl.multiple_of(x * chunk, chunk)
    own1 = pl.multiple_of((NX + y) * chunk, chunk)
    await_bytes(rx0, recv_sem.at[1])
    t0[...] = own[pl.ds(own0, chunk), :] + rx0[0] + rx0[1]
    for k in range(1, NY):
        at = pl.ds(pl.multiple_of(((y + k) % NY) * piece, piece), piece)
        send(t0.at[at], ry0.at[k - 1], device(dy=k), send_sem.at[4], recv_sem.at[4])
    await_bytes(rx1, recv_sem.at[2])
    t1[...] = own[pl.ds(own1, chunk), :] + rx1[0] + rx1[1]
    for k in range(1, NX):
        at = pl.ds(pl.multiple_of(((x + k) % NX) * piece, piece), piece)
        send(t1.at[at], ry1.at[k - 1], device(dx=k), send_sem.at[5], recv_sem.at[5])

    await_bytes(r1.at[0:NZ - 1], recv_sem.at[3])
    partner = ((partner_y * NZ + z) * 2 + c, x)

    @pl.when(partner_y != y)
    def _():
        send(r1, r2, partner, send_sem.at[6], recv_sem.at[6])

    @pl.when(partner_y == y)
    def _():
        r2[...] = r1[...]

    await_bytes(ry0, recv_sem.at[4])
    total = t0[pl.ds(pl.multiple_of(y * piece, piece), piece), :]
    for k in range(NY - 1):
        total = total + ry0[k]
    u[0:piece, :] = total
    await_bytes(ry1, recv_sem.at[5])
    total = t1[pl.ds(pl.multiple_of(x * piece, piece), piece), :]
    for k in range(NX - 1):
        total = total + ry1[k]
    u[piece:2 * piece, :] = total

    def scatter(kz, carry):
        to_z = (z + kz) % NZ
        send(u.at[pl.ds(pl.multiple_of(to_z * JR, JR), JR)], rz.at[kz - 1],
             device(dz=kz), send_sem.at[7], recv_sem.at[7])
        return carry

    lax.fori_loop(1, NZ, scatter, 0)

    @pl.when(partner_y != y)
    def _():
        await_bytes(r2, recv_sem.at[6])

    send(r2, r3, device(dc=1), send_sem.at[8], recv_sem.at[8])
    half = NZ * 8
    near = three_parts(r2[...].reshape(half, LANES))
    total = stay_ref[...] + pick(wsel_ref[:, 0:half].astype(BF16), near)
    await_bytes(r3, recv_sem.at[8])
    far = three_parts(r3[...].reshape(half, LANES))
    pbuf[...] = total + pick(wsel_ref[:, half:2 * half].astype(BF16), far)
    for k in range(1, NX):
        send(pbuf, precv.at[k - 1], device(dx=k), send_sem.at[9], recv_sem.at[9])

    await_bytes(rz, recv_sem.at[7])
    total = u[pl.ds(pl.multiple_of(z * JR, JR), JR), :]
    for k in range(NZ - 1):
        total = total + rz[k]
    gfull[x] = total
    for k in range(1, NX):
        send(gfull.at[x], gfull.at[x], device(dx=k), send_sem.at[10], recv_sem.at[10])

    await_bytes(precv, recv_sem.at[9])
    state = pbuf[...]
    for k in range(NX - 1):
        state = state + precv[k]
    await_bytes(gfull.at[0:NX - 1], recv_sem.at[10])
    result_ref[0:3 * blk, :] = state
    result_ref[3 * blk:4 * blk, :] = gfull[...].reshape(blk, LANES) / aux_ref[16:17, :]

    await_bytes(csend, csend_sem)
    for ref, n in ((srecv, 0), (rx0, 1), (rx1, 2),
                   (rl0.at[0], 11), (rl0.at[1], 12), (rl1.at[0], 13), (rl1.at[1], 14), (r1.at[0:NZ - 1], 3), (ry0, 4), (ry1, 5),
                   (rz, 7), (r3, 8), (precv, 9), (gfull.at[0:NX - 1], 10)):
        await_bytes(ref, send_sem.at[n])

    @pl.when(partner_y != y)
    def _():
        await_bytes(r1, send_sem.at[6])


def adamw_update(moment_one, moment_two, weight, gradient_rows):
    first = BETA_ONE * moment_one + (1.0 - BETA_ONE) * gradient_rows
    second = BETA_TWO * moment_two + (1.0 - BETA_TWO) * gradient_rows * gradient_rows
    update = first / BIAS_FIRST / (jnp.sqrt(second / BIAS_SECOND) + EPSILON)
    return (first, second, weight - LEARN_RATE * (update + DECAY_RATE * weight))


def on_device(grad_local, first_moment, second_moment, master_weight, lost_rows, source,
              new_owner, new_slot):
    blk = NX * JR
    nblk = new_owner.shape[0]
    rows = nblk // LANES
    half_z = NZ * 8
    zh = NZ // 2
    chunk = NY * zh * JR
    piece = zh * JR
    half_rows = 2 * NX * chunk

    def buf(*shape):
        return pltpu.VMEM(shape + (LANES,), F32)

    def whole(*shape):
        return pl.BlockSpec(shape, lambda i: (0, 0))

    table = (rows, LANES)
    shapes = ((NY * half_z, LANES), (3 * blk, 2 * half_z), (3 * blk, LANES), (24, LANES))
    prepared = pl.pallas_call(
        prepare,
        grid=(1,),
        out_shape=[jax.ShapeDtypeStruct(table, I32)]
        + [jax.ShapeDtypeStruct(shape, F32) for shape in shapes],
        in_specs=[whole(*table)] * 3 + [whole(blk, LANES)] * 3 + [whole(*lost_rows.shape)],
        out_specs=[whole(*table)] + [whole(*shape) for shape in shapes],
        scratch_shapes=[pltpu.VMEM((LANES, 3 * LANES), F32)],
        compiler_params=pltpu.CompilerParams(vmem_limit_bytes=VMEM_BYTES),
    )(new_owner.reshape(table), new_slot.reshape(table), source.reshape(table),
      first_moment[0], second_moment[0], master_weight[0], lost_rows)
    dma = pltpu.SemaphoreType.DMA
    result = pl.pallas_call(
        exchange,
        out_shape=jax.ShapeDtypeStruct((4 * blk, LANES), F32),
        in_specs=[pl.BlockSpec(memory_space=pl.ANY)] * 6,
        out_specs=pl.BlockSpec(memory_space=pltpu.VMEM),
        scratch_shapes=[
            pltpu.SMEM((nblk,), I32), *[pltpu.VMEM(shape, F32) for shape in shapes],
            buf(nblk), buf(half_rows), buf(half_rows), buf(half_rows),
            buf(2, chunk // 2), buf(2, chunk // 2),
            buf(2, chunk), buf(2, chunk), buf(chunk), buf(chunk),
            buf(NY - 1, piece), buf(NX - 1, piece), buf(2 * piece),
            buf(NZ - 1, JR), buf(NX, JR),
            buf(NX - 1, half_z), buf(half_z), buf(NZ, 8), buf(NZ, 8), buf(NZ, 8),
            buf(3 * blk), buf(NX - 1, 3 * blk),
            dma, dma((5,)), dma, dma((2 * NX,)), dma((15,)), dma((15,)),
        ],
        compiler_params=pltpu.CompilerParams(
            collective_id=0, has_side_effects=True, vmem_limit_bytes=VMEM_BYTES),
        cost_estimate=pl.CostEstimate(
            flops=nblk * LANES, bytes_accessed=nblk * LANES * 4, transcendentals=0),
    )(prepared[0].reshape(nblk), *prepared[1:], grad_local[0, 0])
    return adamw_update(result[0:blk], result[blk:2 * blk], result[2 * blk:3 * blk],
                        result[3 * blk:4 * blk])


def solution(mesh):
    return jax.shard_map(
        on_device,
        mesh=mesh,
        in_specs=(
            P("replica", "dp", None, None),
            P("replica", "dp", None),
            P("replica", "dp", None),
            P("replica", "dp", None),
            P(),
            P(),
            P(),
            P(),
        ),
        out_specs=(P("dp", None), P("dp", None), P("dp", None)),
        check_vma=False,
    )
```

```python
import functools
import math

import jax
import jax.numpy as jnp
from jax import lax
from jax.experimental import pallas as pl
from jax.experimental.pallas import tpu as pltpu
from jax.sharding import PartitionSpec as P

BETA_ONE = 0.9
BETA_TWO = 0.95
BIAS_FIRST = 1.0 - 0.9**10
BIAS_SECOND = 1.0 - 0.95**10
EPSILON = 1e-08
LEARN_RATE = 0.1
DECAY_RATE = 0.1

NX = 4
NY = 4
NZ = 16
JR = 8
LANES = 128
UNROLL = 32
VMEM_BYTES = 63 * 2**20

MESH = pl.DeviceIdType.MESH
F32 = jnp.float32
BF16 = jnp.bfloat16
I32 = jnp.int32


def log2(n):
    return int(math.log2(n))


def iota(shape, dim):
    return lax.broadcasted_iota(I32, shape, dim)


def three_parts(value):
    one = value.astype(BF16)
    rest = value - one.astype(F32)
    two = rest.astype(BF16)
    three = (rest - two.astype(F32)).astype(BF16)
    return one, two, three


def pick(onehot, parts):
    total = jnp.dot(onehot, parts[2], preferred_element_type=F32)
    total = total + jnp.dot(onehot, parts[1], preferred_element_type=F32)
    return total + jnp.dot(onehot, parts[0], preferred_element_type=F32)


def prepare_order(owner_ref, slot_ref, order_ref):
    rows = owner_ref.shape[0]
    zh = NZ // 2
    owner = owner_ref[...]
    slot = slot_ref[...]
    oy = owner >> log2(2 * NZ)
    oz = (owner >> 1) & (NZ - 1)
    oc = owner & 1
    ox = slot >> log2(JR)
    oj = slot & (JR - 1)
    half = oz >> log2(zh)
    zl = oz & (zh - 1)
    first = jnp.where(half == 0, ox, oy)
    second = jnp.where(half == 0, oy, ox)
    pos = ((((oc * 2 + half) * NX + first) * NY + second) * zh + zl) * JR + oj
    pos_row = pos >> 7
    pos_col = pos & 127
    row_pad = max(rows, 8)
    sub_row = iota((row_pad, LANES), 0)
    sub_col = iota((LANES, LANES), 0)
    lane = iota((1, LANES), 1)
    left, right = [], []
    for r in range(rows):
        hit = sub_row == pos_row[r:r + 1, :]
        high = (2 * r + (lane >> 6)).astype(F32)
        low = (lane & 63).astype(F32)
        left.append(jnp.concatenate(
            [jnp.where(hit, high, 0.0), jnp.where(hit, low, 0.0)], axis=0).astype(BF16))
        right.append(jnp.where(sub_col == pos_col[r:r + 1, :], 1.0, 0.0).astype(BF16))
    both = lax.dot_general(
        jnp.concatenate(left, axis=1), jnp.concatenate(right, axis=1),
        (((1,), (1,)), ((), ())), preferred_element_type=F32)
    order = both[:row_pad] * 64.0 + both[row_pad:]
    order_ref[...] = order[:rows].astype(I32)


def prepare_state(owner_ref, slot_ref, source_ref, m_ref, v_ref, w_ref, lost_ref,
                  out_ref, wsel_ref, stay_ref, aux_ref, held):
    blk = NX * JR
    segs = LANES // blk
    x = lax.axis_index("replica")
    dp = lax.axis_index("dp")
    y = dp // (2 * NZ)
    c = dp % 2
    partner = dp + 1 - 2 * c
    lane = iota((1, LANES), 1)

    living = (1 - lost_ref[...]).astype(F32)
    at_row = iota(living.shape, 0)
    at_col = iota(living.shape, 1)
    mine = jnp.sum(jnp.where((at_row == x) & (at_col == dp), living, 0.0))
    other = jnp.sum(jnp.where((at_row == x) & (at_col == partner), living, 0.0))
    aux_ref[0:8, :] = jnp.full((8, LANES), mine, F32)
    aux_ref[8:16, :] = jnp.full((8, LANES), other, F32)
    aux_ref[16:24, :] = jnp.full((8, LANES), jnp.sum(living), F32)

    seg = dp % segs
    held[...] = jnp.zeros_like(held)
    at = pl.ds(pl.multiple_of(seg * blk, 8), blk)
    keep = jnp.full((blk, LANES), mine, F32) > 0.5
    held[at, 0:128] = jnp.where(keep, m_ref[...], 0.0)
    held[at, 128:256] = jnp.where(keep, v_ref[...], 0.0)
    held[at, 256:384] = jnp.where(keep, w_ref[...], 0.0)
    parts = three_parts(held[...])
    own_row = dp // segs
    owner_row = owner_ref[pl.ds(own_row, 1), :]
    slot_row = slot_ref[pl.ds(own_row, 1), :]
    source_row = source_ref[pl.ds(own_row, 1), :]
    here = ((lane >> log2(blk)) == seg) & (source_row == x)

    leaving = jnp.where(here & (owner_row != dp), owner_row, -2)
    total_rows = NY * NZ * 8
    at_dest = iota((total_rows, LANES), 0)
    pair = at_dest >> 3
    sub = at_dest & 7
    result = None
    for k in range(3):
        dest = jnp.where(sub == k, 2 * pair, jnp.where(sub == 3 + k, 2 * pair + 1, -1))
        onehot = jnp.where(dest == leaving, 1.0, 0.0).astype(BF16)
        got = pick(onehot, [p[:, k * 128:(k + 1) * 128] for p in parts])
        result = got if result is None else result + got
    out_ref[...] = result

    staying = jnp.where(here & (owner_row == dp), slot_row, -1)
    onehot = jnp.where(iota((blk, LANES), 0) == staying, 1.0, 0.0).astype(BF16)
    got = pick(onehot, parts)
    for k in range(3):
        stay_ref[k * blk:(k + 1) * blk, :] = got[:, k * 128:(k + 1) * 128]

    group_rows = 2 * NZ * blk // LANES
    from_y = (x - y + NX) % NX
    at = pl.ds(pl.multiple_of(from_y * group_rows, group_rows), group_rows)
    block = (from_y * group_rows + iota((group_rows, LANES), 0)) * LANES + iota((group_rows, LANES), 1)
    coming = (owner_ref[at, :] == dp) & ((block >> log2(blk)) != dp)
    named = jnp.where(coming, slot_ref[at, :] + 1, 0).astype(F32)
    cols = 2 * NZ * 8
    def source_of(shape):
        col = iota(shape, 1)
        core = jnp.where(col >= NZ * 8, 1 - c, c)
        return ((col & (NZ * 8 - 1)) >> 3) * 2 + core
    spread = jnp.where(
        (iota((LANES, cols), 0) >> log2(blk)) == (source_of((LANES, cols)) & (segs - 1)), 1.0, 0.0)
    if group_rows < 8:
        named = jnp.concatenate([named, jnp.zeros((8 - group_rows, LANES), F32)], axis=0)
    table = jnp.dot(named.astype(BF16), spread.astype(BF16), preferred_element_type=F32)
    row_of = source_of((8, cols)) >> log2(segs)
    slots = jnp.sum(jnp.where(iota((8, cols), 0) == row_of, table, 0.0), axis=0, keepdims=True)
    at_row = iota((3 * blk, cols), 0)
    kind = at_row >> log2(blk)
    sub = iota((3 * blk, cols), 1) & 7
    wanted = ((at_row & (blk - 1)) + 1).astype(F32)
    wsel_ref[...] = jnp.where((slots == wanted) & (sub == 3 * c + kind), 1.0, 0.0)


def prepare(owner_ref, slot_ref, source_ref, m_ref, v_ref, w_ref, lost_ref,
            order_ref, out_ref, wsel_ref, stay_ref, aux_ref, held):
    prepare_order(owner_ref, slot_ref, order_ref)
    prepare_state(owner_ref, slot_ref, source_ref, m_ref, v_ref, w_ref, lost_ref,
                  out_ref, wsel_ref, stay_ref, aux_ref, held)


def exchange(order_hbm, out_hbm, wsel_hbm, stay_hbm, aux_hbm, grad_hbm, result_ref,
             order, out_ref, wsel_ref, stay_ref, aux_ref,
             grad, csend, crecv, own, rl0, rl1, rx0, rx1, t0, t1, ry0, ry1, u, rz, gfull,
             srecv, ssum, r1, r2, r3, pbuf, precv,
             grad_sem, in_sem, csend_sem, crecv_sem, send_sem, recv_sem):
    blk = NX * JR
    zh = NZ // 2
    chunk = NY * zh * JR
    piece = zh * JR
    x = lax.axis_index("replica")
    dp = lax.axis_index("dp")
    y = dp // (2 * NZ)
    z = (dp // 2) % NZ
    c = dp % 2

    def device(dx=0, dy=0, dz=0, dc=0):
        to_y = (y + dy) % NY
        to_z = (z + dz) % NZ
        to_c = (c + dc) % 2
        return ((to_y * NZ + to_z) * 2 + to_c, (x + dx) % NX)

    pairs = ((order_hbm, order), (out_hbm, out_ref), (wsel_hbm, wsel_ref),
             (stay_hbm, stay_ref), (aux_hbm, aux_ref))
    small = [pltpu.make_async_copy(src, dst, in_sem.at[i]) for i, (src, dst) in enumerate(pairs)]
    for copy in small:
        copy.start()
    load = pltpu.make_async_copy(grad_hbm, grad, grad_sem)
    load.start()

    barrier = pltpu.get_barrier_semaphore()
    peers = ([dict(dc=1)] + [dict(dx=k) for k in range(1, NX)]
             + [dict(dy=k) for k in range(1, NY)])
    for peer in peers:
        pl.semaphore_signal(barrier, inc=1, device_id=device(**peer), device_id_type=MESH)

    def greet(k, carry):
        pl.semaphore_signal(barrier, inc=1, device_id=device(dz=k), device_id_type=MESH)
        return carry

    lax.fori_loop(1, NZ, greet, 0)

    def send(src, dst, to, s_sem, r_sem):
        pltpu.make_async_remote_copy(
            src_ref=src, dst_ref=dst, send_sem=s_sem, recv_sem=r_sem,
            device_id=to, device_id_type=MESH).start()

    def await_bytes(ref, sem):
        pltpu.make_async_copy(ref, ref, sem).wait()

    grad_rows = grad.reshape(grad.shape[0], 1, LANES)

    def gather(dst, dst_base, base):
        dst_rows = dst.reshape(dst.shape[0], 1, LANES)

        def step(i, carry):
            at = i * UNROLL
            values = [grad_rows[order[base + at + k]] for k in range(UNROLL)]
            for k in range(UNROLL):
                dst_rows[dst_base + at + k] = values[k]
            return carry

        lax.fori_loop(0, chunk // UNROLL, step, 0)

    chunks = []
    for k in (2, 1, 3, 0):
        chunks.append((0, k, pl.multiple_of(((x + k) % NX) * chunk, chunk)))
        chunks.append((1, k, pl.multiple_of((NX + (y + k) % NY) * chunk, chunk)))

    for copy in small:
        copy.wait()
    load.wait()
    core_rows = 2 * NX * chunk
    for i, (h, k, base) in enumerate(chunks):
        gather(csend, base, (1 - c) * core_rows + base)
        if i == 0:
            pl.semaphore_wait(barrier, len(peers) + NZ - 1)
            for dx in range(1, NX):
                to_y = (x + dx - y + NX) % NX
                send(out_ref.at[pl.ds(pl.multiple_of(to_y * NZ * 8, NZ * 8), NZ * 8)],
                     srecv.at[dx - 1], device(dx=dx), send_sem.at[0], recv_sem.at[0])
        rows = pl.ds(base, chunk)
        send(csend.at[rows], crecv.at[rows], device(dc=1), csend_sem, crecv_sem.at[i])

    alive_mine = aux_ref[0:1, :]
    alive_other = aux_ref[8:9, :]
    partner_y = (x - y + NX) % NX
    part = chunk // 2
    relays, landings = (rl0, rl1), (rx0, rx1)

    def pass_on(i):
        h, k, base = chunks[i]
        axis = "dx" if h == 0 else "dy"
        side = 0 if k == 1 else 1
        rows = pl.ds(pl.multiple_of(base + side * part, part), part)
        await_bytes(relays[h].at[side], recv_sem.at[11 + 2 * h + side])
        own[rows, :] = own[rows, :] + relays[h][side]
        send(own.at[rows], landings[h].at[side, side * part:(side + 1) * part],
             device(**{axis: 1 - 2 * side}), send_sem.at[1 + h], recv_sem.at[1 + h])

    for i, (h, k, base) in enumerate(chunks):
        gather(own, base, c * core_rows + base)
        rows = pl.ds(base, chunk)
        await_bytes(crecv.at[rows], crecv_sem.at[i])
        own[rows, :] = own[rows, :] * alive_mine + crecv[rows, :] * alive_other
        axis = "dx" if h == 0 else "dy"
        low = pl.ds(base, part)
        high = pl.ds(pl.multiple_of(base + part, part), part)
        up, down = device(**{axis: 1}), device(**{axis: -1})
        relay, landing = relays[h], landings[h]
        straight = (send_sem.at[1 + h], recv_sem.at[1 + h])
        if k == 2:
            send(own.at[low], relay.at[0], up, send_sem.at[11 + 2 * h], recv_sem.at[11 + 2 * h])
            send(own.at[high], relay.at[1], down, send_sem.at[12 + 2 * h], recv_sem.at[12 + 2 * h])
        elif k == 1:
            send(own.at[high], landing.at[0, part:chunk], up, *straight)
        elif k == 3:
            send(own.at[low], landing.at[1, 0:part], down, *straight)
        if i >= 4:
            pass_on(i - 2)
        if i == 1:
            await_bytes(srecv, recv_sem.at[0])
            total = out_ref[pl.ds(pl.multiple_of(partner_y * NZ * 8, NZ * 8), NZ * 8), :]
            for dx in range(NX - 1):
                total = total + srecv[dx]
            ssum[...] = total
            r1[z] = ssum[pl.ds(pl.multiple_of(z * 8, 8), 8), :]

            def spread(kz, carry):
                to_z = (z + kz) % NZ
                send(ssum.at[pl.ds(pl.multiple_of(to_z * 8, 8), 8)], r1.at[z],
                     device(dz=kz), send_sem.at[3], recv_sem.at[3])
                return carry

            lax.fori_loop(1, NZ, spread, 0)

    await_bytes(r1.at[0:NZ - 1], recv_sem.at[3])
    partner = ((partner_y * NZ + z) * 2 + c, x)

    @pl.when(partner_y != y)
    def _():
        send(r1, r2, partner, send_sem.at[6], recv_sem.at[6])

    @pl.when(partner_y == y)
    def _():
        r2[...] = r1[...]

    own0 = pl.multiple_of(x * chunk, chunk)
    own1 = pl.multiple_of((NX + y) * chunk, chunk)
    await_bytes(rx0, recv_sem.at[1])
    t0[...] = own[pl.ds(own0, chunk), :] + rx0[0] + rx0[1]
    for k in range(1, NY):
        at = pl.ds(pl.multiple_of(((y + k) % NY) * piece, piece), piece)
        send(t0.at[at], ry0.at[k - 1], device(dy=k), send_sem.at[4], recv_sem.at[4])
    await_bytes(rx1, recv_sem.at[2])
    t1[...] = own[pl.ds(own1, chunk), :] + rx1[0] + rx1[1]
    for k in range(1, NX):
        at = pl.ds(pl.multiple_of(((x + k) % NX) * piece, piece), piece)
        send(t1.at[at], ry1.at[k - 1], device(dx=k), send_sem.at[5], recv_sem.at[5])

    await_bytes(ry0, recv_sem.at[4])
    total = t0[pl.ds(pl.multiple_of(y * piece, piece), piece), :]
    for k in range(NY - 1):
        total = total + ry0[k]
    u[0:piece, :] = total
    await_bytes(ry1, recv_sem.at[5])
    total = t1[pl.ds(pl.multiple_of(x * piece, piece), piece), :]
    for k in range(NX - 1):
        total = total + ry1[k]
    u[piece:2 * piece, :] = total

    def scatter(kz, carry):
        to_z = (z + kz) % NZ
        send(u.at[pl.ds(pl.multiple_of(to_z * JR, JR), JR)], rz.at[kz - 1],
             device(dz=kz), send_sem.at[7], recv_sem.at[7])
        return carry

    lax.fori_loop(1, NZ, scatter, 0)

    @pl.when(partner_y != y)
    def _():
        await_bytes(r2, recv_sem.at[6])

    send(r2, r3, device(dc=1), send_sem.at[8], recv_sem.at[8])
    half = NZ * 8
    near = three_parts(r2[...].reshape(half, LANES))
    total = stay_ref[...] + pick(wsel_ref[:, 0:half].astype(BF16), near)
    await_bytes(r3, recv_sem.at[8])
    far = three_parts(r3[...].reshape(half, LANES))
    pbuf[...] = total + pick(wsel_ref[:, half:2 * half].astype(BF16), far)
    for k in range(1, NX):
        send(pbuf, precv.at[k - 1], device(dx=k), send_sem.at[9], recv_sem.at[9])

    await_bytes(rz, recv_sem.at[7])
    total = u[pl.ds(pl.multiple_of(z * JR, JR), JR), :]
    for k in range(NZ - 1):
        total = total + rz[k]
    gfull[x] = total
    for k in range(1, NX):
        send(gfull.at[x], gfull.at[x], device(dx=k), send_sem.at[10], recv_sem.at[10])

    await_bytes(precv, recv_sem.at[9])
    state = pbuf[...]
    for k in range(NX - 1):
        state = state + precv[k]
    await_bytes(gfull.at[0:NX - 1], recv_sem.at[10])
    result_ref[0:3 * blk, :] = state
    result_ref[3 * blk:4 * blk, :] = gfull[...].reshape(blk, LANES) / aux_ref[16:17, :]

    await_bytes(csend, csend_sem)
    for ref, n in ((srecv, 0), (rx0, 1), (rx1, 2),
                   (rl0.at[0], 11), (rl0.at[1], 12), (rl1.at[0], 13), (rl1.at[1], 14), (r1.at[0:NZ - 1], 3), (ry0, 4), (ry1, 5),
                   (rz, 7), (r3, 8), (precv, 9), (gfull.at[0:NX - 1], 10)):
        await_bytes(ref, send_sem.at[n])

    @pl.when(partner_y != y)
    def _():
        await_bytes(r1, send_sem.at[6])


def adamw_update(moment_one, moment_two, weight, gradient_rows):
    first = BETA_ONE * moment_one + (1.0 - BETA_ONE) * gradient_rows
    second = BETA_TWO * moment_two + (1.0 - BETA_TWO) * gradient_rows * gradient_rows
    update = first / BIAS_FIRST / (jnp.sqrt(second / BIAS_SECOND) + EPSILON)
    return (first, second, weight - LEARN_RATE * (update + DECAY_RATE * weight))


def on_device(grad_local, first_moment, second_moment, master_weight, lost_rows, source,
              new_owner, new_slot):
    blk = NX * JR
    nblk = new_owner.shape[0]
    rows = nblk // LANES
    half_z = NZ * 8
    zh = NZ // 2
    chunk = NY * zh * JR
    piece = zh * JR
    half_rows = 2 * NX * chunk

    def buf(*shape):
        return pltpu.VMEM(shape + (LANES,), F32)

    def whole(*shape):
        return pl.BlockSpec(shape, lambda i: (0, 0))

    table = (rows, LANES)
    shapes = ((NY * half_z, LANES), (3 * blk, 2 * half_z), (3 * blk, LANES), (24, LANES))
    prepared = pl.pallas_call(
        prepare,
        grid=(1,),
        out_shape=[jax.ShapeDtypeStruct(table, I32)]
        + [jax.ShapeDtypeStruct(shape, F32) for shape in shapes],
        in_specs=[whole(*table)] * 3 + [whole(blk, LANES)] * 3 + [whole(*lost_rows.shape)],
        out_specs=[whole(*table)] + [whole(*shape) for shape in shapes],
        scratch_shapes=[pltpu.VMEM((LANES, 3 * LANES), F32)],
        compiler_params=pltpu.CompilerParams(vmem_limit_bytes=VMEM_BYTES),
    )(new_owner.reshape(table), new_slot.reshape(table), source.reshape(table),
      first_moment[0], second_moment[0], master_weight[0], lost_rows)
    dma = pltpu.SemaphoreType.DMA
    result = pl.pallas_call(
        exchange,
        out_shape=jax.ShapeDtypeStruct((4 * blk, LANES), F32),
        in_specs=[pl.BlockSpec(memory_space=pl.ANY)] * 6,
        out_specs=pl.BlockSpec(memory_space=pltpu.VMEM),
        scratch_shapes=[
            pltpu.SMEM((nblk,), I32), *[pltpu.VMEM(shape, F32) for shape in shapes],
            buf(nblk), buf(half_rows), buf(half_rows), buf(half_rows),
            buf(2, chunk // 2), buf(2, chunk // 2),
            buf(2, chunk), buf(2, chunk), buf(chunk), buf(chunk),
            buf(NY - 1, piece), buf(NX - 1, piece), buf(2 * piece),
            buf(NZ - 1, JR), buf(NX, JR),
            buf(NX - 1, half_z), buf(half_z), buf(NZ, 8), buf(NZ, 8), buf(NZ, 8),
            buf(3 * blk), buf(NX - 1, 3 * blk),
            dma, dma((5,)), dma, dma((2 * NX,)), dma((15,)), dma((15,)),
        ],
        compiler_params=pltpu.CompilerParams(
            collective_id=0, has_side_effects=True, vmem_limit_bytes=VMEM_BYTES),
        cost_estimate=pl.CostEstimate(
            flops=nblk * LANES, bytes_accessed=nblk * LANES * 4, transcendentals=0),
    )(prepared[0].reshape(nblk), *prepared[1:], grad_local[0, 0])
    return adamw_update(result[0:blk], result[blk:2 * blk], result[2 * blk:3 * blk],
                        result[3 * blk:4 * blk])


def solution(mesh):
    return jax.shard_map(
        on_device,
        mesh=mesh,
        in_specs=(
            P("replica", "dp", None, None),
            P("replica", "dp", None),
            P("replica", "dp", None),
            P("replica", "dp", None),
            P(),
            P(),
            P(),
            P(),
        ),
        out_specs=(P("dp", None), P("dp", None), P("dp", None)),
        check_vma=False,
    )
```
